32 devices in a mesh: batch: 4 (over x, core), edge: 8 (over z, y).
Axes of the slice: x: 2, y: 2, z: 4, core: 2. Of those that a mesh axis runs over, the one named last changes fastest.
Arguments:
- states: bfloat16 [4, 1024, 128], P('batch', 'edge'), may hold values from -6 to 6
- edge_feats: bfloat16 [4, 16384, 16], P('batch', 'edge'), may hold values from -6 to 6
- molecule: int32 [4, 1024], P('batch', 'edge'), may hold values from 0 to 1023, as said below
- source: int32 [4, 16384], P('batch', 'edge'), may hold values from 0 to 1023, as said below
- target: int32 [4, 16384], P('batch', 'edge'), may hold values from 0 to 1023, as said below
- edge_mask: int32 [4, 16384], P('batch', 'edge'), may hold values 0 or 1
- w_edge_in: bfloat16 [16, 128], replicated, may hold values from -1.5 to 1.5
- b_edge_in: bfloat16 [128], replicated, may hold values from -3 to 3
- w_edge_out: bfloat16 [128, 16384], replicated, may hold values from -0.01171875 to 0.01171875
- b_edge_out: bfloat16 [16384], replicated, may hold values from -0.119628906 to 0.119628906
- w_input: bfloat16 [128, 384], replicated, may hold values from -0.5 to 0.5
- w_hidden: bfloat16 [128, 384], replicated, may hold values from -0.5 to 0.5
- b_input: bfloat16 [384], replicated, may hold values from -3 to 3
- b_hidden: bfloat16 [384], replicated, may hold values from -3 to 3
- cotangent: bfloat16 [4, 1024, 128], P('batch', 'edge'), may hold values from -6 to 6
Outputs:
- new_states: bfloat16 [4, 1024, 128], P('batch', 'edge')
- state_grads: float32 [4, 1024, 128], P('batch', 'edge')
- edge_grads: float32 [4, 16384, 16], P('batch', 'edge')
- grad_w_edge_in: float32 [16, 128], replicated
- grad_b_edge_in: float32 [128], replicated
- grad_w_edge_out: float32 [128, 16384], replicated
- grad_b_edge_out: float32 [16384], replicated
- grad_w_input: float32 [128, 384], replicated
- grad_w_hidden: float32 [128, 384], replicated
- grad_b_input: float32 [384], replicated
- grad_b_hidden: float32 [384], replicated
The draws below stay inside these ranges and needn't reach their ends.
Inputs may be any that keep to these rules, and one draw needn't show every extreme that they name: The molecule number of a node is the lowest position of its molecule in a hidden packing order; nodes of one molecule share it; each graph batch holds one molecule of min(100, 512) nodes. `source`: node index within the graph batch; most edges join two nodes of one molecule. `target`: node index within the graph batch.
All inputs are finite; a program needn't handle non-finite values. No bound on the sum of `edge_mask` on one device may be relied on, other than what follows from the above.
Results may differ from the reference program's by a relative error of at most 0.011.
Values may be sent and summed in bfloat16 or wider, within the bound.
No kernel may reach another device: no remote copies, remote signals or barrier semaphores. Data moves between devices by JAX's collectives and lax.ppermute only.
A program may use at most 128 MiB of HBM per device.

```python
import jax
import jax.numpy as jnp
from jax import lax

H = 128
EH = 128
EF = 16
GRAPHS = 4
NODES = 1024
EDGES = 16384


def layout(key):
    keys = jax.random.split(key, 7)
    big_size = min(100, NODES // 2)
    position = jnp.arange(NODES, dtype=jnp.int32)[None, :]
    begins = jax.random.randint(keys[0], (GRAPHS, NODES), 0, 16) == 0
    big_at = jax.random.randint(keys[1], (GRAPHS, 1), 1, NODES - big_size + 1)
    inside = (position > big_at) & (position < big_at + big_size)
    begins = begins & jnp.logical_not(inside) | (position == 0) | (position == big_at) | (position == big_at + big_size)
    first = lax.cummax(jnp.where(begins, position, 0), axis=1)
    upcoming = lax.cummin(jnp.where(begins, position, NODES), axis=1, reverse=True)
    following = jnp.concatenate([upcoming[:, 1:], jnp.full((GRAPHS, 1), NODES, jnp.int32)], axis=1)
    length = following - first
    order = jax.vmap(lambda k: jax.random.permutation(k, NODES))(jax.random.split(keys[2], GRAPHS)).astype(jnp.int32)
    labels = jax.vmap(lambda o, f: jnp.zeros((NODES,), jnp.int32).at[o].set(f))(order, first)
    picked = jax.random.randint(keys[3], (GRAPHS, EDGES), 0, NODES)
    start_of = jnp.take_along_axis(first, picked, axis=1)
    size_of = jnp.take_along_axis(length, picked, axis=1)
    partner = start_of + jax.random.randint(keys[4], (GRAPHS, EDGES), 0, size_of)
    stray = jax.random.randint(keys[5], (GRAPHS, EDGES), 0, 16) == 0
    partner = jnp.where(stray, jax.random.randint(keys[6], (GRAPHS, EDGES), 0, NODES), partner)
    sources = jnp.take_along_axis(order, picked, axis=1)
    targets = jnp.take_along_axis(order, partner, axis=1)
    return (labels, sources, targets)


def draw_molecule(key, part):
    return layout(key)[0]


def draw_source(key, part):
    return layout(key)[1]


def draw_target(key, part):
    return layout(key)[2]


def place_ends(array, stream_key, low, high):
    index_at = [jax.random.randint(jax.random.fold_in(stream_key, axis), (), 0, length) for axis, length in enumerate(array.shape)]
    widest = array.shape.index(max(array.shape))
    beside = index_at[:widest] + [(index_at[widest] + 1) % array.shape[widest]] + index_at[widest + 1:]
    return array.at[tuple(index_at)].set(low).at[tuple(beside)].set(high)


def shard_levels(rng, dims, cuts, least, high):
    def one(dim, blocks):
        draws = jax.random.uniform(jax.random.fold_in(jax.random.fold_in(rng, 6), dim), (blocks,), jnp.float32, least / len(cuts), high / len(cuts))
        return jnp.repeat(jnp.exp(draws), dims[dim] // blocks).reshape((-1,) + (1,) * (len(dims) - dim - 1))

    gain = one(*cuts[0])
    for cut in cuts[1:]:
        gain = gain * one(*cut)
    return gain


def centred(key, extent, scale, bound, cuts=(), held_as=jnp.bfloat16):
    factor_of = shard_levels(key, extent, cuts, -0.22, 0.18) if cuts else 1.0
    values = jax.random.normal(key, extent, jnp.float32) * scale * factor_of
    return jnp.minimum(jnp.maximum(values, -bound), bound).astype(held_as)


def setup_inputs(seed: int = 0) -> dict:
    splits = jax.random.split(jax.random.key(seed), 16)
    states = centred(splits[0], (GRAPHS, NODES, H), 1.0, 6.0, ((0, 4), (1, 8)))
    edge_feats = centred(splits[1], (GRAPHS, EDGES, EF), 1.0, 6.0, ((0, 4), (1, 8)))
    molecule = draw_molecule(jax.random.fold_in(splits[15], 71), 0)
    source = draw_source(jax.random.fold_in(splits[15], 71), 0)
    target = draw_target(jax.random.fold_in(splits[15], 71), 0)
    edge_mask = place_ends((jax.random.randint(splits[5], (GRAPHS, EDGES), 0, 8) < 7).astype(jnp.int32), jax.random.fold_in(splits[5], 1), 0, 1)
    w_edge_in = centred(splits[6], (EF, EH), EF ** -0.5, 1.5)
    b_edge_in = centred(splits[7], (EH,), 0.5, 3.0)
    w_edge_out = centred(splits[8], (EH, H * H), (EH * H * 16) ** -0.5, 0.01171875)
    b_edge_out = centred(splits[9], (H * H,), 0.02, 0.119628906)
    w_input = centred(splits[10], (H, 3 * H), H ** -0.5, 0.5)
    w_hidden = centred(splits[11], (H, 3 * H), H ** -0.5, 0.5)
    b_input = centred(splits[12], (3 * H,), 0.5, 3.0)
    b_hidden = centred(splits[13], (3 * H,), 0.5, 3.0)
    cotangent = centred(splits[14], (GRAPHS, NODES, H), 1.0, 6.0, ((0, 4), (1, 8)))
    return dict(states=states, edge_feats=edge_feats, molecule=molecule, source=source, target=target, edge_mask=edge_mask, w_edge_in=w_edge_in, b_edge_in=b_edge_in, w_edge_out=w_edge_out, b_edge_out=b_edge_out, w_input=w_input, w_hidden=w_hidden, b_input=b_input, b_hidden=b_hidden, cotangent=cotangent)


HIGH = lax.Precision.HIGHEST

@jax.custom_vjp
def low(v):
    return lax.optimization_barrier(v.astype(jnp.bfloat16)).astype(jnp.float32)

@jax.custom_vjp
def low_back(v):
    return v

def low_keep(v):
    return (low(v), None)

def low_pass(kept, grad):
    return (grad,)

def back_keep(v):
    return (v, None)

def back_low(kept, grad):
    return (low(grad),)
low.defvjp(low_keep, low_pass)
low_back.defvjp(back_keep, back_low)

def gated_update(mixed, prior, w_input, w_hidden, b_input, b_hidden):
    width = prior.shape[1]
    from_input = jnp.dot(mixed, w_input, precision=HIGH) + b_input
    from_state = jnp.dot(prior, w_hidden, precision=HIGH) + b_hidden
    reset = jax.nn.sigmoid(from_input[:, :width] + from_state[:, :width])
    update = jax.nn.sigmoid(from_input[:, width:2 * width] + from_state[:, width:2 * width])
    candidate = jnp.tanh(from_input[:, 2 * width:] + reset * from_state[:, 2 * width:])
    return (1.0 - update) * candidate + update * prior

def graph_layer(states_f, feats_f, w_edge_in, b_edge_in, w_edge_out, b_edge_out, w_input, w_hidden, b_input, b_hidden, source_ids, target_ids, valid):
    width = states_f.shape[1]
    nodes = states_f.shape[0]
    edges = source_ids.shape[0]
    block = min(1024, edges)
    count = edges // block

    @jax.checkpoint
    def edge_block(total, item):
        feats_b, src_b, dst_b, valid_b = item
        hidden = jax.nn.silu(jnp.dot(feats_b, w_edge_in, precision=HIGH) + b_edge_in)
        flat = low(low_back(jnp.dot(low(hidden), w_edge_out, precision=HIGH) + b_edge_out))
        mats = flat.reshape(block, width, width)
        near = low_back(states_f[src_b])
        message = jnp.einsum('bij,bj->bi', mats, near, precision=HIGH) * valid_b[:, None]
        return (total.at[dst_b].add(low(message)), None)
    items = (feats_f.reshape(count, block, -1), source_ids.reshape(count, block), target_ids.reshape(count, block), valid.reshape(count, block))
    summed, unused = lax.scan(edge_block, jnp.zeros((nodes, width), jnp.float32), items)
    mixed = low(low_back(summed))
    return gated_update(mixed, states_f, w_input, w_hidden, b_input, b_hidden)

def reference(states, edge_feats, molecule, source, target, edge_mask, w_edge_in, b_edge_in, w_edge_out, b_edge_out, w_input, w_hidden, b_input, b_hidden, cotangent):
    weights = tuple((x.astype(jnp.float32) for x in (w_edge_in, b_edge_in, w_edge_out, b_edge_out, w_input, w_hidden, b_input, b_hidden)))

    def one_graph(total, item):
        states_g, feats_g, mol_g, src_g, dst_g, mask_g, cot_g = item
        valid = mask_g.astype(jnp.float32) * (mol_g[src_g] == mol_g[dst_g]).astype(jnp.float32)

        def layer(s_in, f_in, wa, wb, wc, wd, we, wf, wg, wh_):
            return graph_layer(s_in, f_in, wa, wb, wc, wd, we, wf, wg, wh_, src_g, dst_g, valid)
        result, pull = jax.vjp(layer, states_g.astype(jnp.float32), feats_g.astype(jnp.float32), weights[0], weights[1], weights[2], weights[3], weights[4], weights[5], weights[6], weights[7])
        grads = pull(cot_g.astype(jnp.float32))
        total = tuple((a + b for a, b in zip(total, grads[2:])))
        return (total, (result.astype(jnp.bfloat16), grads[0], grads[1]))
    zeros = tuple((jnp.zeros_like(w) for w in weights))
    total, outs = lax.scan(one_graph, zeros, (states, edge_feats, molecule, source, target, edge_mask, cotangent))
    return (outs[0], outs[1], outs[2], total[0], total[1], total[2], total[3], total[4], total[5], total[6], total[7])
```

```python
import functools

import jax
import jax.numpy as jnp
from jax import lax
from jax.experimental import pallas as pl
from jax.experimental.pallas import tpu as pltpu
from jax.sharding import PartitionSpec as P

F32 = jnp.float32
BF16 = jnp.bfloat16
H = 128
CAP = 64
GROUP = 16
PIECES = 32
UNITS = H // PIECES
EXTRA = 32
VMEM_LIMIT = 60 * 1024 * 1024
BACK = 4
UNROLL = 1
AGG = 16


def nn(a, b):
    return lax.dot_general(a, b, (((1,), (0,)), ((), ())), preferred_element_type=F32)


def nt(a, b):
    return lax.dot_general(a, b, (((1,), (1,)), ((), ())), preferred_element_type=F32)


def eye(n):
    rows = lax.broadcasted_iota(jnp.int32, (n, n), 0)
    cols = lax.broadcasted_iota(jnp.int32, (n, n), 1)
    return jnp.where(rows == cols, 1.0, 0.0).astype(BF16)


def one_hot_rows(rel, count):
    rel = jnp.clip(rel, -1, count).astype(F32).astype(BF16)
    rows = lax.broadcasted_iota(jnp.int32, (count, rel.shape[1]), 0).astype(F32).astype(BF16)
    return jnp.where(rows == rel, jnp.ones((), BF16), jnp.zeros((), BF16))


def slot_hots(slot, count):
    return one_hot_rows(jnp.right_shift(slot, 7), count), one_hot_rows(jnp.bitwise_and(slot, H - 1), H)


def sort_kernel(shape, target_ref, source_ref, mask_ref, label_ref, feats_ref, states_ref, out_ref, slot_ref, data_ref):
    holders, own, groups = shape
    blocks = groups // 2
    edges = target_ref.shape[1]
    target = target_ref[...]
    owner = jnp.right_shift(target, own.bit_length() - 1)
    local = jnp.bitwise_and(target, own - 1)
    bucket = owner * groups + jnp.right_shift(local, 4)
    bucket = jnp.where(mask_ref[...] != 0, bucket, -1)
    buckets = holders * groups

    block = 256
    rows = lax.broadcasted_iota(jnp.int32, (block, block), 0)
    cols = lax.broadcasted_iota(jnp.int32, (block, block), 1)
    upto = jnp.where(rows <= cols, 1.0, 0.0).astype(BF16)
    numbers = lax.broadcasted_iota(jnp.int32, (buckets, block), 0)
    carry = jnp.zeros((buckets, 1), F32)
    slots = []
    for b in range(edges // block):
        here = bucket[:, b * block : (b + 1) * block]
        hot = numbers == here
        within = nn(hot.astype(F32).astype(BF16), upto) + carry
        rank = jnp.sum(jnp.where(hot, within - 1.0, 0.0), axis=0, keepdims=True).astype(jnp.int32)
        carry = within[:, block - 1 : block]
        slots.append(jnp.where((here >= 0) & (rank < CAP), here * CAP + rank, -1))
    worst = jnp.max(carry, axis=0, keepdims=True)
    flag = jnp.where(worst > CAP, 1.0, 0.0)
    slot = jnp.concatenate(slots, axis=1)
    slot_ref[...] = slot

    data_ref[16:32, :] = jnp.zeros((16, edges), F32)
    data_ref[0:16, :] = feats_ref[...].astype(F32)
    source = source_ref[...]
    data_ref[16:17, :] = jnp.right_shift(source, 6).astype(F32)
    data_ref[17:18, :] = jnp.bitwise_and(source, 63).astype(F32)
    data_ref[18:19, :] = (local + 1).astype(F32)
    data = data_ref[...].astype(BF16)

    tags = []
    for t in range(own // H):
        label = label_ref[:, t * H : (t + 1) * H]
        tags += [jnp.right_shift(label, 6).astype(F32), jnp.bitwise_and(label, 63).astype(F32)]
    tags.append(jnp.broadcast_to(flag, (1, H)))
    tags.append(jnp.zeros((16 - 3 * blocks - len(tags), H), F32))
    high, low = slot_hots(slot, holders * blocks)
    together = min(4, holders)
    for s0 in range(0, holders, together):
        part = high[s0 * blocks : (s0 + together) * blocks, :]
        spread = (part[:, None, :] * data[None, :, :]).reshape(together * blocks * 32, edges)
        moved = nt(spread, low)
        for n in range(together):
            out = out_ref.at[s0 + n]
            out[0:own, :] = states_ref[...]
            ids = []
            for q in range(blocks):
                at = (n * blocks + q) * 32
                out[own + 16 * q : own + 16 * (q + 1), :] = moved[at : at + 16, :].astype(BF16)
                ids.append(moved[at + 16 : at + 19, :])
            out[own + 16 * blocks : own + 16 * blocks + 16, :] = jnp.concatenate(ids + tags, axis=0).astype(BF16)


def swap_rows(outer, inner, flip=None):
    n = outer * inner
    rows = lax.broadcasted_iota(jnp.int32, (n, n), 0)
    cols = lax.broadcasted_iota(jnp.int32, (n, n), 1)
    number = rows % inner
    if flip is not None:
        number = jnp.bitwise_xor(number, flip)
    return jnp.where(number * outer + rows // inner == cols, 1.0, 0.0).astype(BF16)


def split_kernel(w_ref, out_ref):
    order = swap_rows(16, 16)
    for ib in range(0, H, 32):
        sides = []
        for half in range(2):
            rows = [w_ref[:, (ib + 16 * half + i) * H : (ib + 16 * half + i + 1) * H] for i in range(16)]
            sides.append(jnp.concatenate(rows, axis=0))
        moved = nn(order, jnp.concatenate(sides, axis=1)).astype(BF16)
        for half in range(2):
            at = ib + 16 * half
            out_ref[:, at : at + 16, :] = moved[:, half * H : (half + 1) * H].reshape(16, 16, H)


def front_kernel(shape, chunks, *refs):
    holders, own, groups = shape
    blocks = groups // 2
    refs = list(refs)
    take = lambda n: [refs.pop(0) for _ in range(n)]
    piece_ref, given, states_ref, own_label_ref, t_in, b2_ref, w1_ref, b1_ref, wi_ref, wh_ref, bi_ref, bh_ref, cot_ref = take(13)
    new_ref, direct_ref, d_ref, lat_out, near_out, meta_out, flag_ref = take(7)
    keeps_out = take(len(chunks))
    sends_out = take(len(chunks))
    table_ref, p_ref, sum_ref, small_ref, dt_ref, rows_ref, bias_ref, extra_ref, t_ref, lat_ref, near_ref, meta_ref = take(12)
    keeps = take(len(chunks))
    sends = take(len(chunks))
    (sems,) = refs
    waiting = []

    def copy(source, target):
        moving = pltpu.make_async_copy(source, target, sems.at[len(waiting)])
        moving.start()
        waiting.append(moving)
        return moving

    t_copy = copy(t_in, t_ref)

    nodes = holders * own
    lanes = holders * CAP
    ident = eye(H)
    tags_at = own + 16 * blocks

    flag = jnp.zeros((1, 1), F32)
    for s in range(holders):
        tags = given[s, tags_at : tags_at + 16, :].astype(F32)
        flag = jnp.maximum(flag, tags[3 * blocks + 2 * (own // H) : 3 * blocks + 2 * (own // H) + 1, 0:1])
        for t in range(own // H):
            at = s * own + t * H
            table_ref[0:H, at : at + H] = nt(ident, given[s, t * H : (t + 1) * H, :]).astype(BF16)
            both = tags[3 * blocks + 2 * t : 3 * blocks + 2 * t + 2, :]
            table_ref[H : H + 16, at : at + H] = jnp.concatenate([both, jnp.zeros((14, H), F32)], axis=0).astype(BF16)
    flag_ref[...] = jnp.broadcast_to(flag, flag_ref.shape)
    for t in range(own // H):
        label = own_label_ref[:, t * H : (t + 1) * H]
        label = jnp.concatenate([jnp.right_shift(label, 6), jnp.bitwise_and(label, 63)], axis=0).astype(F32)
        cols = nt(ident, jnp.concatenate([label, jnp.zeros((14, H), F32)], axis=0).astype(BF16))
        small_ref[t * H : (t + 1) * H, 0:1] = cols[:, 0:1] * 64.0 + cols[:, 1:2]

    low_lanes = lax.broadcasted_iota(jnp.int32, (24, H), 1) < CAP
    for q in range(blocks):
        for s in range(0, holders, 2):
            parts = []
            for n in range(2):
                feats = given[s + n, own + 16 * q : own + 16 * (q + 1), :].astype(F32)
                ids = given[s + n, tags_at : tags_at + 16, :].astype(F32)[3 * q : 3 * q + 3, :]
                parts.append(jnp.concatenate([feats, ids, jnp.zeros((5, H), F32)], axis=0))
            first, second = parts
            at = slice(s // 2 * H, (s // 2 + 1) * H)
            meta_ref[2 * q, 0:24, at] = jnp.where(low_lanes, first, pltpu.roll(second, CAP, 1))
            meta_ref[2 * q + 1, 0:24, at] = jnp.where(low_lanes, pltpu.roll(first, CAP, 1), second)

    w1 = nt(ident, w1_ref[...]).astype(BF16)
    b1 = nt(ident, jnp.broadcast_to(b1_ref[...].astype(F32), (16, H)).astype(BF16))[:, 0:1]

    def group_step(g, unused):
        data = meta_ref[g, 0:24, :]
        source = (data[16:17, :] * 64.0 + data[17:18, :]).astype(jnp.int32)
        meta_ref[g, 19:20, :] = source.astype(F32)
        picked = jnp.zeros((H + 16, lanes), F32)
        for c in range(0, nodes, 256):
            picked = picked + nn(table_ref[:, c : c + 256], one_hot_rows(source - c, 256))
        near = picked[0:H, :].astype(BF16)
        label = picked[H : H + 1, :] * 64.0 + picked[H + 1 : H + 2, :]
        inside = data[18:19, :] - 1.0 - (g * GROUP).astype(F32)
        numbers = lax.broadcasted_iota(jnp.int32, (GROUP, lanes), 0).astype(F32)
        own_label = small_ref[pl.ds(pl.multiple_of(g * GROUP, GROUP), GROUP), 0:1]
        member = jnp.where((numbers == inside) & (own_label == label), 1.0, 0.0)
        meta_ref[g, 32 : 32 + GROUP, :] = member
        member = member.astype(BF16)
        before = nn(w1, data[0:16, :].astype(BF16)) + b1
        latent = (before / (1.0 + jnp.exp(-before))).astype(BF16)
        lat_ref[g] = latent
        near_ref[g] = near
        spread = (latent[:, None, :] * member[None, :, :]).reshape(H * GROUP, lanes)
        at = pl.ds(pl.multiple_of(g * GROUP, GROUP), GROUP)
        p_ref[:, at, :] = nt(spread, near).reshape(H, GROUP, H).astype(BF16)
        sum_ref[at, :] = nt(member, near)
        return unused

    lax.fori_loop(0, groups, group_step, 0, unroll=UNROLL)
    copy(lat_ref, lat_out)
    copy(near_ref, near_out)
    copy(meta_ref, meta_out)

    def agg_step(n, total):
        left = jnp.concatenate([p_ref[n * AGG + m] for m in range(AGG)], axis=1)
        right = jnp.concatenate([t_ref[n * AGG + m] for m in range(AGG)], axis=1)
        return total + nt(left, right)

    total = nt(sum_ref[...].astype(BF16), b2_ref[...])
    t_copy.wait()
    total = lax.fori_loop(0, H // AGG, agg_step, total)

    mixed = total.astype(BF16)
    prior = states_ref[...]
    prior_f = prior.astype(F32)
    cot = cot_ref[...].astype(F32)
    wi, wh = wi_ref[...], wh_ref[...]
    gi = nn(mixed, wi) + bi_ref[...]
    gh = nn(prior, wh) + bh_ref[...]
    r = jax.nn.sigmoid(gi[:, 0:H] + gh[:, 0:H])
    u = jax.nn.sigmoid(gi[:, H : 2 * H] + gh[:, H : 2 * H])
    n = jnp.tanh(gi[:, 2 * H :] + r * gh[:, 2 * H :])
    new_ref[...] = ((1.0 - u) * n + u * prior_f).astype(BF16)
    d_pre = (1.0 - u) * cot * (1.0 - n * n)
    d_r = d_pre * gh[:, 2 * H :] * r * (1.0 - r)
    d_u = (prior_f - n) * cot * u * (1.0 - u)
    d_gi = jnp.concatenate([d_r, d_u, d_pre], axis=1)
    d_gh = jnp.concatenate([d_r, d_u, d_pre * r], axis=1)

    def halves(x):
        high = x.astype(BF16)
        return high, (x - high.astype(F32)).astype(BF16)

    def twice(x):
        return jnp.concatenate([x, x], axis=1)

    gi_high, gi_low = halves(d_gi)
    gh_high, gh_low = halves(d_gh)
    d_agg = nt(jnp.concatenate([gi_high, gi_low], axis=1), twice(wi)).astype(BF16)
    d_ref[...] = d_agg
    dt_ref[...] = nt(ident, d_agg).astype(BF16)
    direct_ref[...] = u * cot + nt(jnp.concatenate([gh_high, gh_low], axis=1), twice(wh))

    piece_me = piece_ref[0]
    for rel in list(range(PIECES // 2, PIECES)) + list(range(PIECES // 2)):
        k0 = jnp.bitwise_xor(piece_me, rel) * UNITS
        for m in range(0, UNITS, 2):
            out = nn(dt_ref[...], jnp.concatenate([p_ref[k0 + m], p_ref[k0 + m + 1]], axis=1)).astype(BF16)
            for c, chunk in enumerate(chunks):
                dest = sends[c] if rel >= PIECES // 2 else keeps[c]
                for h in range(2):
                    rows = slice((m + h) * chunk.rows, (m + h + 1) * chunk.rows)
                    dest[chunk.place(rel), rows, :] = out[chunk.first : chunk.first + chunk.rows, h * H : (h + 1) * H]
        if rel == PIECES - 1:
            for c in range(len(chunks) - 1):
                copy(sends[c], sends_out[c])
        if rel == PIECES // 2 - 1:
            for c in range(len(chunks) - 1):
                copy(keeps[c], keeps_out[c])

    mixed_t = nt(ident, mixed).astype(BF16)
    prior_t = nt(ident, prior).astype(BF16)
    from_input = nn(twice(mixed_t), jnp.concatenate([gi_high, gi_low], axis=0))
    from_state = nn(twice(prior_t), jnp.concatenate([gh_high, gh_low], axis=0))
    for t in range(3):
        rows_ref[t] = from_input[:, t * H : (t + 1) * H]
        rows_ref[3 + t] = from_state[:, t * H : (t + 1) * H]
    rows_ref[6] = nn(dt_ref[...], sum_ref[...].astype(BF16))
    bias_ref[...] = jnp.zeros_like(bias_ref)
    for n, part in enumerate((d_gi, d_gh)):
        part = jnp.sum(part, axis=0, keepdims=True)
        for t in range(3):
            bias_ref[3 * n + t : 3 * n + t + 1, :] = part[:, t * H : (t + 1) * H]
    extra_ref[...] = jnp.zeros_like(extra_ref)
    last = chunks[-1]
    for rel in range(PIECES):
        p = jnp.bitwise_xor(piece_me, rel)
        for t in range(7):
            extra_ref[UNITS * t : UNITS * (t + 1), :] = rows_ref[t, pl.ds(p * UNITS, UNITS), :]
        extra_ref[28:29, :] = bias_ref[pl.ds(p, 1), :]
        dest = sends[-1] if rel >= PIECES // 2 else keeps[-1]
        dest[last.place(rel), UNITS * last.rows : last.height, :] = extra_ref[...].astype(BF16)
    copy(sends[-1], sends_out[-1])
    copy(keeps[-1], keeps_out[-1])
    for moving in waiting[1:]:
        moving.wait()


def spread_kernel(shape, d_ref, t_ref, b2_ref, wide_ref, bias_ref, dp_ref):
    holders, own, groups = shape
    d = d_ref[...]
    bias_ref[...] = nn(d, b2_ref[...])
    order = swap_rows(16, 16)
    for n in range(0, 16, 2):
        out = nn(d, jnp.concatenate([t_ref[n], t_ref[n + 1]], axis=1)).astype(BF16)
        dp_ref[n] = out[:, :H]
        dp_ref[n + 1] = out[:, H:]
    for g in range(0, groups, 2):
        sides = [dp_ref[:, (g + n) * GROUP : (g + n + 1) * GROUP, :].reshape(256, H) for n in range(2)]
        moved = nn(order, jnp.concatenate(sides, axis=1)).astype(BF16)
        for n in range(2):
            for v in range(GROUP):
                wide_ref[g + n, :, v * H : (v + 1) * H] = moved[v * 16 : (v + 1) * 16, n * H : (n + 1) * H]


def back_kernel(shape, count, *refs):
    holders, own, groups = shape
    wide_ref, bias_ref, w1_ref, b1_ref, lat_ref, near_ref, meta_ref, part_in_ref, first_in_ref = refs[:9]
    part_ref, first_ref, edge_ref = refs[9:]
    nodes = holders * own
    lanes = holders * CAP
    ident = eye(H)
    part_ref[...] = part_in_ref[...]
    w1n = w1_ref[...]
    w1 = nt(ident, w1n).astype(BF16)
    b1 = nt(ident, jnp.broadcast_to(b1_ref[...].astype(F32), (16, H)).astype(BF16))[:, 0:1]
    one_row = jnp.where(lax.broadcasted_iota(jnp.int32, (16, lanes), 0) == 0, 1.0, 0.0).astype(BF16)

    def group_step(g, first_total):
        data = meta_ref[g, 0:16, :].astype(BF16)
        source = meta_ref[g, 19:20, :].astype(jnp.int32)
        member = meta_ref[g, 32 : 32 + GROUP, :].astype(BF16)
        latent = lat_ref[g]
        near = near_ref[g]
        wide = wide_ref[g]
        spread = (near[None, :, :] * member[:, None, :]).reshape(GROUP * H, lanes)
        d_latent = nn(wide, spread)
        tall = jnp.concatenate([wide[:, v * H : (v + 1) * H] for v in range(GROUP)], axis=0)
        wide_t = nt(ident, tall).astype(BF16)
        spread = (latent[None, :, :] * member[:, None, :]).reshape(GROUP * H, lanes)
        d_near = nn(wide_t, spread)
        bias_rows = bias_ref[pl.ds(pl.multiple_of(g * GROUP, GROUP), GROUP), :].astype(BF16)
        bias_t = nt(ident, bias_rows).astype(BF16)
        d_near = (d_near + nn(bias_t, member)).astype(BF16)
        for c in range(0, nodes, 256):
            part_ref[c : c + 256, :] += nt(one_hot_rows(source - c, 256), d_near)
        before = nn(w1, data) + b1
        gate = 1.0 / (1.0 + jnp.exp(-before))
        d_before = (d_latent * gate * (1.0 + before * (1.0 - gate))).astype(BF16)
        edge_ref[g] = nn(w1n, d_before)
        return first_total + nt(jnp.concatenate([data, one_row], axis=0), d_before)

    first_ref[...] = lax.fori_loop(0, count, group_step, first_in_ref[...])


def return_kernel(shape, me_ref, part_ref, first_ref, *refs):
    holders, own, groups = shape
    blocks = groups // 2
    edges, (keep_d, keep_e, send_ref, slab_ref) = refs[:-4], refs[-4:]
    low_lanes = lax.broadcasted_iota(jnp.int32, (16, H), 1) < CAP
    pick = lambda g, at: edges[g * len(edges) // groups][g % (groups // len(edges)), :, at]
    for q in range(blocks):
        for s in range(0, holders, 2):
            at = slice(s // 2 * H, (s // 2 + 1) * H)
            even, odd = pick(2 * q, at), pick(2 * q + 1, at)
            slab_ref[s, 16 * q : 16 * (q + 1), :] = jnp.where(low_lanes, even, pltpu.roll(odd, CAP, 1)).astype(BF16)
            slab_ref[s + 1, 16 * q : 16 * (q + 1), :] = jnp.where(low_lanes, pltpu.roll(even, CAP, 1), odd).astype(BF16)
    half = holders // 2
    for rel in range(holders):
        h = jnp.bitwise_xor(me_ref[0], rel)
        rows = part_ref[pl.ds(pl.multiple_of(h * own, own), own), :].astype(BF16)
        n = rel // 2
        if rel % 2 == 0:
            keep_d[n] = rows
            keep_e[n] = slab_ref[h]
        else:
            send_ref[n * own : (n + 1) * own, :] = rows
            at = half * own + n * 16 * blocks
            send_ref[at : at + 16 * blocks, :] = slab_ref[h]
    at = half * (own + 16 * blocks)
    send_ref[at : at + 32, :] = first_ref[...].astype(BF16)


def gather_kernel(shape, me_ref, slot_ref, direct_ref, part_ref, slabs_ref, state_ref, edge_ref, data_ref):
    holders, own, groups = shape
    blocks = groups // 2
    state_ref[...] = direct_ref[...] + part_ref[...].astype(F32)
    for rel in range(holders):
        h = jnp.bitwise_xor(me_ref[0], rel)
        data_ref[pl.ds(pl.multiple_of(h * 16 * blocks, 16), 16 * blocks), :] = slabs_ref[rel]
    edges = slot_ref.shape[1]
    data = data_ref[...]
    count = holders * blocks
    block = 512
    for b in range(edges // block):
        high, low = slot_hots(slot_ref[:, b * block : (b + 1) * block], count)
        high = high.astype(F32)
        found = nn(data, low)
        total = jnp.zeros((16, block), F32)
        for n in range(count):
            total = total + found[16 * n : 16 * (n + 1), :] * high[n : n + 1, :]
        edge_ref[:, b * block : (b + 1) * block] = total


class Chunk:
    def __init__(self, first, rows, extra, order):
        self.first, self.rows, self.extra, self.order = first, rows, extra, order
        self.height = UNITS * rows + extra

    def place(self, rel):
        at = 0
        for bit in self.order:
            at = at * 2 + (rel >> bit & 1)
        return at

    def shape(self):
        return (2,) * len(self.order) + (self.height, H)


def plan(batch, edge):
    core, x = [edge], [edge << n for n in range(1, batch.bit_length() - 1)]
    z = [2 << n for n in reversed(range(3 - len(x)))]
    bits = z + [1] + x + core
    chunks = [Chunk(0, 64, 0, (3, 2, 1, 0)), Chunk(64, 64, EXTRA, (2, 3, 1, 0))]
    device = lax.axis_index(("batch", "edge")).astype(jnp.int32)
    piece = sum(jnp.where(device & mask != 0, 1 << n, 0) for n, mask in enumerate(bits))
    return bits, chunks, piece.astype(jnp.int32).reshape(1)


def swap(x, mask, devices):
    return lax.ppermute(x, ("batch", "edge"), [(i, i ^ mask) for i in range(devices)])


def add(terms):
    total = terms[0].astype(F32)
    for term in terms[1:]:
        total = total + term.astype(F32)
    return total.astype(BF16)


def rounded(x):
    return lax.reduce_precision(x.astype(F32), 8, 7).astype(BF16)


def assemble_kernel(chunks, piece_ref, *refs):
    count = len(chunks)
    pairs = refs[: 2 * count]
    w_out, wi_ref, wh_ref, b2_ref, bi_ref, bh_ref, rows_ref, extra_ref, bias_ref, order_ref, sems = refs[2 * count :]
    me = piece_ref[0]
    flip = jnp.bitwise_and(me, 1)
    order_ref[...] = swap_rows(32, 2 * UNITS, flip * UNITS)

    def moving(step):
        pair = jnp.bitwise_xor(jnp.right_shift(me, 1), step)
        rows = pl.ds(pl.multiple_of(pair * 2 * UNITS, 2 * UNITS), 2 * UNITS)
        return pltpu.make_async_copy(rows_ref.at[step % 4], w_out.at[rows, :], sems.at[step % 4])

    for step in range(PIECES // 2):
        if step >= 4:
            moving(step - 4).wait()
        rel = 2 * step
        which = rel // (PIECES // 2)
        blocks = [pairs[2 * c + which] for c in range(count)]
        places = [[chunk.place(rel + n) for n in range(2)] for chunk in chunks]
        for ib in range(0, H, 64):
            sides = []
            for half in range(2):
                at = ib + 32 * half
                c = max(n for n in range(count) if chunks[n].first <= at)
                first, rows = chunks[c].first, chunks[c].rows
                sides.append(
                    jnp.concatenate(
                        [
                            blocks[c][places[c][n], m * rows + at - first : m * rows + at - first + 32, :]
                            for n in range(2)
                            for m in range(UNITS)
                        ],
                        axis=0,
                    )
                )
            moved = nn(order_ref[...], jnp.concatenate(sides, axis=1))
            for half in range(2):
                for i in range(32):
                    at = (ib + 32 * half + i) * H
                    rows_ref[step % 4, :, at : at + H] = moved[8 * i : 8 * (i + 1), half * H : (half + 1) * H]
        moving(step).start()
        for n in range(2):
            start = UNITS * chunks[-1].rows
            extra = blocks[-1][places[-1][n], start : start + EXTRA, :].astype(F32)
            p = jnp.bitwise_xor(me, rel + n)
            for t in range(7):
                extra_ref[t, pl.ds(p * UNITS, UNITS), :] = extra[UNITS * t : UNITS * (t + 1), :]
            bias_ref[pl.ds(p, 1), :] = extra[28:29, :]
    for t in range(3):
        wi_ref[:, t * H : (t + 1) * H] = extra_ref[t]
        wh_ref[:, t * H : (t + 1) * H] = extra_ref[3 + t]
        bi_ref[t * H : (t + 1) * H] = bias_ref[t : t + 1, :].reshape(H)
        bh_ref[t * H : (t + 1) * H] = bias_ref[3 + t : 4 + t, :].reshape(H)
    b2_ref[...] = extra_ref[6]
    for step in range(PIECES // 2 - 4, PIECES // 2):
        moving(step).wait()


def vmem():
    return pl.BlockSpec(memory_space=pltpu.VMEM)


def anywhere():
    return pl.BlockSpec(memory_space=pl.ANY)


def smem():
    return pl.BlockSpec(memory_space=pltpu.SMEM)


def cost(us):
    return pl.CostEstimate(flops=int(us * 1e9), bytes_accessed=int(us * 3e6), transcendentals=0)


def params():
    return pltpu.CompilerParams(vmem_limit_bytes=VMEM_LIMIT)


def fast_path(batch, edge, args):
    (states, edge_feats, molecule, source, target, edge_mask, w_edge_in, b_edge_in, w_edge_out, b_edge_out,
     w_input, w_hidden, b_input, b_hidden, cotangent) = args
    devices = batch * edge
    states_here = states[0]
    own = states_here.shape[0]
    edges = source.shape[1]
    holders, groups = edge, own // GROUP
    shape = (holders, own, groups)
    blocks = groups // 2
    bits, chunks, piece_arr = plan(batch, edge)
    rest = [m for m in (1 << n for n in range(devices.bit_length() - 1)) if m not in bits]
    me_arr = lax.axis_index("edge").astype(jnp.int32).reshape(1)
    lanes = holders * CAP

    slots_out, slot = pl.pallas_call(
        functools.partial(sort_kernel, shape),
        name="edges_to_slots",
        out_shape=[
            jax.ShapeDtypeStruct((holders, own + 16 * blocks + 16, H), BF16),
            jax.ShapeDtypeStruct((1, edges), jnp.int32),
        ],
        in_specs=[vmem()] * 6,
        out_specs=[vmem()] * 2,
        scratch_shapes=[pltpu.VMEM((32, edges), F32)],
        compiler_params=params(),
    )(target, source, edge_mask, molecule, jnp.swapaxes(edge_feats, 1, 2)[0], states_here)
    given = lax.all_to_all(slots_out, "edge", 0, 0)

    t_units = pl.pallas_call(
        split_kernel,
        name="split_weight",
        grid=(H // 16,),
        in_specs=[pl.BlockSpec((16, H * H), lambda i: (i, 0))],
        out_specs=pl.BlockSpec((16, H, H), lambda i: (i, 0, 0)),
        out_shape=jax.ShapeDtypeStruct((H, H, H), BF16),
        compiler_params=params(),
    )(w_edge_out)
    b2 = b_edge_out.reshape(H, H)
    b1 = b_edge_in.reshape(1, H)
    half = [jax.ShapeDtypeStruct((PIECES // 2, c.height, H), BF16) for c in chunks]
    front = pl.pallas_call(
        functools.partial(front_kernel, shape, chunks),
        name="messages_update_weight_gradient",
        out_shape=[
            jax.ShapeDtypeStruct((own, H), BF16),
            jax.ShapeDtypeStruct((own, H), F32),
            jax.ShapeDtypeStruct((own, H), BF16),
            jax.ShapeDtypeStruct((groups, H, lanes), BF16),
            jax.ShapeDtypeStruct((groups, H, lanes), BF16),
            jax.ShapeDtypeStruct((groups, 32 + GROUP, lanes), F32),
            jax.ShapeDtypeStruct((8, H), F32),
        ]
        + half
        + half,
        in_specs=[smem()] + [vmem()] * 3 + [anywhere()] + [vmem()] * 8,
        out_specs=[vmem()] * 3 + [anywhere()] * 3 + [vmem()] + [anywhere()] * (2 * len(chunks)),
        scratch_shapes=[
            pltpu.VMEM((H + 16, holders * own), BF16),
            pltpu.VMEM((H, own, H), BF16),
            pltpu.VMEM((own, H), F32),
            pltpu.VMEM((own, H), F32),
            pltpu.VMEM((H, own), BF16),
            pltpu.VMEM((7, H, H), F32),
            pltpu.VMEM((PIECES, H), F32),
            pltpu.VMEM((EXTRA, H), F32),
            pltpu.VMEM((H, H, H), BF16),
            pltpu.VMEM((groups, H, lanes), BF16),
            pltpu.VMEM((groups, H, lanes), BF16),
            pltpu.VMEM((groups, 32 + GROUP, lanes), F32),
        ]
        + [pltpu.VMEM(h.shape, BF16) for h in half] * 2
        + [pltpu.SemaphoreType.DMA((4 + 2 * len(chunks),))],
        compiler_params=params(),
    )(
        piece_arr, given, states_here, molecule, t_units, b2, w_edge_in, b1, w_input, w_hidden,
        b_input.astype(F32).reshape(1, -1), b_hidden.astype(F32).reshape(1, -1), cotangent[0],
    )
    new_states, direct, d_agg, latent, near, meta, flag = front[:7]
    keeps = front[7 : 7 + len(chunks)]
    sends = front[7 + len(chunks) :]

    got = [swap(sends[c].reshape(chunk.shape()), bits[-1], devices) for c, chunk in enumerate(chunks)]
    terms = [[keeps[c].reshape(chunk.shape()), got[c]] for c, chunk in enumerate(chunks)]

    def scatter_step(step, work):
        sent = [add([t[1] for t in terms[c]]) for c in range(len(chunks))]
        given, run = work
        sent, given = lax.optimization_barrier((sent, given))
        got = [swap(sent[c], bits[chunk.order[step]], devices) for c, chunk in enumerate(chunks)]
        result = run(given)
        got, result = lax.optimization_barrier((got, result))
        for c in range(len(chunks)):
            terms[c] = [t[0] for t in terms[c]] + [got[c]]
        return result

    matrix_gradients = pl.pallas_call(
        functools.partial(spread_kernel, shape),
        name="matrix_gradients",
        out_shape=[jax.ShapeDtypeStruct((groups, H, GROUP * H), BF16), jax.ShapeDtypeStruct((own, H), F32)],
        grid=(H // 16,),
        in_specs=[
            pl.BlockSpec((own, H), lambda i: (0, 0)),
            pl.BlockSpec((16, H, H), lambda i: (i, 0, 0)),
            pl.BlockSpec((H, H), lambda i: (0, 0)),
        ],
        out_specs=[
            pl.BlockSpec((groups, 16, GROUP * H), lambda i: (0, i, 0)),
            pl.BlockSpec((own, H), lambda i: (0, 0)),
        ],
        scratch_shapes=[pltpu.VMEM((16, own, H), BF16)],
        compiler_params=params(),
        cost_estimate=cost(6),
    )

    part = jnp.zeros((holders * own, H), F32)
    first = jnp.concatenate([jnp.zeros((24, H), F32), flag], axis=0)
    count = groups // BACK
    edge_parts = []
    pending = []

    def back_step(n, wide, bias, part, first):
        at = slice(n * count, (n + 1) * count)
        part, first, edge_part = pl.pallas_call(
            functools.partial(back_kernel, shape, count),
            name="edge_gradients",
            out_shape=[
                jax.ShapeDtypeStruct((holders * own, H), F32),
                jax.ShapeDtypeStruct((32, H), F32),
                jax.ShapeDtypeStruct((count, 16, lanes), F32),
            ],
            grid=(1,),
            in_specs=[
                pl.BlockSpec((count, H, GROUP * H), lambda i: (n, 0, 0)),
                pl.BlockSpec((count * GROUP, H), lambda i: (n, 0)),
                pl.BlockSpec((16, H), lambda i: (0, 0)),
                pl.BlockSpec((1, H), lambda i: (0, 0)),
                pl.BlockSpec((count, H, lanes), lambda i: (n, 0, 0)),
                pl.BlockSpec((count, H, lanes), lambda i: (n, 0, 0)),
                pl.BlockSpec((count, 32 + GROUP, lanes), lambda i: (n, 0, 0)),
                pl.BlockSpec((holders * own, H), lambda i: (0, 0)),
                pl.BlockSpec((32, H), lambda i: (0, 0)),
            ],
            out_specs=[
                pl.BlockSpec((holders * own, H), lambda i: (0, 0)),
                pl.BlockSpec((32, H), lambda i: (0, 0)),
                pl.BlockSpec((count, 16, lanes), lambda i: (0, 0, 0)),
            ],
            compiler_params=params(),
            cost_estimate=cost(24 // BACK),
        )(wide, bias, w_edge_in, b1, latent, near, meta, part, first)
        edge_parts.append(edge_part)
        return part, first

    steps = 4
    state = (d_agg, part, first)

    def work(step, state):
        if step == 0:
            d_agg, part, first = state
            state = (*matrix_gradients(d_agg, t_units, b2), part, first)
        wide, bias, part, first = state
        for n in range(step * BACK // steps, (step + 1) * BACK // steps):
            part, first = back_step(n, wide, bias, part, first)
        return wide, bias, part, first

    for step in range(steps):
        state = scatter_step(step, (state, functools.partial(work, step)))
    part, first = state[2:]

    keep_d, keep_e, send = pl.pallas_call(
        functools.partial(return_kernel, shape),
        name="returned",
        out_shape=[
            jax.ShapeDtypeStruct((holders // 2, own, H), BF16),
            jax.ShapeDtypeStruct((holders // 2, 16 * blocks, H), BF16),
            jax.ShapeDtypeStruct((holders // 2 * (own + 16 * blocks) + 32, H), BF16),
        ],
        in_specs=[smem()] + [vmem()] * (2 + BACK),
        out_specs=[vmem()] * 3,
        scratch_shapes=[pltpu.VMEM((holders, 16 * blocks, H), BF16)],
        compiler_params=params(),
        cost_estimate=cost(2),
    )(me_arr, part, first, *edge_parts)

    slabs = keep_e[:, None]
    mask, n, first = 1, holders // 2, rounded(first)
    while True:
        got = swap(send, mask, devices)
        cut = n * own
        keep_d = add([keep_d, got[:cut].reshape(n, own, H)])
        got_e = got[cut:-32].reshape(n, -1, 16 * blocks, H)
        slabs = jnp.concatenate([slabs, got_e], axis=1)
        first = rounded(first.astype(F32) + got[-32:].astype(F32))
        if n == 1:
            break
        mask, n = mask * 2, n // 2
        send = jnp.concatenate([keep_d[1::2].reshape(-1, H), slabs[1::2].reshape(-1, H), first], axis=0)
        keep_d, slabs = keep_d[0::2], slabs[0::2]
    mask = edge
    while mask < devices:
        first = rounded(first.astype(F32) + swap(first, mask, devices).astype(F32))
        mask *= 2
    first = first.astype(F32)
    state_grads, edge_grads = pl.pallas_call(
        functools.partial(gather_kernel, shape),
        name="slots_to_edges",
        out_shape=[
            jax.ShapeDtypeStruct((own, H), F32),
            jax.ShapeDtypeStruct((edge_feats.shape[2], edges), F32),
        ],
        in_specs=[smem()] + [vmem()] * 4,
        out_specs=[vmem()] * 2,
        scratch_shapes=[pltpu.VMEM((holders * 16 * blocks, H), BF16)],
        compiler_params=params(),
        cost_estimate=cost(3),
    )(me_arr, slot, direct, keep_d[0], slabs[0])

    whole = [add(t) for t in terms]
    for mask in rest:
        whole = [rounded(w.astype(F32) + swap(w, mask, devices).astype(F32)) for w in whole]
    return new_states, state_grads, edge_grads, first, gather_back(chunks, bits, devices, whole)


def gather_back(chunks, bits, devices, whole):
    for step in reversed(range(len(bits) - 1)):
        whole = [
            jnp.stack([w, swap(w, bits[chunk.order[step]], devices)], axis=0) for w, chunk in zip(whole, chunks)
        ]
    return whole


def finish(batch, edge, results):
    new_states, state_grads, edge_grads, first, whole = results
    bits, chunks, piece_arr = plan(batch, edge)
    devices = batch * edge
    pairs = []
    for c, chunk in enumerate(chunks):
        other = swap(whole[c], bits[-1], devices)
        pairs += [x.reshape(PIECES // 2, chunk.height, H) for x in (whole[c], other)]
    grad_w2, grad_wi, grad_wh, grad_b2, grad_bi, grad_bh = pl.pallas_call(
        functools.partial(assemble_kernel, chunks),
        name="assemble",
        in_specs=[smem()] + [vmem()] * (2 * len(chunks)),
        out_specs=[anywhere()] + [vmem()] * 5,
        scratch_shapes=[
            pltpu.VMEM((4, 2 * UNITS, H * H), F32),
            pltpu.VMEM((7, H, H), F32),
            pltpu.VMEM((PIECES, H), F32),
            pltpu.VMEM((256, 256), BF16),
            pltpu.SemaphoreType.DMA((4,)),
        ],
        out_shape=[jax.ShapeDtypeStruct((H, H * H), F32)]
        + [jax.ShapeDtypeStruct((H, 3 * H), F32)] * 2
        + [jax.ShapeDtypeStruct((H, H), F32)]
        + [jax.ShapeDtypeStruct((3 * H,), F32)] * 2,
        compiler_params=params(),
    )(piece_arr, *pairs)
    return (
        new_states[None],
        state_grads[None],
        jnp.swapaxes(edge_grads[None], 1, 2),
        first[0:16],
        first[16],
        grad_w2,
        grad_b2.reshape(-1),
        grad_wi,
        grad_wh,
        grad_bi,
        grad_bh,
    )


HIGH = lax.Precision.HIGHEST


def gated_update(mixed, prior, w_input, w_hidden, b_input, b_hidden):
    width = prior.shape[1]
    from_input = jnp.dot(mixed, w_input, precision=HIGH) + b_input
    from_state = jnp.dot(prior, w_hidden, precision=HIGH) + b_hidden
    reset = jax.nn.sigmoid(from_input[:, :width] + from_state[:, :width])
    update = jax.nn.sigmoid(from_input[:, width : 2 * width] + from_state[:, width : 2 * width])
    candidate = jnp.tanh(from_input[:, 2 * width :] + reset * from_state[:, 2 * width :])
    return (1.0 - update) * candidate + update * prior


def edge_hidden(feats, w_edge_in, b_edge_in):
    return jax.nn.silu(jnp.dot(feats, w_edge_in, precision=HIGH) + b_edge_in)


def pick_by(index_rows, piece):
    columns = lax.broadcasted_iota(jnp.int32, (1, piece.shape[0]), 1)
    onehot = (index_rows[:, None] == columns).astype(jnp.bfloat16)
    return jnp.dot(onehot, piece, preferred_element_type=jnp.float32)


def spread_by(index_rows, values, count):
    rows = lax.broadcasted_iota(jnp.int32, (count, 1), 0)
    onehot = (rows == index_rows[None, :]).astype(jnp.bfloat16)
    return jnp.dot(onehot, values, preferred_element_type=jnp.float32)


def from_all(x, edge):
    got = lax.all_to_all(jnp.broadcast_to(x[None], (edge,) + x.shape), "edge", 0, 0)
    return got.reshape((-1,) + x.shape[1:])


def to_owners(x, edge):
    got = lax.all_to_all(x.reshape((edge, -1) + x.shape[1:]), "edge", 0, 0)
    return jnp.sum(got.astype(F32), axis=0)


def slow_path(batch, edge, args):
    (states, edge_feats, molecule, source, target, edge_mask, w_edge_in, b_edge_in, w_edge_out, b_edge_out,
     w_input, w_hidden, b_input, b_hidden, cotangent) = args
    states_here = states[0]
    feats = edge_feats[0]
    source_ids = source[0]
    target_ids = target[0]
    width = states_here.shape[1]
    owned = states_here.shape[0]
    edges = source_ids.shape[0]
    block = min(512, edges)
    count = edges // block
    labels = from_all(molecule[0], edge)
    same = (jnp.take(labels, source_ids) == jnp.take(labels, target_ids)).astype(jnp.float32)
    valid = edge_mask[0].astype(jnp.float32) * same
    near = pick_by(source_ids, from_all(states_here, edge)).astype(
        jnp.bfloat16
    )
    hidden, edge_pull = jax.vjp(
        edge_hidden,
        feats.astype(jnp.float32),
        w_edge_in.astype(jnp.float32),
        b_edge_in.astype(jnp.float32),
    )
    latent_blocks = hidden.astype(jnp.bfloat16).reshape(count, block, -1)
    near_blocks = near.reshape(count, block, width)
    bias_out = b_edge_out.astype(jnp.float32)

    def expand(latent):
        flat = jnp.dot(latent, w_edge_out, preferred_element_type=jnp.float32) + bias_out
        return flat.astype(jnp.bfloat16).reshape(latent.shape[0], width, width)

    def apply(mats, vectors):
        return jnp.einsum("bij,bj->bi", mats, vectors, preferred_element_type=jnp.float32)

    outgoing = lax.map(lambda item: apply(expand(item[0]), item[1]), (latent_blocks, near_blocks))
    messages = (outgoing.reshape(edges, width) * valid[:, None]).astype(jnp.bfloat16)
    summed = to_owners(spread_by(target_ids, messages, edge * owned), edge)
    mixed = summed.astype(jnp.bfloat16).astype(jnp.float32)
    updated, update_pull = jax.vjp(
        gated_update,
        mixed,
        states_here.astype(jnp.float32),
        w_input.astype(jnp.float32),
        w_hidden.astype(jnp.float32),
        b_input.astype(jnp.float32),
        b_hidden.astype(jnp.float32),
    )
    new_states = updated.astype(jnp.bfloat16)
    d_mixed, d_direct, grad_wi, grad_wh, grad_bi, grad_bh = update_pull(
        cotangent[0].astype(jnp.float32)
    )
    pulled = pick_by(
        target_ids, from_all(d_mixed.astype(jnp.bfloat16), edge)
    )
    d_message = (pulled * valid[:, None]).astype(jnp.bfloat16)
    d_message_blocks = d_message.reshape(count, block, width)

    def backward_core(carry, mats, latent, vectors, d_out):
        grad_weight, grad_bias = carry
        outer = (
            d_out.astype(jnp.float32)[:, :, None] * vectors.astype(jnp.float32)[:, None, :]
        ).astype(jnp.bfloat16)
        flat = outer.reshape(latent.shape[0], width * width)
        d_latent = lax.dot_general(
            flat, w_edge_out, (((1,), (1,)), ((), ())), preferred_element_type=jnp.float32
        )
        grad_weight = grad_weight + lax.dot_general(
            latent, flat, (((0,), (0,)), ((), ())), preferred_element_type=jnp.float32
        )
        grad_bias = grad_bias + jnp.sum(flat.astype(jnp.float32), axis=0)
        d_vectors = jnp.einsum(
            "bij,bi->bj", mats, d_out, preferred_element_type=jnp.float32
        ).astype(jnp.bfloat16)
        return ((grad_weight, grad_bias), (d_latent, d_vectors))

    start_carry = (
        jnp.zeros((w_edge_out.shape[0], width * width), jnp.float32),
        jnp.zeros((width * width,), jnp.float32),
    )

    def backward_block(carry, item):
        return backward_core(carry, expand(item[0]), item[0], item[1], item[2])

    sums_out, per_edge = lax.scan(
        backward_block, start_carry, (latent_blocks, near_blocks, d_message_blocks)
    )
    grad_w2, grad_b2 = sums_out
    d_latent_all = per_edge[0].reshape(edges, -1)
    d_near_all = per_edge[1].reshape(edges, width)
    d_feats, grad_w1, grad_b1 = edge_pull(d_latent_all)
    returned = to_owners(spread_by(source_ids, d_near_all, owned * edge).astype(jnp.bfloat16), edge)
    state_grads = d_direct + returned

    bits, chunks, piece_arr = plan(batch, edge)
    devices = batch * edge
    pieces = grad_w2.reshape(PIECES, UNITS, H, H)
    small = jnp.concatenate([grad_wi, grad_wh, grad_b2.reshape(H, H)], axis=1).reshape(PIECES, UNITS, 7, H)
    small = small.transpose(0, 2, 1, 3).reshape(PIECES, 7 * UNITS, H)
    biases = jnp.concatenate([grad_bi, grad_bh]).reshape(6, H)
    biases = jnp.concatenate([biases, jnp.zeros((PIECES - 6, H), F32)], axis=0)[:, None]
    small = jnp.concatenate([small, biases, jnp.zeros((PIECES, EXTRA - 7 * UNITS - 1, H), F32)], axis=1)
    terms = []
    for chunk in chunks:
        block = pieces[:, :, chunk.first : chunk.first + chunk.rows].reshape(PIECES, -1, H)
        if chunk.extra:
            block = jnp.concatenate([block, small], axis=1)
        rel_of = sorted(range(PIECES // 2), key=chunk.place)
        order = jnp.array(rel_of + [PIECES // 2 + r for r in rel_of], jnp.int32)
        block = jnp.take(block, jnp.bitwise_xor(order, piece_arr[0]), axis=0).astype(BF16)
        shape = chunk.shape()
        kept, sent = block[: PIECES // 2].reshape(shape), block[PIECES // 2 :].reshape(shape)
        total = add([kept, swap(sent, bits[-1], devices)])
        for bit in chunk.order:
            total = add([total[0], swap(total[1], bits[bit], devices)])
        terms.append(total)
    first = jnp.concatenate([grad_w1, grad_b1[None], jnp.zeros((15, H), F32)], axis=0)
    for n in range(devices.bit_length() - 1):
        mask = 1 << n
        if mask not in bits:
            terms = [rounded(w.astype(F32) + swap(w, mask, devices).astype(F32)) for w in terms]
        first = first + swap(first, mask, devices)
    return new_states, state_grads, d_feats.T, first, gather_back(chunks, bits, devices, terms)


def per_device(batch, edge, *args):
    results = fast_path(batch, edge, args)
    overflow = results[3][24, 0] > 0.0
    results = lax.while_loop(
        lambda carry: carry[0], lambda carry: (jnp.bool_(False), slow_path(batch, edge, args)), (overflow, results)
    )[1]
    return finish(batch, edge, results)


def solution(mesh):
    batch, edge = mesh.shape["batch"], mesh.shape["edge"]
    nodes, edges, all_ = P("batch", "edge", None), P("batch", "edge"), P()
    return jax.shard_map(
        functools.partial(per_device, batch, edge),
        mesh=mesh,
        in_specs=(nodes, nodes, edges, edges, edges, edges) + (all_,) * 8 + (nodes,),
        out_specs=(nodes, nodes, nodes) + (all_,) * 8,
        check_vma=False,
    )
```

```python
import functools

import jax
import jax.numpy as jnp
from jax import lax
from jax.experimental import pallas as pl
from jax.experimental.pallas import tpu as pltpu
from jax.sharding import PartitionSpec as P

F32 = jnp.float32
BF16 = jnp.bfloat16
H = 128
CAP = 64
GROUP = 16
SUB = 8
SIDE = CAP // 2
PIECES = 32
UNITS = H // PIECES
EXTRA = 32
VMEM_LIMIT = 60 * 1024 * 1024
BACK = 2
UNROLL = 4
AGG = 32
WORK = {(0, 1): (0,), (1, 1): (1,)}
COST = 0.02
KSTEP = 32
MATRIX_FIRST = True


def nn(a, b):
    return lax.dot_general(a, b, (((1,), (0,)), ((), ())), preferred_element_type=F32)


def nt(a, b):
    return lax.dot_general(a, b, (((1,), (1,)), ((), ())), preferred_element_type=F32)


def eye(n):
    rows = lax.broadcasted_iota(jnp.int32, (n, n), 0)
    cols = lax.broadcasted_iota(jnp.int32, (n, n), 1)
    return jnp.where(rows == cols, 1.0, 0.0).astype(BF16)


def one_hot_rows(rel, count):
    rel = jnp.clip(rel, -1, count).astype(F32).astype(BF16)
    rows = lax.broadcasted_iota(jnp.int32, (count, rel.shape[1]), 0).astype(F32).astype(BF16)
    return jnp.where(rows == rel, jnp.ones((), BF16), jnp.zeros((), BF16))


def slot_hots(slot, count):
    return one_hot_rows(jnp.right_shift(slot, 7), count), one_hot_rows(jnp.bitwise_and(slot, H - 1), H)


def sort_kernel(shape, me_ref, target_ref, source_ref, mask_ref, label_ref, feats_ref, states_ref, out_ref, slot_ref, data_ref):
    holders, own, groups = shape
    blocks = groups // 2
    edges = target_ref.shape[1]
    target = target_ref[...]
    owner = jnp.right_shift(target, own.bit_length() - 1)
    local = jnp.bitwise_and(target, own - 1)
    bucket = owner * (2 * groups) + jnp.right_shift(local, 3)
    bucket = jnp.where(mask_ref[...] != 0, bucket, -1)
    buckets = holders * groups * 2
    turn = jnp.bitwise_and(me_ref[0], 3)

    block = 256
    rows = lax.broadcasted_iota(jnp.int32, (block, block), 0)
    cols = lax.broadcasted_iota(jnp.int32, (block, block), 1)
    upto = jnp.where(rows <= cols, 1.0, 0.0).astype(BF16)
    numbers = lax.broadcasted_iota(jnp.int32, (buckets, block), 0)
    carry = jnp.zeros((buckets, 1), F32)
    slots = []
    for b in range(edges // block):
        here = bucket[:, b * block : (b + 1) * block]
        hot = numbers == here
        within = nn(hot.astype(F32).astype(BF16), upto) + carry
        rank = jnp.sum(jnp.where(hot, within - 1.0, 0.0), axis=0, keepdims=True).astype(jnp.int32)
        carry = within[:, block - 1 : block]
        at = jnp.where(jnp.bitwise_and(here, 1) == 0, rank, CAP - 1 - rank)
        side = jnp.bitwise_and(jnp.bitwise_and(here, 2) + jnp.right_shift(at, 5) + turn, 3)
        place = jnp.right_shift(here, 2) * H + side * SIDE + jnp.bitwise_and(at, SIDE - 1)
        slots.append(jnp.where((here >= 0) & (rank < CAP), place, -1))
    both = carry + jnp.concatenate([carry[1:, :], carry[:1, :]], axis=0)
    first_of_two = jnp.bitwise_and(lax.broadcasted_iota(jnp.int32, (buckets, 1), 0), 1) == 0
    worst = jnp.max(jnp.where(first_of_two, both, 0.0), axis=0, keepdims=True)
    flag = jnp.where(worst > CAP, 1.0, 0.0)
    slot = jnp.concatenate(slots, axis=1)
    slot_ref[...] = slot

    data_ref[16:32, :] = jnp.zeros((16, edges), F32)
    data_ref[0:16, :] = feats_ref[...].astype(F32)
    source = source_ref[...]
    data_ref[16:17, :] = jnp.right_shift(source, 6).astype(F32)
    data_ref[17:18, :] = jnp.bitwise_and(source, 63).astype(F32)
    data_ref[18:19, :] = (local + 1).astype(F32)
    data = data_ref[...].astype(BF16)

    tags = []
    for t in range(own // H):
        label = label_ref[:, t * H : (t + 1) * H]
        tags += [jnp.right_shift(label, 6).astype(F32), jnp.bitwise_and(label, 63).astype(F32)]
    tags.append(jnp.broadcast_to(flag, (1, H)))
    tags.append(jnp.zeros((16 - 3 * blocks - len(tags), H), F32))
    high, low = slot_hots(slot, holders * blocks)
    together = min(4, holders)
    for s0 in range(0, holders, together):
        part = high[s0 * blocks : (s0 + together) * blocks, :]
        spread = (part[:, None, :] * data[None, :, :]).reshape(together * blocks * 32, edges)
        moved = nt(spread, low)
        for n in range(together):
            out = out_ref.at[s0 + n]
            out[0:own, :] = states_ref[...]
            ids = []
            for q in range(blocks):
                at = (n * blocks + q) * 32
                out[own + 16 * q : own + 16 * (q + 1), :] = moved[at : at + 16, :].astype(BF16)
                ids.append(moved[at + 16 : at + 19, :])
            out[own + 16 * blocks : own + 16 * blocks + 16, :] = jnp.concatenate(ids + tags, axis=0).astype(BF16)


def swap_rows(outer, inner, flip=None):
    n = outer * inner
    rows = lax.broadcasted_iota(jnp.int32, (n, n), 0)
    cols = lax.broadcasted_iota(jnp.int32, (n, n), 1)
    number = jnp.bitwise_and(rows, inner - 1)
    if flip is not None:
        number = jnp.bitwise_xor(number, flip)
    source = number * outer + jnp.right_shift(rows, inner.bit_length() - 1)
    return jnp.where(source == cols, 1.0, 0.0).astype(BF16)


def split_kernel(w_ref, out_ref, order_ref):
    @pl.when(pl.program_id(0) == 0)
    def _():
        order_ref[...] = swap_rows(16, 16)

    order = order_ref[...]
    for ib in range(0, H, 32):
        sides = []
        for half in range(2):
            rows = [w_ref[:, (ib + 16 * half + i) * H : (ib + 16 * half + i + 1) * H] for i in range(16)]
            sides.append(jnp.concatenate(rows, axis=0))
        moved = nn(order, jnp.concatenate(sides, axis=1)).astype(BF16)
        for half in range(2):
            at = ib + 16 * half
            out_ref[:, at : at + 16, :] = moved[:, half * H : (half + 1) * H].reshape(16, 16, H)


def front_kernel(shape, chunks, *refs):
    holders, own, groups = shape
    blocks = groups // 2
    refs = list(refs)
    take = lambda n: [refs.pop(0) for _ in range(n)]
    piece_ref, given, states_ref, own_label_ref, t_in, b2_ref, w1_ref, b1_ref, wi_ref, wh_ref, bi_ref, bh_ref, cot_ref = take(13)
    new_ref, direct_ref, d_ref, crossed_ref, lat_out, near_out, meta_out = take(7)
    outs = take(3 * len(chunks) + 1)
    table_ref, p_ref, sum_ref, small_ref, dt_ref, rows_ref, bias_ref, extra_ref, t_ref, lat_ref, near_ref, meta_ref = take(12)
    built = take(3 * len(chunks) + 1)
    (sems,) = refs
    waiting = []

    def copy(source, target):
        moving = pltpu.make_async_copy(source, target, sems.at[len(waiting)])
        moving.start()
        waiting.append(moving)
        return moving

    t_copy = copy(t_in, t_ref)

    nodes = holders * own
    lanes = holders * SIDE
    ident = eye(H)
    tags_at = own + 16 * blocks

    flag = jnp.zeros((1, 1), F32)
    for s in range(holders):
        tags = given[s, tags_at : tags_at + 16, :].astype(F32)
        flag = jnp.maximum(flag, tags[3 * blocks + 2 * (own // H) : 3 * blocks + 2 * (own // H) + 1, 0:1])
        for t in range(own // H):
            at = s * own + t * H
            table_ref[0:H, at : at + H] = nt(ident, given[s, t * H : (t + 1) * H, :]).astype(BF16)
            both = tags[3 * blocks + 2 * t : 3 * blocks + 2 * t + 2, :]
            table_ref[H : H + 16, at : at + H] = jnp.concatenate([both, jnp.zeros((14, H), F32)], axis=0).astype(BF16)
    for t in range(own // H):
        label = own_label_ref[:, t * H : (t + 1) * H]
        label = jnp.concatenate([jnp.right_shift(label, 6), jnp.bitwise_and(label, 63)], axis=0).astype(F32)
        cols = nt(ident, jnp.concatenate([label, jnp.zeros((14, H), F32)], axis=0).astype(BF16))
        small_ref[t * H : (t + 1) * H, 0:1] = cols[:, 0:1] * 64.0 + cols[:, 1:2]

    side = lax.broadcasted_iota(jnp.int32, (24, H), 1) // SIDE
    crossing = jnp.zeros((1, H), F32)
    for q in range(blocks):
        for s in range(0, holders, 4):
            parts = []
            for n in range(4):
                feats = given[s + n, own + 16 * q : own + 16 * (q + 1), :].astype(F32)
                ids = given[s + n, tags_at : tags_at + 16, :].astype(F32)[3 * q : 3 * q + 3, :]
                parts.append(jnp.concatenate([feats, ids, jnp.zeros((5, H), F32)], axis=0))
            at = slice(s // 4 * H, (s // 4 + 1) * H)
            for u in range(4):
                page = parts[(3 - u) % 4]
                for c in range(3):
                    page = jnp.where(side == c, parts[(c - u) % 4], page)
                meta_ref[4 * q + u, 0:24, at] = page
                low = float((4 * q + u) * SUB)
                node = page[18:19, :] - 1.0
                outside = (node >= 0.0) & ((node < low) | (node >= low + SUB))
                crossing = jnp.maximum(crossing, jnp.where(outside, 1.0, 0.0))
    crossed = jnp.max(crossing) > 0.0
    crossed_ref[0] = crossed.astype(jnp.int32)

    w1 = nt(ident, w1_ref[...]).astype(BF16)
    b1 = nt(ident, jnp.broadcast_to(b1_ref[...].astype(F32), (16, H)).astype(BF16))[:, 0:1]

    def both_pages(ref, g, rows):
        return jnp.concatenate([ref[2 * g + n, rows, :] for n in range(2)], axis=1)

    def group_step(usual, g, unused):
        data = both_pages(meta_ref, g, slice(0, 24))
        source = (data[16:17, :] * 64.0 + data[17:18, :]).astype(jnp.int32)
        picked = jnp.zeros((H + 16, 2 * lanes), F32)
        for c in range(0, nodes, 256):
            picked = picked + nn(table_ref[:, c : c + 256], one_hot_rows(source - c, 256))
        near = picked[0:H, :].astype(BF16)
        label = picked[H : H + 1, :] * 64.0 + picked[H + 1 : H + 2, :]
        inside = data[18:19, :] - 1.0 - (g * GROUP).astype(F32)
        numbers = lax.broadcasted_iota(jnp.int32, (GROUP, 2 * lanes), 0).astype(F32)
        own_label = small_ref[pl.ds(pl.multiple_of(g * GROUP, GROUP), GROUP), 0:1]
        member = jnp.where((numbers == inside) & (own_label == label), 1.0, 0.0)
        before = nn(w1, data[0:16, :].astype(BF16)) + b1
        latent = before / (1.0 + jnp.exp(-before))
        made = []
        for n in range(2):
            page = slice(n * lanes, (n + 1) * lanes)
            meta_ref[2 * g + n, 24:25, :] = source[:, page].astype(F32)
            meta_ref[2 * g + n, 32 : 32 + GROUP, :] = member[:, page]
            lat_ref[2 * g + n] = latent[:, page].astype(BF16)
            near_ref[2 * g + n] = near[:, page]
            mine = member[n * SUB : (n + 1) * SUB, :]
            if usual:
                units, states, mine = latent[:, page], near[:, page], mine[:, page]
            else:
                units, states = latent, near
            spread = (units[:, None, :] * mine[None, :, :]).reshape(H * SUB, -1).astype(BF16)
            made.append(nt(spread, states).reshape(H, SUB, H))
        at = pl.ds(pl.multiple_of(g * GROUP, GROUP), GROUP)
        p_ref[:, at, :] = jnp.concatenate(made, axis=1).astype(BF16)
        sum_ref[at, :] = nt(member.astype(BF16), near)
        return unused

    @pl.when(jnp.logical_not(crossed))
    def _():
        lax.fori_loop(0, groups, functools.partial(group_step, True), 0, unroll=UNROLL)

    @pl.when(crossed)
    def _():
        lax.fori_loop(0, groups, functools.partial(group_step, False), 0)

    copy(lat_ref, lat_out)
    copy(near_ref, near_out)
    copy(meta_ref, meta_out)

    def agg_step(n, total):
        left = jnp.concatenate([p_ref[n * AGG + m] for m in range(AGG)], axis=1)
        right = jnp.concatenate([t_ref[n * AGG + m] for m in range(AGG)], axis=1)
        return total + nt(left, right)

    total = nt(sum_ref[...].astype(BF16), b2_ref[...])
    t_copy.wait()
    total = lax.fori_loop(0, H // AGG, agg_step, total)

    mixed = total.astype(BF16)
    prior = states_ref[...]
    prior_f = prior.astype(F32)
    cot = cot_ref[...].astype(F32)
    wi, wh = wi_ref[...], wh_ref[...]
    gi = nn(mixed, wi) + bi_ref[...]
    gh = nn(prior, wh) + bh_ref[...]
    r = jax.nn.sigmoid(gi[:, 0:H] + gh[:, 0:H])
    u = jax.nn.sigmoid(gi[:, H : 2 * H] + gh[:, H : 2 * H])
    n = jnp.tanh(gi[:, 2 * H :] + r * gh[:, 2 * H :])
    new_ref[...] = ((1.0 - u) * n + u * prior_f).astype(BF16)
    d_pre = (1.0 - u) * cot * (1.0 - n * n)
    d_r = d_pre * gh[:, 2 * H :] * r * (1.0 - r)
    d_u = (prior_f - n) * cot * u * (1.0 - u)
    d_gi = jnp.concatenate([d_r, d_u, d_pre], axis=1)
    d_gh = jnp.concatenate([d_r, d_u, d_pre * r], axis=1)

    def halves(x):
        high = x.astype(BF16)
        return high, (x - high.astype(F32)).astype(BF16)

    def twice(x):
        return jnp.concatenate([x, x], axis=1)

    gi_high, gi_low = halves(d_gi)
    gh_high, gh_low = halves(d_gh)
    d_agg = nt(jnp.concatenate([gi_high, gi_low], axis=1), twice(wi)).astype(BF16)
    d_ref[...] = d_agg
    dt_ref[...] = nt(ident, d_agg).astype(BF16)
    direct_ref[...] = u * cot + nt(jnp.concatenate([gh_high, gh_low], axis=1), twice(wh))

    piece_me = piece_ref[0]
    joint = built[-1]

    def dest(c, rel):
        place = chunks[c].place(rel)
        if rel >= PIECES // 2:
            return joint, place, chunks[c].offset
        for n, count in enumerate((PIECES // 8, PIECES // 8, PIECES // 4)):
            if place < count:
                return built[3 * c + n], place, 0
            place -= count

    for rel in list(range(PIECES // 2, PIECES)) + list(range(PIECES // 2)):
        k0 = jnp.bitwise_xor(piece_me, rel) * UNITS
        for m in range(0, UNITS, 2):
            out = nn(dt_ref[...], jnp.concatenate([p_ref[k0 + m], p_ref[k0 + m + 1]], axis=1)).astype(BF16)
            for c, chunk in enumerate(chunks):
                ref, place, offset = dest(c, rel)
                for h in range(2):
                    start = offset + (m + h) * chunk.rows
                    ref[place, start : start + chunk.rows, :] = out[
                        chunk.first : chunk.first + chunk.rows, h * H : (h + 1) * H
                    ]
        if rel == PIECES // 2 - 1:
            for n in range(3):
                copy(built[n], outs[n])

    mixed_t = nt(ident, mixed).astype(BF16)
    prior_t = nt(ident, prior).astype(BF16)
    from_input = nn(twice(mixed_t), jnp.concatenate([gi_high, gi_low], axis=0))
    from_state = nn(twice(prior_t), jnp.concatenate([gh_high, gh_low], axis=0))
    for t in range(3):
        rows_ref[t] = from_input[:, t * H : (t + 1) * H]
        rows_ref[3 + t] = from_state[:, t * H : (t + 1) * H]
    rows_ref[6] = nn(dt_ref[...], sum_ref[...].astype(BF16))
    bias_ref[...] = jnp.zeros_like(bias_ref)
    for n, part in enumerate((d_gi, d_gh)):
        part = jnp.sum(part, axis=0, keepdims=True)
        for t in range(3):
            bias_ref[3 * n + t : 3 * n + t + 1, :] = part[:, t * H : (t + 1) * H]
    extra_ref[...] = jnp.zeros_like(extra_ref)
    extra_ref[29:30, :] = jnp.broadcast_to(flag, (1, H))
    last = chunks[-1]
    for rel in list(range(PIECES // 2, PIECES)) + list(range(PIECES // 2)):
        p = jnp.bitwise_xor(piece_me, rel)
        for t in range(7):
            extra_ref[UNITS * t : UNITS * (t + 1), :] = rows_ref[t, pl.ds(p * UNITS, UNITS), :]
        extra_ref[28:29, :] = bias_ref[pl.ds(p, 1), :]
        ref, place, offset = dest(len(chunks) - 1, rel)
        ref[place, offset + UNITS * last.rows : offset + last.height, :] = extra_ref[...].astype(BF16)
        if rel == PIECES - 1:
            copy(joint, outs[-1])
    for n in range(3, len(built) - 1):
        copy(built[n], outs[n])
    for moving in waiting[1:]:
        moving.wait()


def spread_kernel(shape, d_ref, t_ref, b2_ref, wide_ref, bias_ref, dp_ref, order_ref):
    holders, own, groups = shape
    d = d_ref[...]

    @pl.when(pl.program_id(0) == 0)
    def _():
        bias_ref[...] = nn(d, b2_ref[...])
        order_ref[...] = swap_rows(16, 16)

    order = order_ref[...]
    for n in range(0, t_ref.shape[0], 2):
        out = nn(d, jnp.concatenate([t_ref[n], t_ref[n + 1]], axis=1)).astype(BF16)
        dp_ref[n] = out[:, :H]
        dp_ref[n + 1] = out[:, H:]
    for k in range(0, t_ref.shape[0], 16):
        for g in range(0, groups, 2):
            sides = [dp_ref[k : k + 16, (g + n) * GROUP : (g + n + 1) * GROUP, :].reshape(256, H) for n in range(2)]
            moved = nn(order, jnp.concatenate(sides, axis=1)).astype(BF16)
            for n in range(2):
                for v in range(GROUP):
                    wide_ref[g + n, k : k + 16, v * H : (v + 1) * H] = moved[v * 16 : (v + 1) * 16, n * H : (n + 1) * H]


def back_kernel(shape, count, begins, *refs):
    holders, own, groups = shape
    crossed_ref, wide_ref, bias_ref, w1_ref, b1_ref, lat_ref, near_ref, meta_ref = refs[:8]
    part_ref, first_ref, edge_ref = refs[-3:]
    nodes = holders * own
    lanes = holders * SIDE
    ident = eye(H)
    if begins:
        part_ref[...] = jnp.zeros_like(part_ref)
        first_ref[...] = jnp.zeros_like(first_ref)
    else:
        part_ref[...] = refs[8][...]
        first_ref[...] = refs[9][...]
    w1n = w1_ref[...]
    w1 = nt(ident, w1n).astype(BF16)
    b1 = nt(ident, jnp.broadcast_to(b1_ref[...].astype(F32), (16, H)).astype(BF16))[:, 0:1]
    one_row = jnp.where(lax.broadcasted_iota(jnp.int32, (16, 2 * lanes), 0) == 0, 1.0, 0.0).astype(BF16)

    def both_pages(ref, g, rows):
        return jnp.concatenate([ref[2 * g + n, rows, :] for n in range(2)], axis=1)

    def group_step(usual, g, first_total):
        wide = wide_ref[g]
        wide_t = jnp.concatenate([wide[:, v * H : (v + 1) * H].T for v in range(GROUP)], axis=1)
        bias_rows = bias_ref[pl.ds(pl.multiple_of(g * GROUP, GROUP), GROUP), :].astype(BF16)
        bias_t = nt(ident, bias_rows).astype(BF16)
        data = both_pages(meta_ref, g, slice(0, 16)).astype(BF16)
        source = both_pages(meta_ref, g, slice(24, 25)).astype(jnp.int32)
        member = both_pages(meta_ref, g, slice(32, 32 + GROUP)).astype(BF16)
        d_latent, d_near = [], []
        for n in range(2):
            low, number = (n * SUB, SUB) if usual else (0, GROUP)
            mine = meta_ref[2 * g + n, 32 + low : 32 + low + number, :].astype(BF16)
            part = slice(low * H, (low + number) * H)
            spread = (near_ref[2 * g + n][None, :, :] * mine[:, None, :]).reshape(number * H, lanes)
            d_latent.append(nn(wide[:, part], spread))
            spread = (lat_ref[2 * g + n][None, :, :] * mine[:, None, :]).reshape(number * H, lanes)
            d_near.append(nn(wide_t[:, part], spread))
        d_latent = jnp.concatenate(d_latent, axis=1)
        d_near = (jnp.concatenate(d_near, axis=1) + nn(bias_t, member)).astype(BF16)
        for c in range(0, nodes, 256):
            part_ref[c : c + 256, :] += nt(one_hot_rows(source - c, 256), d_near)
        before = nn(w1, data) + b1
        gate = 1.0 / (1.0 + jnp.exp(-before))
        d_before = (d_latent * gate * (1.0 + before * (1.0 - gate))).astype(BF16)
        edges = nn(w1n, d_before)
        for n in range(2):
            edge_ref[2 * g + n] = edges[:, n * lanes : (n + 1) * lanes]
        return first_total + nt(jnp.concatenate([data, one_row], axis=0), d_before)

    @pl.when(crossed_ref[0] == 0)
    def _():
        first_ref[...] = lax.fori_loop(
            0, count, functools.partial(group_step, True), first_ref[...], unroll=min(2, count)
        )

    @pl.when(crossed_ref[0] != 0)
    def _():
        first_ref[...] = lax.fori_loop(0, count, functools.partial(group_step, False), first_ref[...])


def return_kernel(shape, masks, me_ref, part_ref, *refs):
    holders, own, groups = shape
    blocks = groups // 2
    edges, (keep_d, keep_e, send_ref, slab_ref) = refs[:-4], refs[-4:]
    side = lax.broadcasted_iota(jnp.int32, (16, H), 1) // SIDE
    each = 2 * groups // len(edges)
    for q in range(blocks):
        for s in range(holders):
            at = slice(s // 4 * H, (s // 4 + 1) * H)
            parts = [edges[(4 * q + u) // each][(4 * q + u) % each, :, at] for u in range(4)]
            page = parts[(3 - s) % 4]
            for c in range(3):
                page = jnp.where(side == c, parts[(c - s) % 4], page)
            slab_ref[s, 16 * q : 16 * (q + 1), :] = page.astype(BF16)
    half = holders // 2
    for n in range(holders):
        rel = sum(mask for i, mask in enumerate(reversed(masks)) if n >> i & 1)
        h = jnp.bitwise_xor(me_ref[0], rel)
        rows = part_ref[pl.ds(pl.multiple_of(h * own, own), own), :].astype(BF16)
        if n < half:
            keep_d[n] = rows
            keep_e[n] = slab_ref[h]
        else:
            send_ref[(n - half) * own : (n - half + 1) * own, :] = rows
            at = half * own + (n - half) * 16 * blocks
            send_ref[at : at + 16 * blocks, :] = slab_ref[h]


def gather_kernel(shape, sources, me_ref, slot_ref, direct_ref, part_ref, slabs_ref, state_ref, edge_ref, data_ref):
    holders, own, groups = shape
    blocks = groups // 2
    state_ref[...] = direct_ref[...] + part_ref[...].astype(F32)
    for n, rel in enumerate(sources):
        h = jnp.bitwise_xor(me_ref[0], rel)
        data_ref[pl.ds(pl.multiple_of(h * 16 * blocks, 16), 16 * blocks), :] = slabs_ref[n]
    edges = slot_ref.shape[1]
    data = data_ref[...]
    count = holders * blocks
    block = 512
    for b in range(edges // block):
        high, low = slot_hots(slot_ref[:, b * block : (b + 1) * block], count)
        high = high.astype(F32)
        found = nn(data, low)
        total = jnp.zeros((16, block), F32)
        for n in range(count):
            total = total + found[16 * n : 16 * (n + 1), :] * high[n : n + 1, :]
        edge_ref[:, b * block : (b + 1) * block] = total


class Chunk:
    def __init__(self, first, rows, extra, order, offset):
        self.first, self.rows, self.extra, self.order, self.offset = first, rows, extra, order, offset
        self.height = UNITS * rows + extra

    def place(self, rel):
        at = 0
        for bit in self.order:
            at = at * 2 + (rel >> bit & 1)
        return at

    def shape(self):
        return (2,) * len(self.order) + (self.height, H)


def plan(batch, edge):
    core, x = [edge], [edge << n for n in range(1, batch.bit_length() - 1)]
    z = [2 << n for n in reversed(range(3 - len(x)))]
    bits = z + [1] + x + core
    chunks = [Chunk(0, 64, 0, (3, 2, 1, 0), 0), Chunk(64, 64, EXTRA, (2, 3, 1, 0), 64 * UNITS)]
    device = lax.axis_index(("batch", "edge")).astype(jnp.int32)
    piece = sum(jnp.where(device & mask != 0, 1 << n, 0) for n, mask in enumerate(bits))
    return bits, chunks, piece.astype(jnp.int32).reshape(1)


def swap(x, mask, devices):
    return lax.ppermute(x, ("batch", "edge"), [(i, i ^ mask) for i in range(devices)])


def add(terms):
    total = terms[0].astype(F32)
    for term in terms[1:]:
        total = total + term.astype(F32)
    return total.astype(BF16)


def rounded(x):
    return lax.reduce_precision(x.astype(F32), 8, 7).astype(BF16)


def unpack(chunks, half, me, order_ref, given, block_refs, w_out, rows_ref, sems, beside=lambda: None):
    steps = PIECES // 8
    width = 4 * UNITS

    def coming(step):
        copies = []
        for c, chunk in enumerate(chunks):
            at = pl.ds(chunk.place(4 * step), 4)
            copies.append(pltpu.make_async_copy(given[c].at[at], block_refs[c].at[at], sems.at[2 + len(chunks) * step + c]))
        return copies

    def leaving(step):
        start = jnp.bitwise_xor(jnp.right_shift(me, 2), step + half * steps) * width
        rows = pl.ds(pl.multiple_of(start, width), width)
        return pltpu.make_async_copy(rows_ref.at[step % 2], w_out.at[rows, :], sems.at[step % 2])

    for step in range(steps):
        for copy in coming(step):
            copy.start()
    order_ref[...] = swap_rows(32, 2 * UNITS, jnp.bitwise_and(me, 1) * UNITS)
    beside()
    for step in range(steps):
        for copy in coming(step):
            copy.wait()
        if step >= 2:
            leaving(step - 2).wait()
        for pair in range(2):
            rel = 4 * step + 2 * pair
            places = [[chunk.place(rel + n) for n in range(2)] for chunk in chunks]
            upper = jnp.bitwise_xor(jnp.bitwise_and(jnp.right_shift(me, 1), 1), pair)
            at_rows = pl.ds(pl.multiple_of(upper * 2 * UNITS, 2 * UNITS), 2 * UNITS)
            for ib in range(0, H, 64):
                sides = []
                for side in range(2):
                    at = ib + 32 * side
                    c = max(n for n in range(len(chunks)) if chunks[n].first <= at)
                    first, rows = chunks[c].first, chunks[c].rows
                    parts = [
                        block_refs[c][places[c][n], m * rows + at - first : m * rows + at - first + 32, :]
                        for n in range(2)
                        for m in range(UNITS)
                    ]
                    sides.append(jnp.concatenate(parts, axis=0))
                moved = nn(order_ref[...], jnp.concatenate(sides, axis=1))
                for side in range(2):
                    for i in range(32):
                        at = (ib + 32 * side + i) * H
                        rows_ref[step % 2, at_rows, at : at + H] = moved[8 * i : 8 * (i + 1), side * H : (side + 1) * H]
        leaving(step).start()

    def end():
        for step in range(steps - 2, steps):
            leaving(step).wait()

    return end


def small_pieces(chunks, half, me, block_refs, extra_ref, bias_ref):
    last = chunks[-1]
    start = UNITS * last.rows
    for n in range(PIECES // 2):
        extra = block_refs[-1][last.place(n), start : start + EXTRA, :].astype(F32)
        p = jnp.bitwise_xor(me, n + half * PIECES // 2)
        for t in range(7):
            extra_ref[t, pl.ds(p * UNITS, UNITS), :] = extra[UNITS * t : UNITS * (t + 1), :]
        bias_ref[pl.ds(p, 1), :] = extra[28:29, :]


def own_half_kernel(chunks, piece_ref, *refs):
    count = len(chunks)
    given, (w_out, extra_ref, bias_ref) = refs[:count], refs[count : count + 3]
    block_refs, (rows_ref, order_ref, sems) = refs[count + 3 : 2 * count + 3], refs[2 * count + 3 :]
    me = piece_ref[0]
    extra_ref[...] = jnp.zeros_like(extra_ref)
    bias_ref[...] = jnp.zeros_like(bias_ref)
    end = unpack(chunks, 0, me, order_ref, given, block_refs, w_out, rows_ref, sems)
    small_pieces(chunks, 0, me, block_refs, extra_ref, bias_ref)
    end()


def other_half_kernel(chunks, piece_ref, *refs):
    count = len(chunks)
    given, (first_ref, extra_in, bias_in, w_in) = refs[:count], refs[count : count + 4]
    w_out, w1_ref, b1_ref, wi_ref, wh_ref, b2_ref, bi_ref, bh_ref = refs[count + 4 : count + 12]
    block_refs = refs[count + 12 : 2 * count + 12]
    rows_ref, order_ref, extra_ref, bias_ref, sems = refs[2 * count + 12 :]
    me = piece_ref[0]

    def beside():
        w1_ref[...] = first_ref[0:16, :].astype(F32)
        b1_ref[...] = first_ref[16:17, :].astype(F32).reshape(H)
        extra_ref[...] = extra_in[...]
        bias_ref[...] = bias_in[...]

    end = unpack(chunks, 1, me, order_ref, given, block_refs, w_out, rows_ref, sems, beside)
    small_pieces(chunks, 1, me, block_refs, extra_ref, bias_ref)
    for t in range(3):
        wi_ref[:, t * H : (t + 1) * H] = extra_ref[t]
        wh_ref[:, t * H : (t + 1) * H] = extra_ref[3 + t]
        bi_ref[t * H : (t + 1) * H] = bias_ref[t : t + 1, :].reshape(H)
        bh_ref[t * H : (t + 1) * H] = bias_ref[3 + t : 4 + t, :].reshape(H)
    b2_ref[...] = extra_ref[6]
    end()


def vmem():
    return pl.BlockSpec(memory_space=pltpu.VMEM)


def anywhere():
    return pl.BlockSpec(memory_space=pl.ANY)


def smem():
    return pl.BlockSpec(memory_space=pltpu.SMEM)


def cost(us):
    return pl.CostEstimate(flops=int(us * COST * 1e9), bytes_accessed=int(us * COST * 3e6), transcendentals=0)


def params():
    return pltpu.CompilerParams(vmem_limit_bytes=VMEM_LIMIT)


def fast_path(batch, edge, args):
    (states, edge_feats, molecule, source, target, edge_mask, w_edge_in, b_edge_in, w_edge_out, b_edge_out,
     w_input, w_hidden, b_input, b_hidden, cotangent) = args
    devices = batch * edge
    states_here = states[0]
    own = states_here.shape[0]
    edges = source.shape[1]
    holders, groups = edge, own // GROUP
    shape = (holders, own, groups)
    blocks = groups // 2
    bits, chunks, piece_arr = plan(batch, edge)
    rest = [m for m in (1 << n for n in range(devices.bit_length() - 1)) if m not in bits]
    me_arr = lax.axis_index("edge").astype(jnp.int32).reshape(1)
    lanes = holders * SIDE
    pages = 2 * groups

    slots_out, slot = pl.pallas_call(
        functools.partial(sort_kernel, shape),
        name="edges_to_slots",
        out_shape=[
            jax.ShapeDtypeStruct((holders, own + 16 * blocks + 16, H), BF16),
            jax.ShapeDtypeStruct((1, edges), jnp.int32),
        ],
        in_specs=[smem()] + [vmem()] * 6,
        out_specs=[vmem()] * 2,
        scratch_shapes=[pltpu.VMEM((32, edges), F32)],
        compiler_params=params(),
    )(me_arr, target, source, edge_mask, molecule, jnp.swapaxes(edge_feats, 1, 2)[0], states_here)
    given = lax.all_to_all(slots_out, "edge", 0, 0)

    t_units = pl.pallas_call(
        split_kernel,
        name="split_weight",
        grid=(H // 16,),
        in_specs=[pl.BlockSpec((16, H * H), lambda i: (i, 0))],
        out_specs=pl.BlockSpec((16, H, H), lambda i: (i, 0, 0)),
        out_shape=jax.ShapeDtypeStruct((H, H, H), BF16),
        scratch_shapes=[pltpu.VMEM((256, 256), BF16)],
        compiler_params=params(),
        cost_estimate=cost(6),
    )(w_edge_out)
    b2 = b_edge_out.reshape(H, H)
    b1 = b_edge_in.reshape(1, H)
    built = [jax.ShapeDtypeStruct((PIECES // n, c.height, H), BF16) for c in chunks for n in (8, 8, 4)]
    built.append(jax.ShapeDtypeStruct((PIECES // 2, sum(c.height for c in chunks), H), BF16))
    front = pl.pallas_call(
        functools.partial(front_kernel, shape, chunks),
        name="messages_update_weight_gradient",
        out_shape=[
            jax.ShapeDtypeStruct((own, H), BF16),
            jax.ShapeDtypeStruct((own, H), F32),
            jax.ShapeDtypeStruct((own, H), BF16),
            jax.ShapeDtypeStruct((1,), jnp.int32),
            jax.ShapeDtypeStruct((pages, H, lanes), BF16),
            jax.ShapeDtypeStruct((pages, H, lanes), BF16),
            jax.ShapeDtypeStruct((pages, 32 + GROUP, lanes), F32),
        ]
        + built,
        in_specs=[smem()] + [vmem()] * 3 + [anywhere()] + [vmem()] * 8,
        out_specs=[vmem()] * 3 + [smem()] + [anywhere()] * (3 + len(built)),
        scratch_shapes=[
            pltpu.VMEM((H + 16, holders * own), BF16),
            pltpu.VMEM((H, own, H), BF16),
            pltpu.VMEM((own, H), F32),
            pltpu.VMEM((own, H), F32),
            pltpu.VMEM((H, own), BF16),
            pltpu.VMEM((7, H, H), F32),
            pltpu.VMEM((PIECES, H), F32),
            pltpu.VMEM((EXTRA, H), F32),
            pltpu.VMEM((H, H, H), BF16),
            pltpu.VMEM((pages, H, lanes), BF16),
            pltpu.VMEM((pages, H, lanes), BF16),
            pltpu.VMEM((pages, 32 + GROUP, lanes), F32),
        ]
        + [pltpu.VMEM(h.shape, BF16) for h in built]
        + [pltpu.SemaphoreType.DMA((4 + len(built),))],
        compiler_params=params(),
    )(
        piece_arr, given, states_here, molecule, t_units, b2, w_edge_in, b1, w_input, w_hidden,
        b_input.astype(F32).reshape(1, -1), b_hidden.astype(F32).reshape(1, -1), cotangent[0],
    )
    new_states, direct, d_agg, crossed, latent, near, meta = front[:7]
    built = front[7:]

    matrix_gradients = pl.pallas_call(
        functools.partial(spread_kernel, shape),
        name="matrix_gradients",
        out_shape=[jax.ShapeDtypeStruct((groups, H, GROUP * H), BF16), jax.ShapeDtypeStruct((own, H), F32)],
        grid=(H // KSTEP,),
        in_specs=[
            pl.BlockSpec((own, H), lambda i: (0, 0)),
            pl.BlockSpec((KSTEP, H, H), lambda i: (i, 0, 0)),
            pl.BlockSpec((H, H), lambda i: (0, 0)),
        ],
        out_specs=[
            pl.BlockSpec((groups, KSTEP, GROUP * H), lambda i: (0, i, 0)),
            pl.BlockSpec((own, H), lambda i: (0, 0)),
        ],
        scratch_shapes=[pltpu.VMEM((KSTEP, own, H), BF16), pltpu.VMEM((256, 256), BF16)],
        compiler_params=params(),
        cost_estimate=cost(6),
    )

    count = groups // BACK
    edge_parts = []
    pending = []

    def back_step(n, wide, bias, sums):
        whole_spec = lambda shp: pl.BlockSpec(shp, lambda i: (0, 0))
        *sums, edge_part = pl.pallas_call(
            functools.partial(back_kernel, shape, count, not sums),
            name="edge_gradients",
            out_shape=[
                jax.ShapeDtypeStruct((holders * own, H), F32),
                jax.ShapeDtypeStruct((32, H), F32),
                jax.ShapeDtypeStruct((2 * count, 16, lanes), F32),
            ],
            grid=(1,),
            in_specs=[
                smem(),
                pl.BlockSpec((count, H, GROUP * H), lambda i: (n, 0, 0)),
                pl.BlockSpec((count * GROUP, H), lambda i: (n, 0)),
                whole_spec((16, H)),
                whole_spec((1, H)),
                pl.BlockSpec((2 * count, H, lanes), lambda i: (n, 0, 0)),
                pl.BlockSpec((2 * count, H, lanes), lambda i: (n, 0, 0)),
                pl.BlockSpec((2 * count, 32 + GROUP, lanes), lambda i: (n, 0, 0)),
            ]
            + [whole_spec((holders * own, H)), whole_spec((32, H))][: len(sums)],
            out_specs=[
                whole_spec((holders * own, H)),
                whole_spec((32, H)),
                pl.BlockSpec((2 * count, 16, lanes), lambda i: (0, 0, 0)),
            ],
            compiler_params=params(),
            cost_estimate=cost(24 // BACK),
        )(crossed, wide, bias, w_edge_in, b1, latent, near, meta, *sums)
        edge_parts.append(edge_part)
        return tuple(sums)

    if MATRIX_FIRST:
        sent, d_agg = lax.optimization_barrier((built[-1], d_agg))
        other = swap(sent, bits[-1], devices)
        other, (wide, bias) = lax.optimization_barrier((other, matrix_gradients(d_agg, t_units, b2)))
    else:
        other = swap(built[-1], bits[-1], devices)
        wide, bias = matrix_gradients(d_agg, t_units, b2)
    other = other.reshape((2,) * 4 + (-1, H))
    kept = [
        {(0, 0): built[3 * c], (0, 1): built[3 * c + 1], (1,): built[3 * c + 2]} for c in range(len(chunks))
    ]
    got = [[] for _ in chunks]

    def mine(c, path):
        for head, x in kept[c].items():
            if path[: len(head)] == head:
                return x.reshape((2,) * (4 - len(head)) + x.shape[1:])[path[len(head) :]]

    def partial_sum(c, path):
        rows = slice(chunks[c].offset, chunks[c].offset + chunks[c].height)
        parts = [mine(c, path), other[path][..., rows, :]]
        for n, x in enumerate(got[c]):
            parts.append(x[path[n + 1 :]])
        return add(parts)

    def scatter_step(c, step, work=None, given=()):
        begun = partial_sum(c, (0,) * step + (1,))
        mask = bits[chunks[c].order[step]]
        if work is None:
            got[c].append(swap(begun, mask, devices))
            return None
        begun, given = lax.optimization_barrier((begun, given))
        new, result = lax.optimization_barrier((swap(begun, mask, devices), work(*given)))
        got[c].append(new)
        return result

    def work_on(numbers, wide, bias):
        def run(*sums):
            for n in numbers:
                sums = back_step(n, wide, bias, sums)
            return sums

        return run

    def gather_step(x, mask):
        return jnp.stack([x, swap(x, mask, devices)], axis=0)

    back_masks = [m for m in (1 << n for n in range(edge.bit_length() - 1))]

    def send_back(part, *edge_parts):
        return pl.pallas_call(
            functools.partial(return_kernel, shape, back_masks),
            name="returned",
            out_shape=[
                jax.ShapeDtypeStruct((holders // 2, own, H), BF16),
                jax.ShapeDtypeStruct((holders // 2, 16 * blocks, H), BF16),
                jax.ShapeDtypeStruct((holders // 2 * (own + 16 * blocks), H), BF16),
            ],
            in_specs=[smem()] + [vmem()] * (1 + BACK),
            out_specs=[vmem()] * 3,
            scratch_shapes=[pltpu.VMEM((holders, 16 * blocks, H), BF16)],
            compiler_params=params(),
            cost_estimate=cost(2),
        )(me_arr, part, *edge_parts)

    sums = ()
    for step in range(4):
        for c in range(len(chunks)):
            if (step, c) in WORK:
                sums = scatter_step(c, step, work_on(WORK[step, c], wide, bias), sums)
            else:
                scatter_step(c, step)
    parts = [partial_sum(c, (0,) * 4) for c in range(len(chunks))]
    for mask in rest:
        parts = [rounded(x.astype(F32) + swap(x, mask, devices).astype(F32)) for x in parts]
    overflow = parts[-1][UNITS * chunks[-1].rows + 29, 0] > 0.0
    for step in (3, 2, 1, 0):
        for c, chunk in enumerate(chunks):
            parts[c] = gather_step(parts[c], bits[chunk.order[step]])
    part, first = sums
    keep_d, keep_e, send = send_back(part, *edge_parts)

    first = rounded(first)
    slabs, sources = keep_e[:, None], [0]
    for mask in back_masks:
        n = keep_d.shape[0]
        cut = n * own
        arrived = swap(jnp.concatenate([send, first], axis=0), mask, devices)
        keep_d = add([keep_d, arrived[:cut].reshape(n, own, H)])
        slabs = jnp.concatenate([slabs, arrived[cut:-32].reshape(n, -1, 16 * blocks, H)], axis=1)
        first = rounded(first.astype(F32) + arrived[-32:].astype(F32))
        sources = sources + [s ^ mask for s in sources]
        if n > 1:
            send = jnp.concatenate([keep_d[n // 2 :].reshape(-1, H), slabs[n // 2 :].reshape(-1, H)], axis=0)
            keep_d, slabs = keep_d[: n // 2], slabs[: n // 2]
    mask = edge
    while mask < devices:
        first = rounded(first.astype(F32) + swap(first, mask, devices).astype(F32))
        mask *= 2
    state_grads, edge_grads = pl.pallas_call(
        functools.partial(gather_kernel, shape, sources),
        name="slots_to_edges",
        out_shape=[
            jax.ShapeDtypeStruct((own, H), F32),
            jax.ShapeDtypeStruct((edge_feats.shape[2], edges), F32),
        ],
        in_specs=[smem()] + [vmem()] * 4,
        out_specs=[vmem()] * 2,
        scratch_shapes=[pltpu.VMEM((holders * 16 * blocks, H), BF16)],
        compiler_params=params(),
        cost_estimate=cost(3),
    )(me_arr, slot, direct, keep_d[0], slabs[0])
    return overflow, (new_states, state_grads, edge_grads, first, parts)


def gather_back(chunks, bits, devices, whole):
    for step in reversed(range(len(bits) - 1)):
        whole = [
            jnp.stack([w, swap(w, bits[chunk.order[step]], devices)], axis=0) for w, chunk in zip(whole, chunks)
        ]
    return whole


def finish(batch, edge, results):
    new_states, state_grads, edge_grads, first, whole = results
    bits, chunks, piece_arr = plan(batch, edge)
    devices = batch * edge
    whole = [x.reshape(PIECES // 2, chunk.height, H) for x, chunk in zip(whole, chunks)]
    others = [swap(x, bits[-1], devices) for x in whole]
    small = [jax.ShapeDtypeStruct((7, H, H), F32), jax.ShapeDtypeStruct((PIECES, H), F32)]
    scratch = [pltpu.VMEM((PIECES // 2, chunk.height, H), BF16) for chunk in chunks] + [
        pltpu.VMEM((2, 4 * UNITS, H * H), F32),
        pltpu.VMEM((256, 256), BF16),
    ]
    semaphores = [pltpu.SemaphoreType.DMA((2 + len(chunks) * PIECES // 8,))]
    grad_w2, extras, biases = pl.pallas_call(
        functools.partial(own_half_kernel, chunks),
        name="assemble_own_half",
        in_specs=[smem()] + [anywhere()] * len(chunks),
        out_specs=[anywhere(), vmem(), vmem()],
        scratch_shapes=scratch + semaphores,
        out_shape=[jax.ShapeDtypeStruct((H, H * H), F32)] + small,
        compiler_params=params(),
        cost_estimate=cost(4),
    )(piece_arr, *whole)
    grad_w2, grad_w1, grad_b1, grad_wi, grad_wh, grad_b2, grad_bi, grad_bh = pl.pallas_call(
        functools.partial(other_half_kernel, chunks),
        name="assemble_other_half",
        in_specs=[smem()] + [anywhere()] * len(chunks) + [vmem()] * 3 + [anywhere()],
        out_specs=[anywhere()] + [vmem()] * 7,
        scratch_shapes=scratch + [pltpu.VMEM(x.shape, F32) for x in small] + semaphores,
        out_shape=[
            jax.ShapeDtypeStruct((H, H * H), F32),
            jax.ShapeDtypeStruct((16, H), F32),
            jax.ShapeDtypeStruct((H,), F32),
        ]
        + [jax.ShapeDtypeStruct((H, 3 * H), F32)] * 2
        + [jax.ShapeDtypeStruct((H, H), F32)]
        + [jax.ShapeDtypeStruct((3 * H,), F32)] * 2,
        input_output_aliases={len(chunks) + 4: 0},
        compiler_params=params(),
    )(piece_arr, *others, first, extras, biases, grad_w2)
    return (
        new_states[None],
        state_grads[None],
        jnp.swapaxes(edge_grads[None], 1, 2),
        grad_w1,
        grad_b1,
        grad_w2,
        grad_b2.reshape(-1),
        grad_wi,
        grad_wh,
        grad_bi,
        grad_bh,
    )


HIGH = lax.Precision.HIGHEST


def gated_update(mixed, prior, w_input, w_hidden, b_input, b_hidden):
    width = prior.shape[1]
    from_input = jnp.dot(mixed, w_input, precision=HIGH) + b_input
    from_state = jnp.dot(prior, w_hidden, precision=HIGH) + b_hidden
    reset = jax.nn.sigmoid(from_input[:, :width] + from_state[:, :width])
    update = jax.nn.sigmoid(from_input[:, width : 2 * width] + from_state[:, width : 2 * width])
    candidate = jnp.tanh(from_input[:, 2 * width :] + reset * from_state[:, 2 * width :])
    return (1.0 - update) * candidate + update * prior


def edge_hidden(feats, w_edge_in, b_edge_in):
    return jax.nn.silu(jnp.dot(feats, w_edge_in, precision=HIGH) + b_edge_in)


def pick_by(index_rows, piece):
    columns = lax.broadcasted_iota(jnp.int32, (1, piece.shape[0]), 1)
    onehot = (index_rows[:, None] == columns).astype(jnp.bfloat16)
    return jnp.dot(onehot, piece, preferred_element_type=jnp.float32)


def spread_by(index_rows, values, count):
    rows = lax.broadcasted_iota(jnp.int32, (count, 1), 0)
    onehot = (rows == index_rows[None, :]).astype(jnp.bfloat16)
    return jnp.dot(onehot, values, preferred_element_type=jnp.float32)


def from_all(x, edge):
    got = lax.all_to_all(jnp.broadcast_to(x[None], (edge,) + x.shape), "edge", 0, 0)
    return got.reshape((-1,) + x.shape[1:])


def to_owners(x, edge):
    got = lax.all_to_all(x.reshape((edge, -1) + x.shape[1:]), "edge", 0, 0)
    return jnp.sum(got.astype(F32), axis=0)


def slow_path(batch, edge, args):
    (states, edge_feats, molecule, source, target, edge_mask, w_edge_in, b_edge_in, w_edge_out, b_edge_out,
     w_input, w_hidden, b_input, b_hidden, cotangent) = args
    states_here = states[0]
    feats = edge_feats[0]
    source_ids = source[0]
    target_ids = target[0]
    width = states_here.shape[1]
    owned = states_here.shape[0]
    edges = source_ids.shape[0]
    block = min(512, edges)
    count = edges // block
    labels = from_all(molecule[0], edge)
    same = (jnp.take(labels, source_ids) == jnp.take(labels, target_ids)).astype(jnp.float32)
    valid = edge_mask[0].astype(jnp.float32) * same
    near = pick_by(source_ids, from_all(states_here, edge)).astype(
        jnp.bfloat16
    )
    hidden, edge_pull = jax.vjp(
        edge_hidden,
        feats.astype(jnp.float32),
        w_edge_in.astype(jnp.float32),
        b_edge_in.astype(jnp.float32),
    )
    latent_blocks = hidden.astype(jnp.bfloat16).reshape(count, block, -1)
    near_blocks = near.reshape(count, block, width)
    bias_out = b_edge_out.astype(jnp.float32)

    def expand(latent):
        flat = jnp.dot(latent, w_edge_out, preferred_element_type=jnp.float32) + bias_out
        return flat.astype(jnp.bfloat16).reshape(latent.shape[0], width, width)

    def apply(mats, vectors):
        return jnp.einsum("bij,bj->bi", mats, vectors, preferred_element_type=jnp.float32)

    outgoing = lax.map(lambda item: apply(expand(item[0]), item[1]), (latent_blocks, near_blocks))
    messages = (outgoing.reshape(edges, width) * valid[:, None]).astype(jnp.bfloat16)
    summed = to_owners(spread_by(target_ids, messages, edge * owned), edge)
    mixed = summed.astype(jnp.bfloat16).astype(jnp.float32)
    updated, update_pull = jax.vjp(
        gated_update,
        mixed,
        states_here.astype(jnp.float32),
        w_input.astype(jnp.float32),
        w_hidden.astype(jnp.float32),
        b_input.astype(jnp.float32),
        b_hidden.astype(jnp.float32),
    )
    new_states = updated.astype(jnp.bfloat16)
    d_mixed, d_direct, grad_wi, grad_wh, grad_bi, grad_bh = update_pull(
        cotangent[0].astype(jnp.float32)
    )
    pulled = pick_by(
        target_ids, from_all(d_mixed.astype(jnp.bfloat16), edge)
    )
    d_message = (pulled * valid[:, None]).astype(jnp.bfloat16)
    d_message_blocks = d_message.reshape(count, block, width)

    def backward_core(carry, mats, latent, vectors, d_out):
        grad_weight, grad_bias = carry
        outer = (
            d_out.astype(jnp.float32)[:, :, None] * vectors.astype(jnp.float32)[:, None, :]
        ).astype(jnp.bfloat16)
        flat = outer.reshape(latent.shape[0], width * width)
        d_latent = lax.dot_general(
            flat, w_edge_out, (((1,), (1,)), ((), ())), preferred_element_type=jnp.float32
        )
        grad_weight = grad_weight + lax.dot_general(
            latent, flat, (((0,), (0,)), ((), ())), preferred_element_type=jnp.float32
        )
        grad_bias = grad_bias + jnp.sum(flat.astype(jnp.float32), axis=0)
        d_vectors = jnp.einsum(
            "bij,bi->bj", mats, d_out, preferred_element_type=jnp.float32
        ).astype(jnp.bfloat16)
        return ((grad_weight, grad_bias), (d_latent, d_vectors))

    start_carry = (
        jnp.zeros((w_edge_out.shape[0], width * width), jnp.float32),
        jnp.zeros((width * width,), jnp.float32),
    )

    def backward_block(carry, item):
        return backward_core(carry, expand(item[0]), item[0], item[1], item[2])

    sums_out, per_edge = lax.scan(
        backward_block, start_carry, (latent_blocks, near_blocks, d_message_blocks)
    )
    grad_w2, grad_b2 = sums_out
    d_latent_all = per_edge[0].reshape(edges, -1)
    d_near_all = per_edge[1].reshape(edges, width)
    d_feats, grad_w1, grad_b1 = edge_pull(d_latent_all)
    returned = to_owners(spread_by(source_ids, d_near_all, owned * edge).astype(jnp.bfloat16), edge)
    state_grads = d_direct + returned

    bits, chunks, piece_arr = plan(batch, edge)
    devices = batch * edge
    pieces = grad_w2.reshape(PIECES, UNITS, H, H)
    small = jnp.concatenate([grad_wi, grad_wh, grad_b2.reshape(H, H)], axis=1).reshape(PIECES, UNITS, 7, H)
    small = small.transpose(0, 2, 1, 3).reshape(PIECES, 7 * UNITS, H)
    biases = jnp.concatenate([grad_bi, grad_bh]).reshape(6, H)
    biases = jnp.concatenate([biases, jnp.zeros((PIECES - 6, H), F32)], axis=0)[:, None]
    small = jnp.concatenate([small, biases, jnp.zeros((PIECES, EXTRA - 7 * UNITS - 1, H), F32)], axis=1)
    terms = []
    for chunk in chunks:
        block = pieces[:, :, chunk.first : chunk.first + chunk.rows].reshape(PIECES, -1, H)
        if chunk.extra:
            block = jnp.concatenate([block, small], axis=1)
        rel_of = sorted(range(PIECES // 2), key=chunk.place)
        order = jnp.array(rel_of + [PIECES // 2 + r for r in rel_of], jnp.int32)
        block = jnp.take(block, jnp.bitwise_xor(order, piece_arr[0]), axis=0).astype(BF16)
        shape = chunk.shape()
        kept, sent = block[: PIECES // 2].reshape(shape), block[PIECES // 2 :].reshape(shape)
        total = add([kept, swap(sent, bits[-1], devices)])
        for bit in chunk.order:
            total = add([total[0], swap(total[1], bits[bit], devices)])
        terms.append(total)
    first = jnp.concatenate([grad_w1, grad_b1[None], jnp.zeros((15, H), F32)], axis=0)
    for n in range(devices.bit_length() - 1):
        mask = 1 << n
        if mask not in bits:
            terms = [rounded(w.astype(F32) + swap(w, mask, devices).astype(F32)) for w in terms]
        first = first + swap(first, mask, devices)
    return new_states, state_grads, d_feats.T, first.astype(BF16), gather_back(chunks, bits, devices, terms)


def per_device(batch, edge, *args):
    overflow, results = fast_path(batch, edge, args)
    results = lax.while_loop(
        lambda carry: carry[0], lambda carry: (jnp.bool_(False), slow_path(batch, edge, args)), (overflow, results)
    )[1]
    return finish(batch, edge, results)


def solution(mesh):
    batch, edge = mesh.shape["batch"], mesh.shape["edge"]
    nodes, edges, all_ = P("batch", "edge", None), P("batch", "edge"), P()
    return jax.shard_map(
        functools.partial(per_device, batch, edge),
        mesh=mesh,
        in_specs=(nodes, nodes, edges, edges, edges, edges) + (all_,) * 8 + (nodes,),
        out_specs=(nodes, nodes, nodes) + (all_,) * 8,
        check_vma=False,
    )
```

```python
import functools

import jax
import jax.numpy as jnp
from jax import lax
from jax.experimental import pallas as pl
from jax.experimental.pallas import tpu as pltpu
from jax.sharding import PartitionSpec as P

F32 = jnp.float32
BF16 = jnp.bfloat16
H = 128
CAP = 64
GROUP = 16
SUB = 8
SIDE = CAP // 2
PIECES = 32
UNITS = H // PIECES
EXTRA = 32
CHUNKS = (
    (0, 64, 0, ((3,), (2,), (1,), (0,))),
    (64, 64, EXTRA, ((2,), (3,), (1,), (0,))),
)
VMEM_LIMIT = 60 * 1024 * 1024
UNROLL = 4
BACK_UNROLL = 2
AGG = 32
TIED = (0, 1)
GIVE = 2
LAST_GIVE = 0
COST = 0.02
KSTEP = 32
MATRIX_FIRST = True


def nn(a, b):
    return lax.dot_general(a, b, (((1,), (0,)), ((), ())), preferred_element_type=F32)


def nt(a, b):
    return lax.dot_general(a, b, (((1,), (1,)), ((), ())), preferred_element_type=F32)


def eye(n):
    rows = lax.broadcasted_iota(jnp.int32, (n, n), 0)
    cols = lax.broadcasted_iota(jnp.int32, (n, n), 1)
    return jnp.where(rows == cols, 1.0, 0.0).astype(BF16)


def one_hot_rows(rel, count):
    rel = jnp.clip(rel, -1, count).astype(F32).astype(BF16)
    rows = lax.broadcasted_iota(jnp.int32, (count, rel.shape[1]), 0).astype(F32).astype(BF16)
    return jnp.where(rows == rel, jnp.ones((), BF16), jnp.zeros((), BF16))


def slot_hots(slot, count):
    return one_hot_rows(jnp.right_shift(slot, 7), count), one_hot_rows(jnp.bitwise_and(slot, H - 1), H)


def sort_kernel(shape, me_ref, target_ref, source_ref, mask_ref, label_ref, feats_ref, states_ref, out_ref, slot_ref, data_ref):
    holders, own, groups = shape
    blocks = groups // 2
    edges = target_ref.shape[1]
    target = target_ref[...]
    owner = jnp.right_shift(target, own.bit_length() - 1)
    local = jnp.bitwise_and(target, own - 1)
    bucket = owner * (2 * groups) + jnp.right_shift(local, 3)
    bucket = jnp.where(mask_ref[...] != 0, bucket, -1)
    buckets = holders * groups * 2
    turn = jnp.bitwise_and(me_ref[0], 3)

    block = 256
    rows = lax.broadcasted_iota(jnp.int32, (block, block), 0)
    cols = lax.broadcasted_iota(jnp.int32, (block, block), 1)
    upto = jnp.where(rows <= cols, 1.0, 0.0).astype(BF16)
    numbers = lax.broadcasted_iota(jnp.int32, (buckets, block), 0)
    carry = jnp.zeros((buckets, 1), F32)
    slots = []
    for b in range(edges // block):
        here = bucket[:, b * block : (b + 1) * block]
        hot = numbers == here
        within = nn(hot.astype(F32).astype(BF16), upto) + carry
        rank = jnp.sum(jnp.where(hot, within - 1.0, 0.0), axis=0, keepdims=True).astype(jnp.int32)
        carry = within[:, block - 1 : block]
        at = jnp.where(jnp.bitwise_and(here, 1) == 0, rank, CAP - 1 - rank)
        side = jnp.bitwise_and(jnp.bitwise_and(here, 2) + jnp.right_shift(at, 5) + turn, 3)
        place = jnp.right_shift(here, 2) * H + side * SIDE + jnp.bitwise_and(at, SIDE - 1)
        slots.append(jnp.where((here >= 0) & (rank < CAP), place, -1))
    both = carry + jnp.concatenate([carry[1:, :], carry[:1, :]], axis=0)
    first_of_two = jnp.bitwise_and(lax.broadcasted_iota(jnp.int32, (buckets, 1), 0), 1) == 0
    worst = jnp.max(jnp.where(first_of_two, both, 0.0), axis=0, keepdims=True)
    flag = jnp.where(worst > CAP, 1.0, 0.0)
    slot = jnp.concatenate(slots, axis=1)
    slot_ref[...] = slot

    data_ref[16:32, :] = jnp.zeros((16, edges), F32)
    data_ref[0:16, :] = feats_ref[...].astype(F32)
    source = source_ref[...]
    data_ref[16:17, :] = jnp.right_shift(source, 6).astype(F32)
    data_ref[17:18, :] = jnp.bitwise_and(source, 63).astype(F32)
    data_ref[18:19, :] = (local + 1).astype(F32)
    data = data_ref[...].astype(BF16)

    tags = []
    for t in range(own // H):
        label = label_ref[:, t * H : (t + 1) * H]
        tags += [jnp.right_shift(label, 6).astype(F32), jnp.bitwise_and(label, 63).astype(F32)]
    tags.append(jnp.broadcast_to(flag, (1, H)))
    tags.append(jnp.zeros((16 - 3 * blocks - len(tags), H), F32))
    high, low = slot_hots(slot, holders * blocks)
    together = min(4, holders)
    for s0 in range(0, holders, together):
        part = high[s0 * blocks : (s0 + together) * blocks, :]
        spread = (part[:, None, :] * data[None, :, :]).reshape(together * blocks * 32, edges)
        moved = nt(spread, low)
        for n in range(together):
            out = out_ref.at[s0 + n]
            out[0:own, :] = states_ref[...]
            ids = []
            for q in range(blocks):
                at = (n * blocks + q) * 32
                out[own + 16 * q : own + 16 * (q + 1), :] = moved[at : at + 16, :].astype(BF16)
                ids.append(moved[at + 16 : at + 19, :])
            out[own + 16 * blocks : own + 16 * blocks + 16, :] = jnp.concatenate(ids + tags, axis=0).astype(BF16)


def swap_rows(outer, inner, flip=None):
    n = outer * inner
    rows = lax.broadcasted_iota(jnp.int32, (n, n), 0)
    cols = lax.broadcasted_iota(jnp.int32, (n, n), 1)
    number = jnp.bitwise_and(rows, inner - 1)
    if flip is not None:
        number = jnp.bitwise_xor(number, flip)
    source = number * outer + jnp.right_shift(rows, inner.bit_length() - 1)
    return jnp.where(source == cols, 1.0, 0.0).astype(BF16)


def split_kernel(w_ref, out_ref, order_ref):
    @pl.when(pl.program_id(0) == 0)
    def _():
        order_ref[...] = swap_rows(16, 16)

    order = order_ref[...]
    for ib in range(0, H, 32):
        sides = []
        for half in range(2):
            rows = [w_ref[:, (ib + 16 * half + i) * H : (ib + 16 * half + i + 1) * H] for i in range(16)]
            sides.append(jnp.concatenate(rows, axis=0))
        moved = nn(order, jnp.concatenate(sides, axis=1)).astype(BF16)
        for half in range(2):
            at = ib + 16 * half
            out_ref[:, at : at + 16, :] = moved[:, half * H : (half + 1) * H].reshape(16, 16, H)


def front_kernel(shape, chunks, *refs):
    holders, own, groups = shape
    blocks = groups // 2
    refs = list(refs)
    take = lambda n: [refs.pop(0) for _ in range(n)]
    piece_ref, given, states_ref, own_label_ref, t_in, b2_ref, w1_ref, b1_ref, wi_ref, wh_ref, bi_ref, bh_ref, cot_ref = take(13)
    new_ref, direct_ref, d_ref, crossed_ref, lat_out, near_out, meta_out = take(7)
    outs = take(sum(len(chunk.heads) for chunk in chunks) + 1)
    table_ref, p_ref, sum_ref, small_ref, dt_ref, rows_ref, bias_ref, extra_ref, t_ref, lat_ref, near_ref, meta_ref = take(12)
    built = take(len(outs))
    (sems,) = refs
    waiting = []

    def copy(source, target):
        moving = pltpu.make_async_copy(source, target, sems.at[len(waiting)])
        moving.start()
        waiting.append(moving)
        return moving

    t_copy = copy(t_in, t_ref)

    nodes = holders * own
    lanes = holders * SIDE
    ident = eye(H)
    tags_at = own + 16 * blocks

    flag = jnp.zeros((1, 1), F32)
    for s in range(holders):
        tags = given[s, tags_at : tags_at + 16, :].astype(F32)
        flag = jnp.maximum(flag, tags[3 * blocks + 2 * (own // H) : 3 * blocks + 2 * (own // H) + 1, 0:1])
        for t in range(own // H):
            at = s * own + t * H
            table_ref[0:H, at : at + H] = nt(ident, given[s, t * H : (t + 1) * H, :]).astype(BF16)
            both = tags[3 * blocks + 2 * t : 3 * blocks + 2 * t + 2, :]
            table_ref[H : H + 16, at : at + H] = jnp.concatenate([both, jnp.zeros((14, H), F32)], axis=0).astype(BF16)
    for t in range(own // H):
        label = own_label_ref[:, t * H : (t + 1) * H]
        label = jnp.concatenate([jnp.right_shift(label, 6), jnp.bitwise_and(label, 63)], axis=0).astype(F32)
        cols = nt(ident, jnp.concatenate([label, jnp.zeros((14, H), F32)], axis=0).astype(BF16))
        small_ref[t * H : (t + 1) * H, 0:1] = cols[:, 0:1] * 64.0 + cols[:, 1:2]

    side = lax.broadcasted_iota(jnp.int32, (24, H), 1) // SIDE
    crossing = jnp.zeros((1, H), F32)
    for q in range(blocks):
        for s in range(0, holders, 4):
            parts = []
            for n in range(4):
                feats = given[s + n, own + 16 * q : own + 16 * (q + 1), :].astype(F32)
                ids = given[s + n, tags_at : tags_at + 16, :].astype(F32)[3 * q : 3 * q + 3, :]
                parts.append(jnp.concatenate([feats, ids, jnp.zeros((5, H), F32)], axis=0))
            at = slice(s // 4 * H, (s // 4 + 1) * H)
            for u in range(4):
                page = parts[(3 - u) % 4]
                for c in range(3):
                    page = jnp.where(side == c, parts[(c - u) % 4], page)
                meta_ref[4 * q + u, 0:24, at] = page
                low = float((4 * q + u) * SUB)
                node = page[18:19, :] - 1.0
                outside = (node >= 0.0) & ((node < low) | (node >= low + SUB))
                crossing = jnp.maximum(crossing, jnp.where(outside, 1.0, 0.0))
    crossed = jnp.max(crossing) > 0.0
    crossed_ref[0] = crossed.astype(jnp.int32)

    w1 = nt(ident, w1_ref[...]).astype(BF16)
    b1 = nt(ident, jnp.broadcast_to(b1_ref[...].astype(F32), (16, H)).astype(BF16))[:, 0:1]

    def both_pages(ref, g, rows):
        return jnp.concatenate([ref[2 * g + n, rows, :] for n in range(2)], axis=1)

    def group_step(usual, g, unused):
        data = both_pages(meta_ref, g, slice(0, 24))
        source = (data[16:17, :] * 64.0 + data[17:18, :]).astype(jnp.int32)
        picked = jnp.zeros((H + 16, 2 * lanes), F32)
        for c in range(0, nodes, 256):
            picked = picked + nn(table_ref[:, c : c + 256], one_hot_rows(source - c, 256))
        near = picked[0:H, :].astype(BF16)
        label = picked[H : H + 1, :] * 64.0 + picked[H + 1 : H + 2, :]
        inside = data[18:19, :] - 1.0 - (g * GROUP).astype(F32)
        numbers = lax.broadcasted_iota(jnp.int32, (GROUP, 2 * lanes), 0).astype(F32)
        own_label = small_ref[pl.ds(pl.multiple_of(g * GROUP, GROUP), GROUP), 0:1]
        member = jnp.where((numbers == inside) & (own_label == label), 1.0, 0.0)
        before = nn(w1, data[0:16, :].astype(BF16)) + b1
        latent = before / (1.0 + jnp.exp(-before))
        made = []
        for n in range(2):
            page = slice(n * lanes, (n + 1) * lanes)
            meta_ref[2 * g + n, 24:25, :] = source[:, page].astype(F32)
            meta_ref[2 * g + n, 32 : 32 + GROUP, :] = member[:, page]
            lat_ref[2 * g + n] = latent[:, page].astype(BF16)
            near_ref[2 * g + n] = near[:, page]
            mine = member[n * SUB : (n + 1) * SUB, :]
            if usual:
                units, states, mine = latent[:, page], near[:, page], mine[:, page]
            else:
                units, states = latent, near
            spread = (units[:, None, :] * mine[None, :, :]).reshape(H * SUB, -1).astype(BF16)
            made.append(nt(spread, states).reshape(H, SUB, H))
        at = pl.ds(pl.multiple_of(g * GROUP, GROUP), GROUP)
        p_ref[:, at, :] = jnp.concatenate(made, axis=1).astype(BF16)
        sum_ref[at, :] = nt(member.astype(BF16), near)
        return unused

    @pl.when(jnp.logical_not(crossed))
    def _():
        lax.fori_loop(0, groups, functools.partial(group_step, True), 0, unroll=UNROLL)

    @pl.when(crossed)
    def _():
        lax.fori_loop(0, groups, functools.partial(group_step, False), 0)

    copy(lat_ref, lat_out)
    copy(near_ref, near_out)
    copy(meta_ref, meta_out)

    def agg_step(n, total):
        left = jnp.concatenate([p_ref[n * AGG + m] for m in range(AGG)], axis=1)
        right = jnp.concatenate([t_ref[n * AGG + m] for m in range(AGG)], axis=1)
        return total + nt(left, right)

    total = nt(sum_ref[...].astype(BF16), b2_ref[...])
    t_copy.wait()
    total = lax.fori_loop(0, H // AGG, agg_step, total)

    mixed = total.astype(BF16)
    prior = states_ref[...]
    prior_f = prior.astype(F32)
    cot = cot_ref[...].astype(F32)
    wi, wh = wi_ref[...], wh_ref[...]
    gi = nn(mixed, wi) + bi_ref[...]
    gh = nn(prior, wh) + bh_ref[...]
    r = jax.nn.sigmoid(gi[:, 0:H] + gh[:, 0:H])
    u = jax.nn.sigmoid(gi[:, H : 2 * H] + gh[:, H : 2 * H])
    n = jnp.tanh(gi[:, 2 * H :] + r * gh[:, 2 * H :])
    new_ref[...] = ((1.0 - u) * n + u * prior_f).astype(BF16)
    d_pre = (1.0 - u) * cot * (1.0 - n * n)
    d_r = d_pre * gh[:, 2 * H :] * r * (1.0 - r)
    d_u = (prior_f - n) * cot * u * (1.0 - u)
    d_gi = jnp.concatenate([d_r, d_u, d_pre], axis=1)
    d_gh = jnp.concatenate([d_r, d_u, d_pre * r], axis=1)

    def halves(x):
        high = x.astype(BF16)
        return high, (x - high.astype(F32)).astype(BF16)

    def twice(x):
        return jnp.concatenate([x, x], axis=1)

    gi_high, gi_low = halves(d_gi)
    gh_high, gh_low = halves(d_gh)
    d_agg = nt(jnp.concatenate([gi_high, gi_low], axis=1), twice(wi)).astype(BF16)
    d_ref[...] = d_agg
    dt_ref[...] = nt(ident, d_agg).astype(BF16)
    direct_ref[...] = u * cot + nt(jnp.concatenate([gh_high, gh_low], axis=1), twice(wh))

    piece_me = piece_ref[0]
    joint = built[-1]

    def dest(c, rel):
        place = chunks[c].place(rel)
        if rel >= PIECES // 2:
            return joint, place, chunks[c].offset
        before = sum(len(chunk.heads) for chunk in chunks[:c])
        for n, head in enumerate(chunks[c].heads):
            count = PIECES // 2 >> len(head)
            if place < count:
                return built[before + n], place, 0
            place -= count

    mixed_t = nt(ident, mixed).astype(BF16)
    prior_t = nt(ident, prior).astype(BF16)
    from_input = nn(twice(mixed_t), jnp.concatenate([gi_high, gi_low], axis=0))
    from_state = nn(twice(prior_t), jnp.concatenate([gh_high, gh_low], axis=0))
    for t in range(3):
        rows_ref[t] = from_input[:, t * H : (t + 1) * H]
        rows_ref[3 + t] = from_state[:, t * H : (t + 1) * H]
    rows_ref[6] = nn(dt_ref[...], sum_ref[...].astype(BF16))
    bias_ref[...] = jnp.zeros_like(bias_ref)
    for n, part in enumerate((d_gi, d_gh)):
        part = jnp.sum(part, axis=0, keepdims=True)
        for t in range(3):
            bias_ref[3 * n + t : 3 * n + t + 1, :] = part[:, t * H : (t + 1) * H]
    extra_ref[...] = jnp.zeros_like(extra_ref)
    extra_ref[29:30, :] = jnp.broadcast_to(flag, (1, H))
    last = chunks[-1]
    for rel in list(range(PIECES // 2, PIECES)) + list(range(PIECES // 2)):
        p = jnp.bitwise_xor(piece_me, rel)
        for t in range(7):
            extra_ref[UNITS * t : UNITS * (t + 1), :] = rows_ref[t, pl.ds(p * UNITS, UNITS), :]
        extra_ref[28:29, :] = bias_ref[pl.ds(p, 1), :]
        ref, place, offset = dest(len(chunks) - 1, rel)
        ref[place, offset + UNITS * last.rows : offset + last.height, :] = extra_ref[...].astype(BF16)

    for rel in list(range(PIECES // 2, PIECES)) + list(range(PIECES // 2)):
        k0 = jnp.bitwise_xor(piece_me, rel) * UNITS
        for m in range(0, UNITS, 2):
            out = nn(dt_ref[...], jnp.concatenate([p_ref[k0 + m], p_ref[k0 + m + 1]], axis=1)).astype(BF16)
            for c, chunk in enumerate(chunks):
                ref, place, offset = dest(c, rel)
                for h in range(2):
                    start = offset + (m + h) * chunk.rows
                    ref[place, start : start + chunk.rows, :] = out[
                        chunk.first : chunk.first + chunk.rows, h * H : (h + 1) * H
                    ]
        if rel == PIECES - 1:
            copy(joint, outs[-1])
    for n in range(len(built) - 1):
        copy(built[n], outs[n])
    for moving in waiting[1:]:
        moving.wait()


def spread_kernel(shape, d_ref, t_ref, b2_ref, wide_ref, bias_ref, dp_ref, order_ref):
    holders, own, groups = shape
    d = d_ref[...]

    @pl.when(pl.program_id(0) == 0)
    def _():
        bias_ref[...] = nn(d, b2_ref[...])
        order_ref[...] = swap_rows(16, 16)

    order = order_ref[...]
    for n in range(0, t_ref.shape[0], 2):
        out = nn(d, jnp.concatenate([t_ref[n], t_ref[n + 1]], axis=1)).astype(BF16)
        dp_ref[n] = out[:, :H]
        dp_ref[n + 1] = out[:, H:]
    for k in range(0, t_ref.shape[0], 16):
        for g in range(0, groups, 2):
            sides = [dp_ref[k : k + 16, (g + n) * GROUP : (g + n + 1) * GROUP, :].reshape(256, H) for n in range(2)]
            moved = nn(order, jnp.concatenate(sides, axis=1)).astype(BF16)
            for n in range(2):
                for v in range(GROUP):
                    wide_ref[g + n, k : k + 16, v * H : (v + 1) * H] = moved[v * 16 : (v + 1) * 16, n * H : (n + 1) * H]


def back_kernel(shape, masks, me_ref, *refs):
    holders, own, groups = shape
    blocks = groups // 2
    crossed_ref, wide_in, bias_ref, w1_ref, b1_ref, lat_in, near_in, meta_in = refs[:8]
    keep_d, keep_e, send_ref, first_ref = refs[8:12]
    part_ref, edge_ref, sum_ref, slab_ref, wide_ref, lat_ref, near_ref, meta_ref, sems = refs[12:]

    def coming(g):
        pages = pl.ds(2 * g, 2)
        return [
            pltpu.make_async_copy(wide_in.at[g], wide_ref.at[g], sems.at[0, g]),
            pltpu.make_async_copy(lat_in.at[pages], lat_ref.at[pages], sems.at[1, g]),
            pltpu.make_async_copy(near_in.at[pages], near_ref.at[pages], sems.at[2, g]),
            pltpu.make_async_copy(meta_in.at[pages], meta_ref.at[pages], sems.at[3, g]),
        ]

    for g in range(groups):
        for copy in coming(g):
            copy.start()
    nodes = holders * own
    lanes = holders * SIDE
    ident = eye(H)
    part_ref[...] = jnp.zeros_like(part_ref)
    w1n = w1_ref[...]
    w1 = nt(ident, w1n).astype(BF16)
    b1 = nt(ident, jnp.broadcast_to(b1_ref[...].astype(F32), (16, H)).astype(BF16))[:, 0:1]
    one_row = jnp.where(lax.broadcasted_iota(jnp.int32, (16, 2 * lanes), 0) == 0, 1.0, 0.0).astype(BF16)

    def both_pages(ref, g, rows):
        return jnp.concatenate([ref[2 * g + n, rows, :] for n in range(2)], axis=1)

    def group_step(usual, g, first_total):
        for copy in coming(g):
            copy.wait()
        wide = wide_ref[g]
        wide_t = jnp.concatenate([wide[:, v * H : (v + 1) * H].T for v in range(GROUP)], axis=1)
        bias_rows = bias_ref[pl.ds(pl.multiple_of(g * GROUP, GROUP), GROUP), :].astype(BF16)
        bias_t = nt(ident, bias_rows).astype(BF16)
        data = both_pages(meta_ref, g, slice(0, 16)).astype(BF16)
        source = both_pages(meta_ref, g, slice(24, 25)).astype(jnp.int32)
        member = both_pages(meta_ref, g, slice(32, 32 + GROUP)).astype(BF16)
        d_latent, d_near = [], []
        for n in range(2):
            low, number = (n * SUB, SUB) if usual else (0, GROUP)
            mine = meta_ref[2 * g + n, 32 + low : 32 + low + number, :].astype(BF16)
            part = slice(low * H, (low + number) * H)
            spread = (near_ref[2 * g + n][None, :, :] * mine[:, None, :]).reshape(number * H, lanes)
            d_latent.append(nn(wide[:, part], spread))
            spread = (lat_ref[2 * g + n][None, :, :] * mine[:, None, :]).reshape(number * H, lanes)
            d_near.append(nn(wide_t[:, part], spread))
        d_latent = jnp.concatenate(d_latent, axis=1)
        d_near = (jnp.concatenate(d_near, axis=1) + nn(bias_t, member)).astype(BF16)
        for c in range(0, nodes, 256):
            part_ref[c : c + 256, :] += nt(one_hot_rows(source - c, 256), d_near)
        before = nn(w1, data) + b1
        gate = 1.0 / (1.0 + jnp.exp(-before))
        d_before = (d_latent * gate * (1.0 + before * (1.0 - gate))).astype(BF16)
        edges = nn(w1n, d_before)
        for n in range(2):
            edge_ref[2 * g + n] = edges[:, n * lanes : (n + 1) * lanes]
        return first_total + nt(jnp.concatenate([data, one_row], axis=0), d_before)

    none = jnp.zeros((32, H), F32)

    @pl.when(crossed_ref[0] == 0)
    def _():
        sum_ref[...] = lax.fori_loop(0, groups, functools.partial(group_step, True), none, unroll=BACK_UNROLL)

    @pl.when(crossed_ref[0] != 0)
    def _():
        sum_ref[...] = lax.fori_loop(0, groups, functools.partial(group_step, False), none)

    first = sum_ref[...].astype(BF16)
    first_ref[...] = first
    half = holders // 2
    side = lax.broadcasted_iota(jnp.int32, (16, H), 1) // SIDE
    for q in range(blocks):
        for s in range(holders):
            at = slice(s // 4 * H, (s // 4 + 1) * H)
            parts = [edge_ref[4 * q + u, :, at] for u in range(4)]
            page = parts[(3 - s) % 4]
            for c in range(3):
                page = jnp.where(side == c, parts[(c - s) % 4], page)
            slab_ref[s, 16 * q : 16 * (q + 1), :] = page.astype(BF16)
    for n in range(holders):
        rel = sum(mask for i, mask in enumerate(reversed(masks)) if n >> i & 1)
        h = jnp.bitwise_xor(me_ref[0], rel)
        rows = part_ref[pl.ds(pl.multiple_of(h * own, own), own), :].astype(BF16)
        if n < half:
            keep_d[n] = rows
            keep_e[n] = slab_ref[h]
        else:
            send_ref[(n - half) * own : (n - half + 1) * own, :] = rows
            at = half * own + (n - half) * 16 * blocks
            send_ref[at : at + 16 * blocks, :] = slab_ref[h]


def gather_kernel(shape, sources, me_ref, slot_ref, direct_ref, part_ref, slabs_ref, state_ref, edge_ref, data_ref):
    holders, own, groups = shape
    blocks = groups // 2
    state_ref[...] = direct_ref[...] + part_ref[...].astype(F32)
    for n, rel in enumerate(sources):
        h = jnp.bitwise_xor(me_ref[0], rel)
        data_ref[pl.ds(pl.multiple_of(h * 16 * blocks, 16), 16 * blocks), :] = slabs_ref[n]
    edges = slot_ref.shape[1]
    data = data_ref[...]
    count = holders * blocks
    block = 512
    for b in range(edges // block):
        high, low = slot_hots(slot_ref[:, b * block : (b + 1) * block], count)
        high = high.astype(F32)
        found = nn(data, low)
        total = jnp.zeros((16, block), F32)
        for n in range(count):
            total = total + found[16 * n : 16 * (n + 1), :] * high[n : n + 1, :]
        edge_ref[:, b * block : (b + 1) * block] = total


class Chunk:
    def __init__(self, first, rows, extra, steps, offset):
        self.first, self.rows, self.extra, self.steps, self.offset = first, rows, extra, steps, offset
        self.height = UNITS * rows + extra
        self.order = sum(steps, ())
        ways = [(n,) for n in range(2)] if len(steps[0]) == 1 else [(n, m) for n in range(2) for m in range(2)]
        self.heads = [(0, 0), (0, 1), (1,)] if len(steps[0]) == 1 else ways

    def place(self, rel):
        at = 0
        for bit in self.order:
            at = at * 2 + (rel >> bit & 1)
        return at

    def shape(self):
        return (2,) * len(self.order) + (self.height, H)

    def partners(self, step, bits):
        group = self.steps[step]
        found = []
        for n in range(1, 2 ** len(group)):
            path = tuple(n >> (len(group) - 1 - i) & 1 for i in range(len(group)))
            found.append((path, sum(bits[bit] for bit, on in zip(group, path) if on)))
        return found


def plan(batch, edge):
    core, x = [edge], [edge << n for n in range(1, batch.bit_length() - 1)]
    z = [2 << n for n in reversed(range(3 - len(x)))]
    bits = z + [1] + x + core
    chunks, offset = [], 0
    for first, rows, extra, steps in CHUNKS:
        chunks.append(Chunk(first, rows, extra, steps, offset))
        offset += chunks[-1].height
    device = lax.axis_index(("batch", "edge")).astype(jnp.int32)
    piece = sum(jnp.where(device & mask != 0, 1 << n, 0) for n, mask in enumerate(bits))
    return bits, chunks, piece.astype(jnp.int32).reshape(1)


def swap(x, mask, devices):
    return lax.ppermute(x, ("batch", "edge"), [(i, i ^ mask) for i in range(devices)])


def add(terms):
    total = terms[0].astype(F32)
    for term in terms[1:]:
        total = total + term.astype(F32)
    return total.astype(BF16)


def rounded(x):
    return lax.reduce_precision(x.astype(F32), 8, 7).astype(BF16)


def jobs_of(chunks, arrived, cores):
    found = []
    for core in cores:
        for c, chunk in enumerate(chunks):
            last, beside = chunk.order[:2]
            for n in range(2):
                found.append((c, core, core * PIECES // 2 + (arrived << last) + (n << beside), 4 * n))
    return found


def unpack(chunks, jobs, me, order_ref, sources, block_refs, w_out, rows_ref, sems, beside=lambda: None):
    width = 4 * UNITS
    coming, leaving = [], []
    for n, (c, core, rel, place) in enumerate(jobs):
        coming.append(pltpu.make_async_copy(sources[n].at[pl.ds(place, 4)], block_refs[n], sems.at[n]))
        rows = pl.ds(pl.multiple_of(jnp.bitwise_xor(jnp.right_shift(me, 2), rel // 4) * width, width), width)
        lanes = pl.ds(chunks[c].first * H, chunks[c].rows * H)
        leaving.append(pltpu.make_async_copy(rows_ref.at[n % 3], w_out.at[rows, lanes], sems.at[len(jobs) + n]))
    for copy in coming:
        copy.start()
    order_ref[...] = swap_rows(32, 2 * UNITS, jnp.bitwise_and(me, 1) * UNITS)
    beside()
    for n, (c, core, rel, place) in enumerate(jobs):
        coming[n].wait()
        if n >= 3:
            leaving[n - 3].wait()
        rows = chunks[c].rows
        for pair in range(2):
            upper = jnp.bitwise_xor(jnp.bitwise_and(jnp.right_shift(me, 1), 1), pair)
            at_rows = pl.ds(pl.multiple_of(upper * 2 * UNITS, 2 * UNITS), 2 * UNITS)
            for ib in range(0, rows, 64):
                sides = []
                for at in (ib, ib + 32):
                    parts = [
                        block_refs[n][2 * pair + i, m * rows + at : m * rows + at + 32, :]
                        for i in range(2)
                        for m in range(UNITS)
                    ]
                    sides.append(jnp.concatenate(parts, axis=0))
                moved = nn(order_ref[...], jnp.concatenate(sides, axis=1))
                for side in range(2):
                    for i in range(32):
                        at = (ib + 32 * side + i) * H
                        rows_ref[n % 3, at_rows, at : at + H] = moved[8 * i : 8 * (i + 1), side * H : (side + 1) * H]
        leaving[n].start()

    def end():
        for copy in leaving[-3:]:
            copy.wait()

    return end


def small_piece(me, rel, extra, extra_ref, bias_ref):
    p = jnp.bitwise_xor(me, rel)
    extra = extra.astype(F32)
    for t in range(7):
        extra_ref[t, pl.ds(p * UNITS, UNITS), :] = extra[UNITS * t : UNITS * (t + 1), :]
    bias_ref[pl.ds(p, 1), :] = extra[28:29, :]


def small_pieces(chunks, jobs, me, block_refs, extra_ref, bias_ref):
    start = UNITS * chunks[-1].rows
    for n, (c, core, rel, place) in enumerate(jobs):
        if c == len(chunks) - 1:
            for i in range(4):
                small_piece(me, rel + i, block_refs[n][i, start : start + EXTRA, :], extra_ref, bias_ref)


def early_kernel(chunks, piece_ref, *refs):
    count = len(chunks)
    jobs = jobs_of(chunks, 0, (0, 1))
    sources = [refs[core * count + c] for c, core, rel, place in jobs]
    w_out, extra_ref, bias_ref = refs[2 * count : 2 * count + 3]
    block_refs, (rows_ref, order_ref, sems) = refs[2 * count + 3 : -3], refs[-3:]
    me = piece_ref[0]
    extra_ref[...] = jnp.zeros_like(extra_ref)
    bias_ref[...] = jnp.zeros_like(bias_ref)
    end = unpack(chunks, jobs, me, order_ref, sources, block_refs, w_out, rows_ref, sems)
    small_pieces(chunks, jobs, me, block_refs, extra_ref, bias_ref)
    end()


def late_kernel(chunks, piece_ref, *refs):
    count = len(chunks)
    jobs = jobs_of(chunks, 1, (0,))
    sources = [refs[c] for c, core, rel, place in jobs]
    w_in, w_out = refs[count : count + 2]
    block_refs, (rows_ref, order_ref, sems) = refs[count + 2 : -3], refs[-3:]
    unpack(chunks, jobs, piece_ref[0], order_ref, sources, block_refs, w_out, rows_ref, sems)()


def last_kernel(chunks, piece_ref, *refs):
    count = len(chunks)
    jobs = jobs_of(chunks, 1, (1,))
    sources = [refs[c] for c, core, rel, place in jobs]
    own_last, first_ref, extra_in, bias_in, w_in = refs[count : count + 5]
    w_out, w1_ref, b1_ref, wi_ref, wh_ref, b2_ref, bi_ref, bh_ref = refs[count + 5 : count + 13]
    block_refs, (rows_ref, order_ref, small_ref, extra_ref, bias_ref, sems) = refs[count + 13 : -6], refs[-6:]
    me = piece_ref[0]
    start = UNITS * chunks[-1].rows
    small = pltpu.make_async_copy(own_last.at[:, start : start + EXTRA, :], small_ref, sems.at[2 * len(jobs)])

    def beside():
        small.start()
        w1_ref[...] = first_ref[0:16, :].astype(F32)
        b1_ref[...] = first_ref[16:17, :].astype(F32).reshape(H)
        extra_ref[...] = extra_in[...]
        bias_ref[...] = bias_in[...]
        small.wait()
        for c, core, rel, place in jobs_of(chunks, 1, (0,)):
            if c == count - 1:
                for i in range(4):
                    small_piece(me, rel + i, small_ref[place + i], extra_ref, bias_ref)

    end = unpack(chunks, jobs, me, order_ref, sources, block_refs, w_out, rows_ref, sems, beside)
    small_pieces(chunks, jobs, me, block_refs, extra_ref, bias_ref)
    for t in range(3):
        wi_ref[:, t * H : (t + 1) * H] = extra_ref[t]
        wh_ref[:, t * H : (t + 1) * H] = extra_ref[3 + t]
        bi_ref[t * H : (t + 1) * H] = bias_ref[t : t + 1, :].reshape(H)
        bh_ref[t * H : (t + 1) * H] = bias_ref[3 + t : 4 + t, :].reshape(H)
    b2_ref[...] = extra_ref[6]
    end()


def unpack_scratch(chunks, jobs, more=()):
    return (
        [pltpu.VMEM((4, chunks[c].height, H), BF16) for c, core, rel, place in jobs]
        + [pltpu.VMEM((3, 4 * UNITS, max(chunk.rows for chunk in chunks) * H), F32), pltpu.VMEM((256, 256), BF16)]
        + list(more)
        + [pltpu.SemaphoreType.DMA((2 * len(jobs) + 1,))]
    )


W_SHAPE = jax.ShapeDtypeStruct((H, H * H), F32)
SMALL = [jax.ShapeDtypeStruct((7, H, H), F32), jax.ShapeDtypeStruct((PIECES, H), F32)]


def early_half(chunks, bits, devices, piece_arr, parts):
    parts = [x.reshape(PIECES // 4, chunk.height, H) for x, chunk in zip(parts, chunks)]
    others = [swap(x, bits[-1], devices) for x in parts]
    return pl.pallas_call(
        functools.partial(early_kernel, chunks),
        name="assemble_early",
        in_specs=[smem()] + [anywhere()] * (2 * len(chunks)),
        out_specs=[anywhere(), vmem(), vmem()],
        scratch_shapes=unpack_scratch(chunks, jobs_of(chunks, 0, (0, 1))),
        out_shape=[W_SHAPE] + SMALL,
        compiler_params=params(),
        cost_estimate=cost(6),
    )(piece_arr, *parts, *others)


def vmem():
    return pl.BlockSpec(memory_space=pltpu.VMEM)


def anywhere():
    return pl.BlockSpec(memory_space=pl.ANY)


def smem():
    return pl.BlockSpec(memory_space=pltpu.SMEM)


def cost(us):
    return pl.CostEstimate(flops=int(us * COST * 1e9), bytes_accessed=int(us * COST * 3e6), transcendentals=0)


def params():
    return pltpu.CompilerParams(vmem_limit_bytes=VMEM_LIMIT)


def fast_path(batch, edge, args):
    (states, edge_feats, molecule, source, target, edge_mask, w_edge_in, b_edge_in, w_edge_out, b_edge_out,
     w_input, w_hidden, b_input, b_hidden, cotangent) = args
    devices = batch * edge
    states_here = states[0]
    own = states_here.shape[0]
    edges = source.shape[1]
    holders, groups = edge, own // GROUP
    shape = (holders, own, groups)
    blocks = groups // 2
    bits, chunks, piece_arr = plan(batch, edge)
    rest = [m for m in (1 << n for n in range(devices.bit_length() - 1)) if m not in bits]
    me_arr = lax.axis_index("edge").astype(jnp.int32).reshape(1)
    lanes = holders * SIDE
    pages = 2 * groups

    slots_out, slot = pl.pallas_call(
        functools.partial(sort_kernel, shape),
        name="edges_to_slots",
        out_shape=[
            jax.ShapeDtypeStruct((holders, own + 16 * blocks + 16, H), BF16),
            jax.ShapeDtypeStruct((1, edges), jnp.int32),
        ],
        in_specs=[smem()] + [vmem()] * 6,
        out_specs=[vmem()] * 2,
        scratch_shapes=[pltpu.VMEM((32, edges), F32)],
        compiler_params=params(),
    )(me_arr, target, source, edge_mask, molecule, jnp.swapaxes(edge_feats, 1, 2)[0], states_here)
    given = lax.all_to_all(slots_out, "edge", 0, 0)

    t_units = pl.pallas_call(
        split_kernel,
        name="split_weight",
        grid=(H // 16,),
        in_specs=[pl.BlockSpec((16, H * H), lambda i: (i, 0))],
        out_specs=pl.BlockSpec((16, H, H), lambda i: (i, 0, 0)),
        out_shape=jax.ShapeDtypeStruct((H, H, H), BF16),
        scratch_shapes=[pltpu.VMEM((256, 256), BF16)],
        compiler_params=params(),
        cost_estimate=cost(6),
    )(w_edge_out)
    b2 = b_edge_out.reshape(H, H)
    b1 = b_edge_in.reshape(1, H)
    built = [jax.ShapeDtypeStruct((PIECES // 2 >> len(h), c.height, H), BF16) for c in chunks for h in c.heads]
    built.append(jax.ShapeDtypeStruct((PIECES // 2, sum(c.height for c in chunks), H), BF16))
    front = pl.pallas_call(
        functools.partial(front_kernel, shape, chunks),
        name="messages_update_weight_gradient",
        out_shape=[
            jax.ShapeDtypeStruct((own, H), BF16),
            jax.ShapeDtypeStruct((own, H), F32),
            jax.ShapeDtypeStruct((own, H), BF16),
            jax.ShapeDtypeStruct((1,), jnp.int32),
            jax.ShapeDtypeStruct((pages, H, lanes), BF16),
            jax.ShapeDtypeStruct((pages, H, lanes), BF16),
            jax.ShapeDtypeStruct((pages, 32 + GROUP, lanes), F32),
        ]
        + built,
        in_specs=[smem()] + [vmem()] * 3 + [anywhere()] + [vmem()] * 8,
        out_specs=[vmem()] * 3 + [smem()] + [anywhere()] * (3 + len(built)),
        scratch_shapes=[
            pltpu.VMEM((H + 16, holders * own), BF16),
            pltpu.VMEM((H, own, H), BF16),
            pltpu.VMEM((own, H), F32),
            pltpu.VMEM((own, H), F32),
            pltpu.VMEM((H, own), BF16),
            pltpu.VMEM((7, H, H), F32),
            pltpu.VMEM((PIECES, H), F32),
            pltpu.VMEM((EXTRA, H), F32),
            pltpu.VMEM((H, H, H), BF16),
            pltpu.VMEM((pages, H, lanes), BF16),
            pltpu.VMEM((pages, H, lanes), BF16),
            pltpu.VMEM((pages, 32 + GROUP, lanes), F32),
        ]
        + [pltpu.VMEM(h.shape, BF16) for h in built]
        + [pltpu.SemaphoreType.DMA((4 + len(built),))],
        compiler_params=params(),
    )(
        piece_arr, given, states_here, molecule, t_units, b2, w_edge_in, b1, w_input, w_hidden,
        b_input.astype(F32).reshape(1, -1), b_hidden.astype(F32).reshape(1, -1), cotangent[0],
    )
    new_states, direct, d_agg, crossed, latent, near, meta = front[:7]
    built = front[7:]

    matrix_gradients = pl.pallas_call(
        functools.partial(spread_kernel, shape),
        name="matrix_gradients",
        out_shape=[jax.ShapeDtypeStruct((groups, H, GROUP * H), BF16), jax.ShapeDtypeStruct((own, H), F32)],
        grid=(H // KSTEP,),
        in_specs=[
            pl.BlockSpec((own, H), lambda i: (0, 0)),
            pl.BlockSpec((KSTEP, H, H), lambda i: (i, 0, 0)),
            pl.BlockSpec((H, H), lambda i: (0, 0)),
        ],
        out_specs=[
            pl.BlockSpec((groups, KSTEP, GROUP * H), lambda i: (0, i, 0)),
            pl.BlockSpec((own, H), lambda i: (0, 0)),
        ],
        scratch_shapes=[pltpu.VMEM((KSTEP, own, H), BF16), pltpu.VMEM((256, 256), BF16)],
        compiler_params=params(),
        cost_estimate=cost(6),
    )

    back_masks = [1 << n for n in range(edge.bit_length() - 1)]

    def edge_work(wide, bias):
        return pl.pallas_call(
            functools.partial(back_kernel, shape, back_masks),
            name="edge_gradients",
            out_shape=[
                jax.ShapeDtypeStruct((holders // 2, own, H), BF16),
                jax.ShapeDtypeStruct((holders // 2, 16 * blocks, H), BF16),
                jax.ShapeDtypeStruct((holders // 2 * (own + 16 * blocks), H), BF16),
                jax.ShapeDtypeStruct((32, H), BF16),
            ],
            in_specs=[smem()] * 2 + [anywhere()] + [vmem()] * 3 + [anywhere()] * 3,
            out_specs=[vmem()] * 4,
            scratch_shapes=[
                pltpu.VMEM((holders * own, H), F32),
                pltpu.VMEM((pages, 16, lanes), F32),
                pltpu.VMEM((32, H), F32),
                pltpu.VMEM((holders, 16 * blocks, H), BF16),
                pltpu.VMEM((groups, H, GROUP * H), BF16),
                pltpu.VMEM((pages, H, lanes), BF16),
                pltpu.VMEM((pages, H, lanes), BF16),
                pltpu.VMEM((pages, 32 + GROUP, lanes), F32),
                pltpu.SemaphoreType.DMA((4, groups)),
            ],
            compiler_params=params(),
            cost_estimate=cost(14),
        )(me_arr, crossed, wide, bias, w_edge_in, b1, latent, near, meta)

    if MATRIX_FIRST:
        sent, d_agg = lax.optimization_barrier((built[-1], d_agg))
        other = swap(sent, bits[-1], devices)
        other, (wide, bias) = lax.optimization_barrier((other, matrix_gradients(d_agg, t_units, b2)))
    else:
        other = swap(built[-1], bits[-1], devices)
        wide, bias = matrix_gradients(d_agg, t_units, b2)
    other = other.reshape((2,) * 4 + (-1, H))
    arrays = iter(built)
    kept = [{head: next(arrays) for head in chunk.heads} for chunk in chunks]
    got = [[] for _ in chunks]

    def mine(c, path):
        for head, x in kept[c].items():
            if path[: len(head)] == head:
                return x.reshape((2,) * (4 - len(head)) + x.shape[1:])[path[len(head) :]]

    def partial_sum(c, path):
        rows = slice(chunks[c].offset, chunks[c].offset + chunks[c].height)
        parts = [mine(c, path), other[path][..., rows, :]]
        for n, arrays in enumerate(got[c]):
            done = sum(len(group) for group in chunks[c].steps[: n + 1])
            parts += [x[path[done:]] for x in arrays]
        return add(parts)

    def scatter_step(step, work=None, given=()):
        begun = []
        for c, chunk in enumerate(chunks):
            done = (0,) * sum(len(group) for group in chunk.steps[:step])
            if step < len(chunk.steps):
                begun.append([partial_sum(c, done + path) for path, mask in chunk.partners(step, bits)])
            else:
                begun.append([])
        if work is not None:
            begun, given = lax.optimization_barrier((begun, given))
        new = [
            [swap(x, mask, devices) for x, (path, mask) in zip(begun[c], chunk.partners(step, bits))] if begun[c] else []
            for c, chunk in enumerate(chunks)
        ]
        result = None
        if work is not None:
            result = work(*given)
            for c in TIED:
                new[c], result = lax.optimization_barrier((new[c], result))
        for c in range(len(chunks)):
            if new[c]:
                got[c].append(new[c])
        return result

    keep_d, keep_e, send, first = scatter_step(0, edge_work, (wide, bias))
    for n in range(edge.bit_length() - 1, devices.bit_length() - 1):
        first = rounded(first.astype(F32) + swap(first, 1 << n, devices).astype(F32))
    scatter_step(1)
    slabs, sources = keep_e[:, None], [0]

    def give_back(mask, after):
        nonlocal keep_d, slabs, sources, send, first
        if after is not None:
            send, after = lax.optimization_barrier((send, after))
        n = keep_d.shape[0]
        cut = n * own
        arrived = swap(jnp.concatenate([send, first], axis=0), mask, devices)
        keep_d = add([keep_d, arrived[:cut].reshape(n, own, H)])
        slabs = jnp.concatenate([slabs, arrived[cut:-32].reshape(n, -1, 16 * blocks, H)], axis=1)
        first = rounded(first.astype(F32) + arrived[-32:].astype(F32))
        sources = sources + [s ^ mask for s in sources]
        if n > 1:
            send = jnp.concatenate([keep_d[n // 2 :].reshape(-1, H), slabs[n // 2 :].reshape(-1, H)], axis=0)
            keep_d, slabs = keep_d[: n // 2], slabs[: n // 2]

    give_back(1, got[1][1])
    scatter_step(2)
    scatter_step(3)
    parts = [partial_sum(c, (0,) * 4) for c in range(len(chunks))]
    for mask in rest:
        parts = [rounded(x.astype(F32) + swap(x, mask, devices).astype(F32)) for x in parts]
    overflow = parts[-1][UNITS * chunks[-1].rows + 29, 0] > 0.0
    for step in (3, 2, 1):
        if step == GIVE:
            for mask in back_masks[1:-1]:
                give_back(mask, parts[0] if mask == 2 else None)
        for c, chunk in enumerate(chunks):
            parts[c] = gather_step(chunk, step, bits, devices, parts[c])
    give_back(back_masks[-1], parts[LAST_GIVE])
    came = [swap(x, bits[chunk.order[0]], devices) for x, chunk in zip(parts, chunks)]
    early = early_half(chunks, bits, devices, piece_arr, parts)
    state_grads, edge_grads = pl.pallas_call(
        functools.partial(gather_kernel, shape, sources),
        name="slots_to_edges",
        out_shape=[
            jax.ShapeDtypeStruct((own, H), F32),
            jax.ShapeDtypeStruct((edge_feats.shape[2], edges), F32),
        ],
        in_specs=[smem()] + [vmem()] * 4,
        out_specs=[vmem()] * 2,
        scratch_shapes=[pltpu.VMEM((holders * 16 * blocks, H), BF16)],
        compiler_params=params(),
        cost_estimate=cost(3),
    )(me_arr, slot, direct, keep_d[0], slabs[0])
    return overflow, (new_states, state_grads, edge_grads, first, came, early)


def gather_step(chunk, step, bits, devices, x):
    partners = chunk.partners(step, bits)
    all_ = jnp.stack([x] + [swap(x, mask, devices) for path, mask in partners], axis=0)
    return all_.reshape((2,) * len(chunk.steps[step]) + x.shape)


def finish(batch, edge, results):
    new_states, state_grads, edge_grads, first, came, early = results
    bits, chunks, piece_arr = plan(batch, edge)
    devices = batch * edge
    came = [x.reshape(PIECES // 4, chunk.height, H) for x, chunk in zip(came, chunks)]
    others = [swap(x, bits[-1], devices) for x in came]
    grad_w2, extras, biases = early
    grad_w2 = pl.pallas_call(
        functools.partial(late_kernel, chunks),
        name="assemble_late",
        in_specs=[smem()] + [anywhere()] * (len(chunks) + 1),
        out_specs=anywhere(),
        scratch_shapes=unpack_scratch(chunks, jobs_of(chunks, 1, (0,))),
        out_shape=W_SHAPE,
        input_output_aliases={len(chunks) + 1: 0},
        compiler_params=params(),
        cost_estimate=cost(4),
    )(piece_arr, *came, grad_w2)
    more = [pltpu.VMEM((PIECES // 4, EXTRA, H), BF16)] + [pltpu.VMEM(x.shape, F32) for x in SMALL]
    grad_w2, grad_w1, grad_b1, grad_wi, grad_wh, grad_b2, grad_bi, grad_bh = pl.pallas_call(
        functools.partial(last_kernel, chunks),
        name="assemble_last",
        in_specs=[smem()] + [anywhere()] * (len(chunks) + 1) + [vmem()] * 3 + [anywhere()],
        out_specs=[anywhere()] + [vmem()] * 7,
        scratch_shapes=unpack_scratch(chunks, jobs_of(chunks, 1, (1,)), more),
        out_shape=[W_SHAPE, jax.ShapeDtypeStruct((16, H), F32), jax.ShapeDtypeStruct((H,), F32)]
        + [jax.ShapeDtypeStruct((H, 3 * H), F32)] * 2
        + [jax.ShapeDtypeStruct((H, H), F32)]
        + [jax.ShapeDtypeStruct((3 * H,), F32)] * 2,
        input_output_aliases={len(chunks) + 5: 0},
        compiler_params=params(),
    )(piece_arr, *others, came[-1], first, extras, biases, grad_w2)
    return (
        new_states[None],
        state_grads[None],
        jnp.swapaxes(edge_grads[None], 1, 2),
        grad_w1,
        grad_b1,
        grad_w2,
        grad_b2.reshape(-1),
        grad_wi,
        grad_wh,
        grad_bi,
        grad_bh,
    )


HIGH = lax.Precision.HIGHEST


def gated_update(mixed, prior, w_input, w_hidden, b_input, b_hidden):
    width = prior.shape[1]
    from_input = jnp.dot(mixed, w_input, precision=HIGH) + b_input
    from_state = jnp.dot(prior, w_hidden, precision=HIGH) + b_hidden
    reset = jax.nn.sigmoid(from_input[:, :width] + from_state[:, :width])
    update = jax.nn.sigmoid(from_input[:, width : 2 * width] + from_state[:, width : 2 * width])
    candidate = jnp.tanh(from_input[:, 2 * width :] + reset * from_state[:, 2 * width :])
    return (1.0 - update) * candidate + update * prior


def edge_hidden(feats, w_edge_in, b_edge_in):
    return jax.nn.silu(jnp.dot(feats, w_edge_in, precision=HIGH) + b_edge_in)


def pick_by(index_rows, piece):
    columns = lax.broadcasted_iota(jnp.int32, (1, piece.shape[0]), 1)
    onehot = (index_rows[:, None] == columns).astype(jnp.bfloat16)
    return jnp.dot(onehot, piece, preferred_element_type=jnp.float32)


def spread_by(index_rows, values, count):
    rows = lax.broadcasted_iota(jnp.int32, (count, 1), 0)
    onehot = (rows == index_rows[None, :]).astype(jnp.bfloat16)
    return jnp.dot(onehot, values, preferred_element_type=jnp.float32)


def from_all(x, edge):
    got = lax.all_to_all(jnp.broadcast_to(x[None], (edge,) + x.shape), "edge", 0, 0)
    return got.reshape((-1,) + x.shape[1:])


def to_owners(x, edge):
    got = lax.all_to_all(x.reshape((edge, -1) + x.shape[1:]), "edge", 0, 0)
    return jnp.sum(got.astype(F32), axis=0)


def slow_path(batch, edge, args):
    (states, edge_feats, molecule, source, target, edge_mask, w_edge_in, b_edge_in, w_edge_out, b_edge_out,
     w_input, w_hidden, b_input, b_hidden, cotangent) = args
    states_here = states[0]
    feats = edge_feats[0]
    source_ids = source[0]
    target_ids = target[0]
    width = states_here.shape[1]
    owned = states_here.shape[0]
    edges = source_ids.shape[0]
    block = min(512, edges)
    count = edges // block
    labels = from_all(molecule[0], edge)
    same = (jnp.take(labels, source_ids) == jnp.take(labels, target_ids)).astype(jnp.float32)
    valid = edge_mask[0].astype(jnp.float32) * same
    near = pick_by(source_ids, from_all(states_here, edge)).astype(
        jnp.bfloat16
    )
    hidden, edge_pull = jax.vjp(
        edge_hidden,
        feats.astype(jnp.float32),
        w_edge_in.astype(jnp.float32),
        b_edge_in.astype(jnp.float32),
    )
    latent_blocks = hidden.astype(jnp.bfloat16).reshape(count, block, -1)
    near_blocks = near.reshape(count, block, width)
    bias_out = b_edge_out.astype(jnp.float32)

    def expand(latent):
        flat = jnp.dot(latent, w_edge_out, preferred_element_type=jnp.float32) + bias_out
        return flat.astype(jnp.bfloat16).reshape(latent.shape[0], width, width)

    def apply(mats, vectors):
        return jnp.einsum("bij,bj->bi", mats, vectors, preferred_element_type=jnp.float32)

    outgoing = lax.map(lambda item: apply(expand(item[0]), item[1]), (latent_blocks, near_blocks))
    messages = (outgoing.reshape(edges, width) * valid[:, None]).astype(jnp.bfloat16)
    summed = to_owners(spread_by(target_ids, messages, edge * owned), edge)
    mixed = summed.astype(jnp.bfloat16).astype(jnp.float32)
    updated, update_pull = jax.vjp(
        gated_update,
        mixed,
        states_here.astype(jnp.float32),
        w_input.astype(jnp.float32),
        w_hidden.astype(jnp.float32),
        b_input.astype(jnp.float32),
        b_hidden.astype(jnp.float32),
    )
    new_states = updated.astype(jnp.bfloat16)
    d_mixed, d_direct, grad_wi, grad_wh, grad_bi, grad_bh = update_pull(
        cotangent[0].astype(jnp.float32)
    )
    pulled = pick_by(
        target_ids, from_all(d_mixed.astype(jnp.bfloat16), edge)
    )
    d_message = (pulled * valid[:, None]).astype(jnp.bfloat16)
    d_message_blocks = d_message.reshape(count, block, width)

    def backward_core(carry, mats, latent, vectors, d_out):
        grad_weight, grad_bias = carry
        outer = (
            d_out.astype(jnp.float32)[:, :, None] * vectors.astype(jnp.float32)[:, None, :]
        ).astype(jnp.bfloat16)
        flat = outer.reshape(latent.shape[0], width * width)
        d_latent = lax.dot_general(
            flat, w_edge_out, (((1,), (1,)), ((), ())), preferred_element_type=jnp.float32
        )
        grad_weight = grad_weight + lax.dot_general(
            latent, flat, (((0,), (0,)), ((), ())), preferred_element_type=jnp.float32
        )
        grad_bias = grad_bias + jnp.sum(flat.astype(jnp.float32), axis=0)
        d_vectors = jnp.einsum(
            "bij,bi->bj", mats, d_out, preferred_element_type=jnp.float32
        ).astype(jnp.bfloat16)
        return ((grad_weight, grad_bias), (d_latent, d_vectors))

    start_carry = (
        jnp.zeros((w_edge_out.shape[0], width * width), jnp.float32),
        jnp.zeros((width * width,), jnp.float32),
    )

    def backward_block(carry, item):
        return backward_core(carry, expand(item[0]), item[0], item[1], item[2])

    sums_out, per_edge = lax.scan(
        backward_block, start_carry, (latent_blocks, near_blocks, d_message_blocks)
    )
    grad_w2, grad_b2 = sums_out
    d_latent_all = per_edge[0].reshape(edges, -1)
    d_near_all = per_edge[1].reshape(edges, width)
    d_feats, grad_w1, grad_b1 = edge_pull(d_latent_all)
    returned = to_owners(spread_by(source_ids, d_near_all, owned * edge).astype(jnp.bfloat16), edge)
    state_grads = d_direct + returned

    bits, chunks, piece_arr = plan(batch, edge)
    devices = batch * edge
    pieces = grad_w2.reshape(PIECES, UNITS, H, H)
    small = jnp.concatenate([grad_wi, grad_wh, grad_b2.reshape(H, H)], axis=1).reshape(PIECES, UNITS, 7, H)
    small = small.transpose(0, 2, 1, 3).reshape(PIECES, 7 * UNITS, H)
    biases = jnp.concatenate([grad_bi, grad_bh]).reshape(6, H)
    biases = jnp.concatenate([biases, jnp.zeros((PIECES - 6, H), F32)], axis=0)[:, None]
    small = jnp.concatenate([small, biases, jnp.zeros((PIECES, EXTRA - 7 * UNITS - 1, H), F32)], axis=1)
    terms = []
    for chunk in chunks:
        block = pieces[:, :, chunk.first : chunk.first + chunk.rows].reshape(PIECES, -1, H)
        if chunk.extra:
            block = jnp.concatenate([block, small], axis=1)
        rel_of = sorted(range(PIECES // 2), key=chunk.place)
        order = jnp.array(rel_of + [PIECES // 2 + r for r in rel_of], jnp.int32)
        block = jnp.take(block, jnp.bitwise_xor(order, piece_arr[0]), axis=0).astype(BF16)
        shape = chunk.shape()
        kept, sent = block[: PIECES // 2].reshape(shape), block[PIECES // 2 :].reshape(shape)
        total = add([kept, swap(sent, bits[-1], devices)])
        for step in range(len(chunk.steps)):
            zero = (0,) * len(chunk.steps[step])
            total = add([total[zero]] + [swap(total[path], mask, devices) for path, mask in chunk.partners(step, bits)])
        terms.append(total)
    first = jnp.concatenate([grad_w1, grad_b1[None], jnp.zeros((15, H), F32)], axis=0)
    for n in range(devices.bit_length() - 1):
        mask = 1 << n
        if mask not in bits:
            terms = [rounded(w.astype(F32) + swap(w, mask, devices).astype(F32)) for w in terms]
        first = first + swap(first, mask, devices)
    for step in (3, 2, 1):
        terms = [gather_step(chunk, step, bits, devices, x) for x, chunk in zip(terms, chunks)]
    came = [swap(x, bits[chunk.order[0]], devices) for x, chunk in zip(terms, chunks)]
    early = early_half(chunks, bits, devices, piece_arr, terms)
    return new_states, state_grads, d_feats.T, first.astype(BF16), came, early


def per_device(batch, edge, *args):
    overflow, results = fast_path(batch, edge, args)
    results = lax.while_loop(
        lambda carry: carry[0], lambda carry: (jnp.bool_(False), slow_path(batch, edge, args)), (overflow, results)
    )[1]
    return finish(batch, edge, results)


def solution(mesh):
    batch, edge = mesh.shape["batch"], mesh.shape["edge"]
    nodes, edges, all_ = P("batch", "edge", None), P("batch", "edge"), P()
    return jax.shard_map(
        functools.partial(per_device, batch, edge),
        mesh=mesh,
        in_specs=(nodes, nodes, edges, edges, edges, edges) + (all_,) * 8 + (nodes,),
        out_specs=(nodes, nodes, nodes) + (all_,) * 8,
        check_vma=False,
    )
```

```python
import functools

import jax
import jax.numpy as jnp
from jax import lax
from jax.experimental import pallas as pl
from jax.experimental.pallas import tpu as pltpu
from jax.sharding import PartitionSpec as P

F32 = jnp.float32
BF16 = jnp.bfloat16
H = 128
CAP = 64
GROUP = 16
SUB = 8
SIDE = CAP // 2
PIECES = 32
UNITS = H // PIECES
EXTRA = 32
CHUNKS = (
    (0, 64, 0, ((3,), (2,), (1,), (0,))),
    (64, 64, EXTRA, ((2,), (3,), (1,), (0,))),
)
VMEM_LIMIT = 60 * 1024 * 1024
UNROLL = 4
BACK_UNROLL = 4
AGG = 32
TIED = (0, 1)
GIVE = 2
LAST_GIVE = 0
COST = 0.02
KSTEP = 64
MATRIX_FIRST = True


def nn(a, b):
    return lax.dot_general(a, b, (((1,), (0,)), ((), ())), preferred_element_type=F32)


def nt(a, b):
    return lax.dot_general(a, b, (((1,), (1,)), ((), ())), preferred_element_type=F32)


def eye(n):
    rows = lax.broadcasted_iota(jnp.int32, (n, n), 0)
    cols = lax.broadcasted_iota(jnp.int32, (n, n), 1)
    return jnp.where(rows == cols, 1.0, 0.0).astype(BF16)


def one_hot_rows(rel, count):
    rel = jnp.clip(rel, -1, count).astype(F32).astype(BF16)
    rows = lax.broadcasted_iota(jnp.int32, (count, rel.shape[1]), 0).astype(F32).astype(BF16)
    return jnp.where(rows == rel, jnp.ones((), BF16), jnp.zeros((), BF16))


def slot_hots(slot, count):
    return one_hot_rows(jnp.right_shift(slot, 7), count), one_hot_rows(jnp.bitwise_and(slot, H - 1), H)


def sort_kernel(shape, me_ref, target_ref, source_ref, mask_ref, label_ref, feats_ref, states_ref, out_ref, slot_ref, data_ref):
    holders, own, groups = shape
    blocks = groups // 2
    edges = target_ref.shape[1]
    target = target_ref[...]
    owner = jnp.right_shift(target, own.bit_length() - 1)
    local = jnp.bitwise_and(target, own - 1)
    bucket = owner * (2 * groups) + jnp.right_shift(local, 3)
    bucket = jnp.where(mask_ref[...] != 0, bucket, -1)
    buckets = holders * groups * 2
    turn = jnp.bitwise_and(me_ref[0], 3)

    block = 256
    rows = lax.broadcasted_iota(jnp.int32, (block, block), 0)
    cols = lax.broadcasted_iota(jnp.int32, (block, block), 1)
    upto = jnp.where(rows <= cols, 1.0, 0.0).astype(BF16)
    numbers = lax.broadcasted_iota(jnp.int32, (buckets, block), 0)
    hots = [numbers == bucket[:, b * block : (b + 1) * block] for b in range(edges // block)]
    counts = nn(jnp.concatenate([hot.astype(F32).astype(BF16) for hot in hots], axis=0), upto)
    carry = jnp.zeros((buckets, 1), F32)
    slots = []
    for b, hot in enumerate(hots):
        here = bucket[:, b * block : (b + 1) * block]
        within = counts[b * buckets : (b + 1) * buckets, :] + carry
        rank = jnp.sum(jnp.where(hot, within - 1.0, 0.0), axis=0, keepdims=True).astype(jnp.int32)
        carry = within[:, block - 1 : block]
        at = jnp.where(jnp.bitwise_and(here, 1) == 0, rank, CAP - 1 - rank)
        side = jnp.bitwise_and(jnp.bitwise_and(here, 2) + jnp.right_shift(at, 5) + turn, 3)
        place = jnp.right_shift(here, 2) * H + side * SIDE + jnp.bitwise_and(at, SIDE - 1)
        slots.append(jnp.where((here >= 0) & (rank < CAP), place, -1))
    both = carry + jnp.concatenate([carry[1:, :], carry[:1, :]], axis=0)
    first_of_two = jnp.bitwise_and(lax.broadcasted_iota(jnp.int32, (buckets, 1), 0), 1) == 0
    worst = jnp.max(jnp.where(first_of_two, both, 0.0), axis=0, keepdims=True)
    flag = jnp.where(worst > CAP, 1.0, 0.0)
    slot = jnp.concatenate(slots, axis=1)
    slot_ref[...] = slot

    data_ref[16:32, :] = jnp.zeros((16, edges), F32)
    data_ref[0:16, :] = feats_ref[...].astype(F32)
    source = source_ref[...]
    data_ref[16:17, :] = jnp.right_shift(source, 6).astype(F32)
    data_ref[17:18, :] = jnp.bitwise_and(source, 63).astype(F32)
    data_ref[18:19, :] = (local + 1).astype(F32)
    data = data_ref[...].astype(BF16)

    tags = []
    for t in range(own // H):
        label = label_ref[:, t * H : (t + 1) * H]
        tags += [jnp.right_shift(label, 6).astype(F32), jnp.bitwise_and(label, 63).astype(F32)]
    tags.append(jnp.broadcast_to(flag, (1, H)))
    tags.append(jnp.zeros((16 - 3 * blocks - len(tags), H), F32))
    high, low = slot_hots(slot, holders * blocks)
    together = min(4, holders)
    for s0 in range(0, holders, together):
        part = high[s0 * blocks : (s0 + together) * blocks, :]
        spread = (part[:, None, :] * data[None, :, :]).reshape(together * blocks * 32, edges)
        moved = nt(spread, low)
        for n in range(together):
            out = out_ref.at[s0 + n]
            out[0:own, :] = states_ref[...]
            ids = []
            for q in range(blocks):
                at = (n * blocks + q) * 32
                out[own + 16 * q : own + 16 * (q + 1), :] = moved[at : at + 16, :].astype(BF16)
                ids.append(moved[at + 16 : at + 19, :])
            out[own + 16 * blocks : own + 16 * blocks + 16, :] = jnp.concatenate(ids + tags, axis=0).astype(BF16)


def swap_rows(outer, inner, flip=None):
    n = outer * inner
    rows = lax.broadcasted_iota(jnp.int32, (n, n), 0)
    cols = lax.broadcasted_iota(jnp.int32, (n, n), 1)
    number = jnp.bitwise_and(rows, inner - 1)
    if flip is not None:
        number = jnp.bitwise_xor(number, flip)
    source = number * outer + jnp.right_shift(rows, inner.bit_length() - 1)
    return jnp.where(source == cols, 1.0, 0.0).astype(BF16)


def split_kernel(w_ref, out_ref, order_ref):
    @pl.when(pl.program_id(0) == 0)
    def _():
        order_ref[...] = swap_rows(16, 16)

    order = order_ref[...]
    for ib in range(0, H, 32):
        sides = []
        for half in range(2):
            rows = [w_ref[:, (ib + 16 * half + i) * H : (ib + 16 * half + i + 1) * H] for i in range(16)]
            sides.append(jnp.concatenate(rows, axis=0))
        moved = nn(order, jnp.concatenate(sides, axis=1)).astype(BF16)
        for half in range(2):
            at = ib + 16 * half
            out_ref[:, at : at + 16, :] = moved[:, half * H : (half + 1) * H].reshape(16, 16, H)


def front_kernel(shape, chunks, *refs):
    holders, own, groups = shape
    blocks = groups // 2
    refs = list(refs)
    take = lambda n: [refs.pop(0) for _ in range(n)]
    piece_ref, given, states_ref, own_label_ref, t_in, b2_ref, w1_ref, b1_ref, wi_ref, wh_ref, bi_ref, bh_ref, cot_ref = take(13)
    new_ref, direct_ref, d_ref, crossed_ref, lat_out, near_out, meta_out = take(7)
    outs = take(sum(len(chunk.heads) for chunk in chunks) + 1)
    table_ref, p_ref, sum_ref, small_ref, dt_ref, rows_ref, bias_ref, extra_ref, t_ref, lat_ref, near_ref, meta_ref = take(12)
    built = take(len(outs))
    (sems,) = refs
    waiting = []

    def copy(source, target):
        moving = pltpu.make_async_copy(source, target, sems.at[len(waiting)])
        moving.start()
        waiting.append(moving)
        return moving

    t_copy = copy(t_in, t_ref)

    nodes = holders * own
    lanes = holders * SIDE
    ident = eye(H)
    tags_at = own + 16 * blocks

    flag = jnp.zeros((1, 1), F32)
    for s in range(holders):
        tags = given[s, tags_at : tags_at + 16, :].astype(F32)
        flag = jnp.maximum(flag, tags[3 * blocks + 2 * (own // H) : 3 * blocks + 2 * (own // H) + 1, 0:1])
        for t in range(own // H):
            at = s * own + t * H
            table_ref[0:H, at : at + H] = nt(ident, given[s, t * H : (t + 1) * H, :]).astype(BF16)
            both = tags[3 * blocks + 2 * t : 3 * blocks + 2 * t + 2, :]
            table_ref[H : H + 16, at : at + H] = jnp.concatenate([both, jnp.zeros((14, H), F32)], axis=0).astype(BF16)
    for t in range(own // H):
        label = own_label_ref[:, t * H : (t + 1) * H]
        label = jnp.concatenate([jnp.right_shift(label, 6), jnp.bitwise_and(label, 63)], axis=0).astype(F32)
        cols = nt(ident, jnp.concatenate([label, jnp.zeros((14, H), F32)], axis=0).astype(BF16))
        small_ref[t * H : (t + 1) * H, 0:1] = cols[:, 0:1] * 64.0 + cols[:, 1:2]

    side = lax.broadcasted_iota(jnp.int32, (24, H), 1) // SIDE
    crossing = jnp.zeros((1, H), F32)
    for q in range(blocks):
        for s in range(0, holders, 4):
            parts = []
            for n in range(4):
                feats = given[s + n, own + 16 * q : own + 16 * (q + 1), :].astype(F32)
                ids = given[s + n, tags_at : tags_at + 16, :].astype(F32)[3 * q : 3 * q + 3, :]
                parts.append(jnp.concatenate([feats, ids, jnp.zeros((5, H), F32)], axis=0))
            at = slice(s // 4 * H, (s // 4 + 1) * H)
            for u in range(4):
                page = parts[(3 - u) % 4]
                for c in range(3):
                    page = jnp.where(side == c, parts[(c - u) % 4], page)
                meta_ref[4 * q + u, 0:24, at] = page
                low = float((4 * q + u) * SUB)
                node = page[18:19, :] - 1.0
                outside = (node >= 0.0) & ((node < low) | (node >= low + SUB))
                crossing = jnp.maximum(crossing, jnp.where(outside, 1.0, 0.0))
    crossed = jnp.max(crossing) > 0.0
    crossed_ref[0] = crossed.astype(jnp.int32)

    w1 = nt(ident, w1_ref[...]).astype(BF16)
    b1 = nt(ident, jnp.broadcast_to(b1_ref[...].astype(F32), (16, H)).astype(BF16))[:, 0:1]

    def both_pages(ref, g, rows):
        return jnp.concatenate([ref[2 * g + n, rows, :] for n in range(2)], axis=1)

    def group_step(usual, g, unused):
        data = both_pages(meta_ref, g, slice(0, 24))
        source = (data[16:17, :] * 64.0 + data[17:18, :]).astype(jnp.int32)
        picked = jnp.zeros((H + 16, 2 * lanes), F32)
        for c in range(0, nodes, 256):
            picked = picked + nn(table_ref[:, c : c + 256], one_hot_rows(source - c, 256))
        near = picked[0:H, :].astype(BF16)
        label = picked[H : H + 1, :] * 64.0 + picked[H + 1 : H + 2, :]
        inside = data[18:19, :] - 1.0 - (g * GROUP).astype(F32)
        numbers = lax.broadcasted_iota(jnp.int32, (GROUP, 2 * lanes), 0).astype(F32)
        own_label = small_ref[pl.ds(pl.multiple_of(g * GROUP, GROUP), GROUP), 0:1]
        member = jnp.where((numbers == inside) & (own_label == label), 1.0, 0.0)
        before = nn(w1, data[0:16, :].astype(BF16)) + b1
        latent = before / (1.0 + jnp.exp(-before))
        made = []
        for n in range(2):
            page = slice(n * lanes, (n + 1) * lanes)
            meta_ref[2 * g + n, 24:25, :] = source[:, page].astype(F32)
            meta_ref[2 * g + n, 32 : 32 + GROUP, :] = member[:, page]
            lat_ref[2 * g + n] = latent[:, page].astype(BF16)
            near_ref[2 * g + n] = near[:, page]
            mine = member[n * SUB : (n + 1) * SUB, :]
            if usual:
                units, states, mine = latent[:, page], near[:, page], mine[:, page]
            else:
                units, states = latent, near
            spread = (units[:, None, :] * mine[None, :, :]).reshape(H * SUB, -1).astype(BF16)
            made.append(nt(spread, states).reshape(H, SUB, H))
        at = pl.ds(pl.multiple_of(g * GROUP, GROUP), GROUP)
        p_ref[:, at, :] = jnp.concatenate(made, axis=1).astype(BF16)
        sum_ref[at, :] = nt(member.astype(BF16), near)
        return unused

    @pl.when(jnp.logical_not(crossed))
    def _():
        lax.fori_loop(0, groups, functools.partial(group_step, True), 0, unroll=UNROLL)

    @pl.when(crossed)
    def _():
        lax.fori_loop(0, groups, functools.partial(group_step, False), 0)

    copy(lat_ref, lat_out)
    copy(near_ref, near_out)
    copy(meta_ref, meta_out)

    def agg_step(n, total):
        left = jnp.concatenate([p_ref[n * AGG + m] for m in range(AGG)], axis=1)
        right = jnp.concatenate([t_ref[n * AGG + m] for m in range(AGG)], axis=1)
        return total + nt(left, right)

    total = nt(sum_ref[...].astype(BF16), b2_ref[...])
    t_copy.wait()
    total = lax.fori_loop(0, H // AGG, agg_step, total)

    mixed = total.astype(BF16)
    prior = states_ref[...]
    prior_f = prior.astype(F32)
    cot = cot_ref[...].astype(F32)
    wi, wh = wi_ref[...], wh_ref[...]
    gi = nn(mixed, wi) + bi_ref[...]
    gh = nn(prior, wh) + bh_ref[...]
    r = jax.nn.sigmoid(gi[:, 0:H] + gh[:, 0:H])
    u = jax.nn.sigmoid(gi[:, H : 2 * H] + gh[:, H : 2 * H])
    n = jnp.tanh(gi[:, 2 * H :] + r * gh[:, 2 * H :])
    new_ref[...] = ((1.0 - u) * n + u * prior_f).astype(BF16)
    d_pre = (1.0 - u) * cot * (1.0 - n * n)
    d_r = d_pre * gh[:, 2 * H :] * r * (1.0 - r)
    d_u = (prior_f - n) * cot * u * (1.0 - u)
    d_gi = jnp.concatenate([d_r, d_u, d_pre], axis=1)
    d_gh = jnp.concatenate([d_r, d_u, d_pre * r], axis=1)

    def halves(x):
        high = x.astype(BF16)
        return high, (x - high.astype(F32)).astype(BF16)

    def twice(x):
        return jnp.concatenate([x, x], axis=1)

    gi_high, gi_low = halves(d_gi)
    gh_high, gh_low = halves(d_gh)
    d_agg = nt(jnp.concatenate([gi_high, gi_low], axis=1), twice(wi)).astype(BF16)
    d_ref[...] = d_agg
    dt_ref[...] = nt(ident, d_agg).astype(BF16)
    direct_ref[...] = u * cot + nt(jnp.concatenate([gh_high, gh_low], axis=1), twice(wh))

    piece_me = piece_ref[0]
    joint = built[-1]

    def dest(c, rel):
        place = chunks[c].place(rel)
        if rel >= PIECES // 2:
            return joint, place, chunks[c].offset
        before = sum(len(chunk.heads) for chunk in chunks[:c])
        for n, head in enumerate(chunks[c].heads):
            count = PIECES // 2 >> len(head)
            if place < count:
                return built[before + n], place, 0
            place -= count

    mixed_t = nt(ident, mixed).astype(BF16)
    prior_t = nt(ident, prior).astype(BF16)
    from_input = nn(twice(mixed_t), jnp.concatenate([gi_high, gi_low], axis=0))
    from_state = nn(twice(prior_t), jnp.concatenate([gh_high, gh_low], axis=0))
    for t in range(3):
        rows_ref[t, 0:H, :] = from_input[:, t * H : (t + 1) * H]
        rows_ref[3 + t, 0:H, :] = from_state[:, t * H : (t + 1) * H]
    rows_ref[6, 0:H, :] = nn(dt_ref[...], sum_ref[...].astype(BF16))
    bias_ref[...] = jnp.zeros_like(bias_ref)
    for n, part in enumerate((d_gi, d_gh)):
        part = jnp.sum(part, axis=0, keepdims=True)
        for t in range(3):
            bias_ref[3 * n + t : 3 * n + t + 1, :] = part[:, t * H : (t + 1) * H]
    extra_ref[...] = jnp.zeros_like(extra_ref)
    extra_ref[29:30, :] = jnp.broadcast_to(flag, (1, H))
    last = chunks[-1]
    for rel in list(range(PIECES // 2, PIECES)) + list(range(PIECES // 2)):
        p = jnp.bitwise_xor(piece_me, rel)
        for t in range(7):
            extra_ref[UNITS * t : UNITS * (t + 1), :] = rows_ref[t, pl.ds(p * UNITS, UNITS), :]
        extra_ref[28:29, :] = bias_ref[pl.ds(p, 1), :]
        ref, place, offset = dest(len(chunks) - 1, rel)
        ref[place, offset + UNITS * last.rows : offset + last.height, :] = extra_ref[...].astype(BF16)

    for rel in list(range(PIECES // 2, PIECES)) + list(range(PIECES // 2)):
        k0 = jnp.bitwise_xor(piece_me, rel) * UNITS
        for m in range(0, UNITS, 2):
            out = nn(dt_ref[...], jnp.concatenate([p_ref[k0 + m], p_ref[k0 + m + 1]], axis=1)).astype(BF16)
            for c, chunk in enumerate(chunks):
                ref, place, offset = dest(c, rel)
                for h in range(2):
                    start = offset + (m + h) * chunk.rows
                    ref[place, start : start + chunk.rows, :] = out[
                        chunk.first : chunk.first + chunk.rows, h * H : (h + 1) * H
                    ]
        if rel == PIECES - 1:
            copy(joint, outs[-1])
    for n in range(len(built) - 1):
        copy(built[n], outs[n])
    for moving in waiting[1:]:
        moving.wait()


def spread_kernel(shape, d_ref, t_ref, b2_ref, wide_ref, bias_ref, dp_ref, order_ref):
    holders, own, groups = shape
    d = d_ref[...]

    @pl.when(pl.program_id(0) == 0)
    def _():
        bias_ref[...] = nn(d, b2_ref[...])
        order_ref[...] = swap_rows(16, 16)

    order = order_ref[...]
    for n in range(0, t_ref.shape[0], 2):
        out = nn(d, jnp.concatenate([t_ref[n], t_ref[n + 1]], axis=1)).astype(BF16)
        dp_ref[n] = out[:, :H]
        dp_ref[n + 1] = out[:, H:]
    for k in range(0, t_ref.shape[0], 16):
        for g in range(0, groups, 2):
            sides = [dp_ref[k : k + 16, (g + n) * GROUP : (g + n + 1) * GROUP, :].reshape(256, H) for n in range(2)]
            moved = nn(order, jnp.concatenate(sides, axis=1)).astype(BF16)
            for n in range(2):
                for v in range(GROUP):
                    wide_ref[g + n, k : k + 16, v * H : (v + 1) * H] = moved[v * 16 : (v + 1) * 16, n * H : (n + 1) * H]


def back_kernel(shape, masks, me_ref, *refs):
    holders, own, groups = shape
    blocks = groups // 2
    crossed_ref, wide_in, bias_ref, w1_ref, b1_ref, lat_in, near_in, meta_in = refs[:8]
    keep_d, keep_e, send_ref, first_ref = refs[8:12]
    part_ref, edge_ref, sum_ref, slab_ref, wide_ref, lat_ref, near_ref, meta_ref, sems = refs[12:]

    def coming(g):
        pages = pl.ds(2 * g, 2)
        return [
            pltpu.make_async_copy(wide_in.at[g], wide_ref.at[g], sems.at[0, g]),
            pltpu.make_async_copy(lat_in.at[pages], lat_ref.at[pages], sems.at[1, g]),
            pltpu.make_async_copy(near_in.at[pages], near_ref.at[pages], sems.at[2, g]),
            pltpu.make_async_copy(meta_in.at[pages], meta_ref.at[pages], sems.at[3, g]),
        ]

    for g in range(groups):
        for copy in coming(g):
            copy.start()
    nodes = holders * own
    lanes = holders * SIDE
    ident = eye(H)
    part_ref[...] = jnp.zeros_like(part_ref)
    w1n = w1_ref[...]
    w1 = nt(ident, w1n).astype(BF16)
    b1 = nt(ident, jnp.broadcast_to(b1_ref[...].astype(F32), (16, H)).astype(BF16))[:, 0:1]
    one_row = jnp.where(lax.broadcasted_iota(jnp.int32, (16, 2 * lanes), 0) == 0, 1.0, 0.0).astype(BF16)

    def both_pages(ref, g, rows):
        return jnp.concatenate([ref[2 * g + n, rows, :] for n in range(2)], axis=1)

    def group_step(usual, g, first_total):
        for copy in coming(g):
            copy.wait()
        wide = wide_ref[g]
        wide_t = jnp.concatenate([wide[:, v * H : (v + 1) * H].T for v in range(GROUP)], axis=1)
        bias_rows = bias_ref[pl.ds(pl.multiple_of(g * GROUP, GROUP), GROUP), :].astype(BF16)
        bias_t = nt(ident, bias_rows).astype(BF16)
        data = both_pages(meta_ref, g, slice(0, 16)).astype(BF16)
        source = both_pages(meta_ref, g, slice(24, 25)).astype(jnp.int32)
        member = both_pages(meta_ref, g, slice(32, 32 + GROUP)).astype(BF16)
        d_latent, d_near = [], []
        for n in range(2):
            low, number = (n * SUB, SUB) if usual else (0, GROUP)
            mine = meta_ref[2 * g + n, 32 + low : 32 + low + number, :].astype(BF16)
            part = slice(low * H, (low + number) * H)
            spread = (near_ref[2 * g + n][None, :, :] * mine[:, None, :]).reshape(number * H, lanes)
            d_latent.append(nn(wide[:, part], spread))
            spread = (lat_ref[2 * g + n][None, :, :] * mine[:, None, :]).reshape(number * H, lanes)
            d_near.append(nn(wide_t[:, part], spread))
        d_latent = jnp.concatenate(d_latent, axis=1)
        d_near = (jnp.concatenate(d_near, axis=1) + nn(bias_t, member)).astype(BF16)
        for c in range(0, nodes, 256):
            part_ref[c : c + 256, :] += nt(one_hot_rows(source - c, 256), d_near)
        before = nn(w1, data) + b1
        gate = 1.0 / (1.0 + jnp.exp(-before))
        d_before = (d_latent * gate * (1.0 + before * (1.0 - gate))).astype(BF16)
        edges = nn(w1n, d_before)
        for n in range(2):
            edge_ref[2 * g + n] = edges[:, n * lanes : (n + 1) * lanes]
        return first_total + nt(jnp.concatenate([data, one_row], axis=0), d_before)

    none = jnp.zeros((32, H), F32)

    @pl.when(crossed_ref[0] == 0)
    def _():
        sum_ref[...] = lax.fori_loop(0, groups, functools.partial(group_step, True), none, unroll=BACK_UNROLL)

    @pl.when(crossed_ref[0] != 0)
    def _():
        sum_ref[...] = lax.fori_loop(0, groups, functools.partial(group_step, False), none)

    first = sum_ref[...].astype(BF16)
    first_ref[...] = first
    half = holders // 2
    side = lax.broadcasted_iota(jnp.int32, (16, H), 1) // SIDE
    for q in range(blocks):
        for s in range(holders):
            at = slice(s // 4 * H, (s // 4 + 1) * H)
            parts = [edge_ref[4 * q + u, :, at] for u in range(4)]
            page = parts[(3 - s) % 4]
            for c in range(3):
                page = jnp.where(side == c, parts[(c - s) % 4], page)
            slab_ref[s, 16 * q : 16 * (q + 1), :] = page.astype(BF16)
    for n in range(holders):
        rel = sum(mask for i, mask in enumerate(reversed(masks)) if n >> i & 1)
        h = jnp.bitwise_xor(me_ref[0], rel)
        rows = part_ref[pl.ds(pl.multiple_of(h * own, own), own), :].astype(BF16)
        if n < half:
            keep_d[n] = rows
            keep_e[n] = slab_ref[h]
        else:
            send_ref[(n - half) * own : (n - half + 1) * own, :] = rows
            at = half * own + (n - half) * 16 * blocks
            send_ref[at : at + 16 * blocks, :] = slab_ref[h]


def gather_kernel(shape, sources, me_ref, slot_ref, direct_ref, part_ref, slabs_ref, state_ref, edge_ref, data_ref):
    holders, own, groups = shape
    blocks = groups // 2
    state_ref[...] = direct_ref[...] + part_ref[...].astype(F32)
    for n, rel in enumerate(sources):
        h = jnp.bitwise_xor(me_ref[0], rel)
        data_ref[pl.ds(pl.multiple_of(h * 16 * blocks, 16), 16 * blocks), :] = slabs_ref[n]
    edges = slot_ref.shape[1]
    data = data_ref[...]
    count = holders * blocks
    block = 512
    for b in range(edges // block):
        high, low = slot_hots(slot_ref[:, b * block : (b + 1) * block], count)
        high = high.astype(F32)
        found = nn(data, low)
        total = jnp.zeros((16, block), F32)
        for n in range(count):
            total = total + found[16 * n : 16 * (n + 1), :] * high[n : n + 1, :]
        edge_ref[:, b * block : (b + 1) * block] = total


class Chunk:
    def __init__(self, first, rows, extra, steps, offset):
        self.first, self.rows, self.extra, self.steps, self.offset = first, rows, extra, steps, offset
        self.height = UNITS * rows + extra
        self.order = sum(steps, ())
        ways = [(n,) for n in range(2)] if len(steps[0]) == 1 else [(n, m) for n in range(2) for m in range(2)]
        self.heads = [(0, 0), (0, 1), (1,)] if len(steps[0]) == 1 else ways

    def place(self, rel):
        at = 0
        for bit in self.order:
            at = at * 2 + (rel >> bit & 1)
        return at

    def shape(self):
        return (2,) * len(self.order) + (self.height, H)

    def partners(self, step, bits):
        group = self.steps[step]
        found = []
        for n in range(1, 2 ** len(group)):
            path = tuple(n >> (len(group) - 1 - i) & 1 for i in range(len(group)))
            found.append((path, sum(bits[bit] for bit, on in zip(group, path) if on)))
        return found


def plan(batch, edge):
    core, x = [edge], [edge << n for n in range(1, batch.bit_length() - 1)]
    z = [2 << n for n in reversed(range(3 - len(x)))]
    bits = z + [1] + x + core
    chunks, offset = [], 0
    for first, rows, extra, steps in CHUNKS:
        chunks.append(Chunk(first, rows, extra, steps, offset))
        offset += chunks[-1].height
    device = lax.axis_index(("batch", "edge")).astype(jnp.int32)
    piece = sum(jnp.where(device & mask != 0, 1 << n, 0) for n, mask in enumerate(bits))
    return bits, chunks, piece.astype(jnp.int32).reshape(1)


def swap(x, mask, devices):
    return lax.ppermute(x, ("batch", "edge"), [(i, i ^ mask) for i in range(devices)])


def add(terms):
    total = terms[0].astype(F32)
    for term in terms[1:]:
        total = total + term.astype(F32)
    return total.astype(BF16)


def rounded(x):
    return lax.reduce_precision(x.astype(F32), 8, 7).astype(BF16)


def jobs_of(chunks, arrived, cores):
    found = []
    for core in cores:
        for c, chunk in enumerate(chunks):
            last, beside = chunk.order[:2]
            for n in range(2):
                found.append((c, core, core * PIECES // 2 + (arrived << last) + (n << beside), 4 * n))
    return found


def unpack(chunks, jobs, me, order_ref, sources, block_refs, w_out, rows_ref, sems, beside=lambda: None):
    width = 4 * UNITS
    coming, leaving = [], []
    for n, (c, core, rel, place) in enumerate(jobs):
        coming.append(pltpu.make_async_copy(sources[n].at[pl.ds(place, 4)], block_refs[n], sems.at[n]))
        rows = pl.ds(pl.multiple_of(jnp.bitwise_xor(jnp.right_shift(me, 2), rel // 4) * width, width), width)
        lanes = pl.ds(chunks[c].first * H, chunks[c].rows * H)
        leaving.append(pltpu.make_async_copy(rows_ref.at[n % 3], w_out.at[rows, lanes], sems.at[len(jobs) + n]))
    for copy in coming:
        copy.start()
    order_ref[...] = swap_rows(32, 2 * UNITS, jnp.bitwise_and(me, 1) * UNITS)
    beside()
    for n, (c, core, rel, place) in enumerate(jobs):
        coming[n].wait()
        if n >= 3:
            leaving[n - 3].wait()
        rows = chunks[c].rows
        for pair in range(2):
            upper = jnp.bitwise_xor(jnp.bitwise_and(jnp.right_shift(me, 1), 1), pair)
            at_rows = pl.ds(pl.multiple_of(upper * 2 * UNITS, 2 * UNITS), 2 * UNITS)
            for ib in range(0, rows, 64):
                sides = []
                for at in (ib, ib + 32):
                    parts = [
                        block_refs[n][2 * pair + i, m * rows + at : m * rows + at + 32, :]
                        for i in range(2)
                        for m in range(UNITS)
                    ]
                    sides.append(jnp.concatenate(parts, axis=0))
                moved = nn(order_ref[...], jnp.concatenate(sides, axis=1))
                for side in range(2):
                    for i in range(32):
                        at = (ib + 32 * side + i) * H
                        rows_ref[n % 3, at_rows, at : at + H] = moved[8 * i : 8 * (i + 1), side * H : (side + 1) * H]
        leaving[n].start()

    def end():
        for copy in leaving[-3:]:
            copy.wait()

    return end


def small_piece(me, rel, extra, extra_ref, bias_ref):
    p = jnp.bitwise_xor(me, rel)
    extra = extra.astype(F32)
    for t in range(7):
        extra_ref[t, pl.ds(p * UNITS, UNITS), :] = extra[UNITS * t : UNITS * (t + 1), :]
    bias_ref[pl.ds(p, 1), :] = extra[28:29, :]


def small_pieces(chunks, jobs, me, block_refs, extra_ref, bias_ref):
    start = UNITS * chunks[-1].rows
    for n, (c, core, rel, place) in enumerate(jobs):
        if c == len(chunks) - 1:
            for i in range(4):
                small_piece(me, rel + i, block_refs[n][i, start : start + EXTRA, :], extra_ref, bias_ref)


def early_kernel(chunks, piece_ref, *refs):
    count = len(chunks)
    jobs = jobs_of(chunks, 0, (0, 1))
    sources = [refs[core * count + c] for c, core, rel, place in jobs]
    w_out, extra_ref, bias_ref = refs[2 * count : 2 * count + 3]
    block_refs, (rows_ref, order_ref, sems) = refs[2 * count + 3 : -3], refs[-3:]
    me = piece_ref[0]
    extra_ref[...] = jnp.zeros_like(extra_ref)
    bias_ref[...] = jnp.zeros_like(bias_ref)
    end = unpack(chunks, jobs, me, order_ref, sources, block_refs, w_out, rows_ref, sems)
    small_pieces(chunks, jobs, me, block_refs, extra_ref, bias_ref)
    end()


def late_kernel(chunks, piece_ref, *refs):
    count = len(chunks)
    jobs = jobs_of(chunks, 1, (0,))
    sources = [refs[c] for c, core, rel, place in jobs]
    w_in, w_out = refs[count : count + 2]
    block_refs, (rows_ref, order_ref, sems) = refs[count + 2 : -3], refs[-3:]
    unpack(chunks, jobs, piece_ref[0], order_ref, sources, block_refs, w_out, rows_ref, sems)()


def last_kernel(chunks, piece_ref, *refs):
    count = len(chunks)
    jobs = jobs_of(chunks, 1, (1,))
    sources = [refs[c] for c, core, rel, place in jobs]
    own_last, first_ref, extra_in, bias_in, w_in = refs[count : count + 5]
    w_out, w1_ref, b1_ref, wi_ref, wh_ref, b2_ref, bi_ref, bh_ref = refs[count + 5 : count + 13]
    block_refs, (rows_ref, order_ref, small_ref, extra_ref, bias_ref, sems) = refs[count + 13 : -6], refs[-6:]
    me = piece_ref[0]
    start = UNITS * chunks[-1].rows
    small = pltpu.make_async_copy(own_last.at[:, start : start + EXTRA, :], small_ref, sems.at[2 * len(jobs)])

    def beside():
        small.start()
        w1_ref[...] = first_ref[0:16, :].astype(F32)
        b1_ref[...] = first_ref[16:32, :].astype(F32)[0:1, :].reshape(H)
        extra_ref[...] = extra_in[...]
        bias_ref[...] = bias_in[...]

    end = unpack(chunks, jobs, me, order_ref, sources, block_refs, w_out, rows_ref, sems, beside)
    small_pieces(chunks, jobs, me, block_refs, extra_ref, bias_ref)
    small.wait()
    for c, core, rel, place in jobs_of(chunks, 1, (0,)):
        if c == count - 1:
            for i in range(4):
                small_piece(me, rel + i, small_ref[place + i], extra_ref, bias_ref)
    for t in range(3):
        wi_ref[:, t * H : (t + 1) * H] = extra_ref[t, 0:H, :]
        wh_ref[:, t * H : (t + 1) * H] = extra_ref[3 + t, 0:H, :]
        bi_ref[t * H : (t + 1) * H] = bias_ref[t : t + 1, :].reshape(H)
        bh_ref[t * H : (t + 1) * H] = bias_ref[3 + t : 4 + t, :].reshape(H)
    b2_ref[...] = extra_ref[6, 0:H, :]
    end()


def unpack_scratch(chunks, jobs, more=()):
    return (
        [pltpu.VMEM((4, chunks[c].height, H), BF16) for c, core, rel, place in jobs]
        + [pltpu.VMEM((3, 4 * UNITS, max(chunk.rows for chunk in chunks) * H), F32), pltpu.VMEM((256, 256), BF16)]
        + list(more)
        + [pltpu.SemaphoreType.DMA((2 * len(jobs) + 1,))]
    )


W_SHAPE = jax.ShapeDtypeStruct((H, H * H), F32)
SMALL = [jax.ShapeDtypeStruct((7, H + 8, H), F32), jax.ShapeDtypeStruct((PIECES + 8, H), F32)]


def early_half(chunks, bits, devices, piece_arr, parts):
    parts = [x.reshape(PIECES // 4, chunk.height, H) for x, chunk in zip(parts, chunks)]
    others = [swap(x, bits[-1], devices) for x in parts]
    return pl.pallas_call(
        functools.partial(early_kernel, chunks),
        name="assemble_early",
        in_specs=[smem()] + [anywhere()] * (2 * len(chunks)),
        out_specs=[anywhere(), vmem(), vmem()],
        scratch_shapes=unpack_scratch(chunks, jobs_of(chunks, 0, (0, 1))),
        out_shape=[W_SHAPE] + SMALL,
        compiler_params=params(),
        cost_estimate=cost(6),
    )(piece_arr, *parts, *others)


def vmem():
    return pl.BlockSpec(memory_space=pltpu.VMEM)


def anywhere():
    return pl.BlockSpec(memory_space=pl.ANY)


def smem():
    return pl.BlockSpec(memory_space=pltpu.SMEM)


def cost(us):
    return pl.CostEstimate(flops=int(us * COST * 1e9), bytes_accessed=int(us * COST * 3e6), transcendentals=0)


def params():
    return pltpu.CompilerParams(vmem_limit_bytes=VMEM_LIMIT)


def fast_path(batch, edge, args):
    (states, edge_feats, molecule, source, target, edge_mask, w_edge_in, b_edge_in, w_edge_out, b_edge_out,
     w_input, w_hidden, b_input, b_hidden, cotangent) = args
    devices = batch * edge
    states_here = states[0]
    own = states_here.shape[0]
    edges = source.shape[1]
    holders, groups = edge, own // GROUP
    shape = (holders, own, groups)
    blocks = groups // 2
    bits, chunks, piece_arr = plan(batch, edge)
    rest = [m for m in (1 << n for n in range(devices.bit_length() - 1)) if m not in bits]
    me_arr = lax.axis_index("edge").astype(jnp.int32).reshape(1)
    lanes = holders * SIDE
    pages = 2 * groups

    slots_out, slot = pl.pallas_call(
        functools.partial(sort_kernel, shape),
        name="edges_to_slots",
        out_shape=[
            jax.ShapeDtypeStruct((holders, own + 16 * blocks + 16, H), BF16),
            jax.ShapeDtypeStruct((1, edges), jnp.int32),
        ],
        in_specs=[smem()] + [vmem()] * 6,
        out_specs=[vmem()] * 2,
        scratch_shapes=[pltpu.VMEM((32, edges), F32)],
        compiler_params=params(),
    )(me_arr, target, source, edge_mask, molecule, jnp.swapaxes(edge_feats, 1, 2)[0], states_here)
    given = lax.all_to_all(slots_out, "edge", 0, 0)

    t_units = pl.pallas_call(
        split_kernel,
        name="split_weight",
        grid=(H // 16,),
        in_specs=[pl.BlockSpec((16, H * H), lambda i: (i, 0))],
        out_specs=pl.BlockSpec((16, H, H), lambda i: (i, 0, 0)),
        out_shape=jax.ShapeDtypeStruct((H, H, H), BF16),
        scratch_shapes=[pltpu.VMEM((256, 256), BF16)],
        compiler_params=params(),
        cost_estimate=cost(6),
    )(w_edge_out)
    b2 = b_edge_out.reshape(H, H)
    b1 = b_edge_in.reshape(1, H)
    built = [jax.ShapeDtypeStruct((PIECES // 2 >> len(h), c.height, H), BF16) for c in chunks for h in c.heads]
    built.append(jax.ShapeDtypeStruct((PIECES // 2, sum(c.height for c in chunks), H), BF16))
    front = pl.pallas_call(
        functools.partial(front_kernel, shape, chunks),
        name="messages_update_weight_gradient",
        out_shape=[
            jax.ShapeDtypeStruct((own, H), BF16),
            jax.ShapeDtypeStruct((own, H), F32),
            jax.ShapeDtypeStruct((own, H), BF16),
            jax.ShapeDtypeStruct((1,), jnp.int32),
            jax.ShapeDtypeStruct((pages, H, lanes), BF16),
            jax.ShapeDtypeStruct((pages, H, lanes), BF16),
            jax.ShapeDtypeStruct((pages, 32 + GROUP, lanes), F32),
        ]
        + built,
        in_specs=[smem()] + [vmem()] * 3 + [anywhere()] + [vmem()] * 8,
        out_specs=[vmem()] * 3 + [smem()] + [anywhere()] * (3 + len(built)),
        scratch_shapes=[
            pltpu.VMEM((H + 16, holders * own), BF16),
            pltpu.VMEM((H, own, H), BF16),
            pltpu.VMEM((own, H), F32),
            pltpu.VMEM((own, H), F32),
            pltpu.VMEM((H, own), BF16),
            pltpu.VMEM((7, H + 8, H), F32),
            pltpu.VMEM((PIECES + 8, H), F32),
            pltpu.VMEM((EXTRA, H), F32),
            pltpu.VMEM((H, H, H), BF16),
            pltpu.VMEM((pages, H, lanes), BF16),
            pltpu.VMEM((pages, H, lanes), BF16),
            pltpu.VMEM((pages, 32 + GROUP, lanes), F32),
        ]
        + [pltpu.VMEM(h.shape, BF16) for h in built]
        + [pltpu.SemaphoreType.DMA((4 + len(built),))],
        compiler_params=params(),
    )(
        piece_arr, given, states_here, molecule, t_units, b2, w_edge_in, b1, w_input, w_hidden,
        b_input.astype(F32).reshape(1, -1), b_hidden.astype(F32).reshape(1, -1), cotangent[0],
    )
    new_states, direct, d_agg, crossed, latent, near, meta = front[:7]
    built = front[7:]

    matrix_gradients = pl.pallas_call(
        functools.partial(spread_kernel, shape),
        name="matrix_gradients",
        out_shape=[jax.ShapeDtypeStruct((groups, H, GROUP * H), BF16), jax.ShapeDtypeStruct((own, H), F32)],
        grid=(H // KSTEP,),
        in_specs=[
            pl.BlockSpec((own, H), lambda i: (0, 0)),
            pl.BlockSpec((KSTEP, H, H), lambda i: (i, 0, 0)),
            pl.BlockSpec((H, H), lambda i: (0, 0)),
        ],
        out_specs=[
            pl.BlockSpec((groups, KSTEP, GROUP * H), lambda i: (0, i, 0)),
            pl.BlockSpec((own, H), lambda i: (0, 0)),
        ],
        scratch_shapes=[pltpu.VMEM((KSTEP, own, H), BF16), pltpu.VMEM((256, 256), BF16)],
        compiler_params=params(),
        cost_estimate=cost(6),
    )

    back_masks = [1 << n for n in range(edge.bit_length() - 1)]

    def edge_work(wide, bias):
        return pl.pallas_call(
            functools.partial(back_kernel, shape, back_masks),
            name="edge_gradients",
            out_shape=[
                jax.ShapeDtypeStruct((holders // 2, own, H), BF16),
                jax.ShapeDtypeStruct((holders // 2, 16 * blocks, H), BF16),
                jax.ShapeDtypeStruct((holders // 2 * (own + 16 * blocks), H), BF16),
                jax.ShapeDtypeStruct((32, H), BF16),
            ],
            in_specs=[smem()] * 2 + [anywhere()] + [vmem()] * 3 + [anywhere()] * 3,
            out_specs=[vmem()] * 4,
            scratch_shapes=[
                pltpu.VMEM((holders * own, H), F32),
                pltpu.VMEM((pages, 16, lanes), F32),
                pltpu.VMEM((32, H), F32),
                pltpu.VMEM((holders, 16 * blocks, H), BF16),
                pltpu.VMEM((groups, H, GROUP * H), BF16),
                pltpu.VMEM((pages, H, lanes), BF16),
                pltpu.VMEM((pages, H, lanes), BF16),
                pltpu.VMEM((pages, 32 + GROUP, lanes), F32),
                pltpu.SemaphoreType.DMA((4, groups)),
            ],
            compiler_params=params(),
            cost_estimate=cost(14),
        )(me_arr, crossed, wide, bias, w_edge_in, b1, latent, near, meta)

    if MATRIX_FIRST:
        sent, d_agg = lax.optimization_barrier((built[-1], d_agg))
        other = swap(sent, bits[-1], devices)
        other, (wide, bias) = lax.optimization_barrier((other, matrix_gradients(d_agg, t_units, b2)))
    else:
        other = swap(built[-1], bits[-1], devices)
        wide, bias = matrix_gradients(d_agg, t_units, b2)
    other = other.reshape((2,) * 4 + (-1, H))
    arrays = iter(built)
    kept = [{head: next(arrays) for head in chunk.heads} for chunk in chunks]
    got = [[] for _ in chunks]

    def mine(c, path):
        for head, x in kept[c].items():
            if path[: len(head)] == head:
                return x.reshape((2,) * (4 - len(head)) + x.shape[1:])[path[len(head) :]]

    def partial_sum(c, path):
        rows = slice(chunks[c].offset, chunks[c].offset + chunks[c].height)
        parts = [mine(c, path), other[path][..., rows, :]]
        for n, arrays in enumerate(got[c]):
            done = sum(len(group) for group in chunks[c].steps[: n + 1])
            parts += [x[path[done:]] for x in arrays]
        return add(parts)

    def scatter_step(step, work=None, given=()):
        begun = []
        for c, chunk in enumerate(chunks):
            done = (0,) * sum(len(group) for group in chunk.steps[:step])
            if step < len(chunk.steps):
                begun.append([partial_sum(c, done + path) for path, mask in chunk.partners(step, bits)])
            else:
                begun.append([])
        if work is not None:
            begun, given = lax.optimization_barrier((begun, given))
        new = [
            [swap(x, mask, devices) for x, (path, mask) in zip(begun[c], chunk.partners(step, bits))] if begun[c] else []
            for c, chunk in enumerate(chunks)
        ]
        result = None
        if work is not None:
            result = work(*given)
            for c in TIED:
                new[c], result = lax.optimization_barrier((new[c], result))
        for c in range(len(chunks)):
            if new[c]:
                got[c].append(new[c])
        return result

    keep_d, keep_e, send, first = scatter_step(0, edge_work, (wide, bias))
    for n in range(edge.bit_length() - 1, devices.bit_length() - 1):
        first = rounded(first.astype(F32) + swap(first, 1 << n, devices).astype(F32))
    scatter_step(1)
    slabs, sources = keep_e[:, None], [0]

    def give_back(mask, after):
        nonlocal keep_d, slabs, sources, send, first
        if after is not None:
            send, after = lax.optimization_barrier((send, after))
        n = keep_d.shape[0]
        cut = n * own
        arrived = swap(jnp.concatenate([send, first], axis=0), mask, devices)
        keep_d = add([keep_d, arrived[:cut].reshape(n, own, H)])
        slabs = jnp.concatenate([slabs, arrived[cut:-32].reshape(n, -1, 16 * blocks, H)], axis=1)
        first = rounded(first.astype(F32) + arrived[-32:].astype(F32))
        sources = sources + [s ^ mask for s in sources]
        if n > 1:
            send = jnp.concatenate([keep_d[n // 2 :].reshape(-1, H), slabs[n // 2 :].reshape(-1, H)], axis=0)
            keep_d, slabs = keep_d[: n // 2], slabs[: n // 2]

    give_back(1, got[1][1])
    scatter_step(2)
    scatter_step(3)
    parts = [partial_sum(c, (0,) * 4) for c in range(len(chunks))]
    for mask in rest:
        parts = [rounded(x.astype(F32) + swap(x, mask, devices).astype(F32)) for x in parts]
    overflow = parts[-1][UNITS * chunks[-1].rows + 29, 0] > 0.0
    for step in (3, 2, 1):
        if step == 2:
            parts[1], overflow = lax.optimization_barrier((parts[1], overflow))
        if step == GIVE:
            for mask in back_masks[1:-1]:
                give_back(mask, parts[0] if mask == 2 else None)
        for c, chunk in enumerate(chunks):
            parts[c] = gather_step(chunk, step, bits, devices, parts[c])
    give_back(back_masks[-1], parts[LAST_GIVE])
    came = [swap(x, bits[chunk.order[0]], devices) for x, chunk in zip(parts, chunks)]
    early = early_half(chunks, bits, devices, piece_arr, parts)
    state_grads, edge_grads = pl.pallas_call(
        functools.partial(gather_kernel, shape, sources),
        name="slots_to_edges",
        out_shape=[
            jax.ShapeDtypeStruct((own, H), F32),
            jax.ShapeDtypeStruct((edge_feats.shape[2], edges), F32),
        ],
        in_specs=[smem()] + [vmem()] * 4,
        out_specs=[vmem()] * 2,
        scratch_shapes=[pltpu.VMEM((holders * 16 * blocks, H), BF16)],
        compiler_params=params(),
        cost_estimate=cost(3),
    )(me_arr, slot, direct, keep_d[0], slabs[0])
    return overflow, (new_states, state_grads, edge_grads, first, came, early)


def gather_step(chunk, step, bits, devices, x):
    partners = chunk.partners(step, bits)
    all_ = jnp.stack([x] + [swap(x, mask, devices) for path, mask in partners], axis=0)
    return all_.reshape((2,) * len(chunk.steps[step]) + x.shape)


def finish(batch, edge, results):
    new_states, state_grads, edge_grads, first, came, early = results
    bits, chunks, piece_arr = plan(batch, edge)
    devices = batch * edge
    came = [x.reshape(PIECES // 4, chunk.height, H) for x, chunk in zip(came, chunks)]
    others = [swap(x, bits[-1], devices) for x in came]
    grad_w2, extras, biases = early
    grad_w2 = pl.pallas_call(
        functools.partial(late_kernel, chunks),
        name="assemble_late",
        in_specs=[smem()] + [anywhere()] * (len(chunks) + 1),
        out_specs=anywhere(),
        scratch_shapes=unpack_scratch(chunks, jobs_of(chunks, 1, (0,))),
        out_shape=W_SHAPE,
        input_output_aliases={len(chunks) + 1: 0},
        compiler_params=params(),
        cost_estimate=cost(4),
    )(piece_arr, *came, grad_w2)
    more = [pltpu.VMEM((PIECES // 4, EXTRA, H), BF16)] + [pltpu.VMEM(x.shape, F32) for x in SMALL]
    grad_w2, grad_w1, grad_b1, grad_wi, grad_wh, grad_b2, grad_bi, grad_bh = pl.pallas_call(
        functools.partial(last_kernel, chunks),
        name="assemble_last",
        in_specs=[smem()] + [anywhere()] * (len(chunks) + 1) + [vmem()] * 3 + [anywhere()],
        out_specs=[anywhere()] + [vmem()] * 7,
        scratch_shapes=unpack_scratch(chunks, jobs_of(chunks, 1, (1,)), more),
        out_shape=[W_SHAPE, jax.ShapeDtypeStruct((16, H), F32), jax.ShapeDtypeStruct((H,), F32)]
        + [jax.ShapeDtypeStruct((H, 3 * H), F32)] * 2
        + [jax.ShapeDtypeStruct((H, H), F32)]
        + [jax.ShapeDtypeStruct((3 * H,), F32)] * 2,
        input_output_aliases={len(chunks) + 5: 0},
        compiler_params=params(),
    )(piece_arr, *others, came[-1], first, extras, biases, grad_w2)
    return (
        new_states[None],
        state_grads[None],
        jnp.swapaxes(edge_grads[None], 1, 2),
        grad_w1,
        grad_b1,
        grad_w2,
        grad_b2.reshape(-1),
        grad_wi,
        grad_wh,
        grad_bi,
        grad_bh,
    )


HIGH = lax.Precision.HIGHEST


def gated_update(mixed, prior, w_input, w_hidden, b_input, b_hidden):
    width = prior.shape[1]
    from_input = jnp.dot(mixed, w_input, precision=HIGH) + b_input
    from_state = jnp.dot(prior, w_hidden, precision=HIGH) + b_hidden
    reset = jax.nn.sigmoid(from_input[:, :width] + from_state[:, :width])
    update = jax.nn.sigmoid(from_input[:, width : 2 * width] + from_state[:, width : 2 * width])
    candidate = jnp.tanh(from_input[:, 2 * width :] + reset * from_state[:, 2 * width :])
    return (1.0 - update) * candidate + update * prior


def edge_hidden(feats, w_edge_in, b_edge_in):
    return jax.nn.silu(jnp.dot(feats, w_edge_in, precision=HIGH) + b_edge_in)


def pick_by(index_rows, piece):
    columns = lax.broadcasted_iota(jnp.int32, (1, piece.shape[0]), 1)
    onehot = (index_rows[:, None] == columns).astype(jnp.bfloat16)
    return jnp.dot(onehot, piece, preferred_element_type=jnp.float32)


def spread_by(index_rows, values, count):
    rows = lax.broadcasted_iota(jnp.int32, (count, 1), 0)
    onehot = (rows == index_rows[None, :]).astype(jnp.bfloat16)
    return jnp.dot(onehot, values, preferred_element_type=jnp.float32)


def from_all(x, edge):
    got = lax.all_to_all(jnp.broadcast_to(x[None], (edge,) + x.shape), "edge", 0, 0)
    return got.reshape((-1,) + x.shape[1:])


def to_owners(x, edge):
    got = lax.all_to_all(x.reshape((edge, -1) + x.shape[1:]), "edge", 0, 0)
    return jnp.sum(got.astype(F32), axis=0)


def slow_path(batch, edge, args):
    (states, edge_feats, molecule, source, target, edge_mask, w_edge_in, b_edge_in, w_edge_out, b_edge_out,
     w_input, w_hidden, b_input, b_hidden, cotangent) = args
    states_here = states[0]
    feats = edge_feats[0]
    source_ids = source[0]
    target_ids = target[0]
    width = states_here.shape[1]
    owned = states_here.shape[0]
    edges = source_ids.shape[0]
    block = min(512, edges)
    count = edges // block
    labels = from_all(molecule[0], edge)
    same = (jnp.take(labels, source_ids) == jnp.take(labels, target_ids)).astype(jnp.float32)
    valid = edge_mask[0].astype(jnp.float32) * same
    near = pick_by(source_ids, from_all(states_here, edge)).astype(
        jnp.bfloat16
    )
    hidden, edge_pull = jax.vjp(
        edge_hidden,
        feats.astype(jnp.float32),
        w_edge_in.astype(jnp.float32),
        b_edge_in.astype(jnp.float32),
    )
    latent_blocks = hidden.astype(jnp.bfloat16).reshape(count, block, -1)
    near_blocks = near.reshape(count, block, width)
    bias_out = b_edge_out.astype(jnp.float32)

    def expand(latent):
        flat = jnp.dot(latent, w_edge_out, preferred_element_type=jnp.float32) + bias_out
        return flat.astype(jnp.bfloat16).reshape(latent.shape[0], width, width)

    def apply(mats, vectors):
        return jnp.einsum("bij,bj->bi", mats, vectors, preferred_element_type=jnp.float32)

    outgoing = lax.map(lambda item: apply(expand(item[0]), item[1]), (latent_blocks, near_blocks))
    messages = (outgoing.reshape(edges, width) * valid[:, None]).astype(jnp.bfloat16)
    summed = to_owners(spread_by(target_ids, messages, edge * owned), edge)
    mixed = summed.astype(jnp.bfloat16).astype(jnp.float32)
    updated, update_pull = jax.vjp(
        gated_update,
        mixed,
        states_here.astype(jnp.float32),
        w_input.astype(jnp.float32),
        w_hidden.astype(jnp.float32),
        b_input.astype(jnp.float32),
        b_hidden.astype(jnp.float32),
    )
    new_states = updated.astype(jnp.bfloat16)
    d_mixed, d_direct, grad_wi, grad_wh, grad_bi, grad_bh = update_pull(
        cotangent[0].astype(jnp.float32)
    )
    pulled = pick_by(
        target_ids, from_all(d_mixed.astype(jnp.bfloat16), edge)
    )
    d_message = (pulled * valid[:, None]).astype(jnp.bfloat16)
    d_message_blocks = d_message.reshape(count, block, width)

    def backward_core(carry, mats, latent, vectors, d_out):
        grad_weight, grad_bias = carry
        outer = (
            d_out.astype(jnp.float32)[:, :, None] * vectors.astype(jnp.float32)[:, None, :]
        ).astype(jnp.bfloat16)
        flat = outer.reshape(latent.shape[0], width * width)
        d_latent = lax.dot_general(
            flat, w_edge_out, (((1,), (1,)), ((), ())), preferred_element_type=jnp.float32
        )
        grad_weight = grad_weight + lax.dot_general(
            latent, flat, (((0,), (0,)), ((), ())), preferred_element_type=jnp.float32
        )
        grad_bias = grad_bias + jnp.sum(flat.astype(jnp.float32), axis=0)
        d_vectors = jnp.einsum(
            "bij,bi->bj", mats, d_out, preferred_element_type=jnp.float32
        ).astype(jnp.bfloat16)
        return ((grad_weight, grad_bias), (d_latent, d_vectors))

    start_carry = (
        jnp.zeros((w_edge_out.shape[0], width * width), jnp.float32),
        jnp.zeros((width * width,), jnp.float32),
    )

    def backward_block(carry, item):
        return backward_core(carry, expand(item[0]), item[0], item[1], item[2])

    sums_out, per_edge = lax.scan(
        backward_block, start_carry, (latent_blocks, near_blocks, d_message_blocks)
    )
    grad_w2, grad_b2 = sums_out
    d_latent_all = per_edge[0].reshape(edges, -1)
    d_near_all = per_edge[1].reshape(edges, width)
    d_feats, grad_w1, grad_b1 = edge_pull(d_latent_all)
    returned = to_owners(spread_by(source_ids, d_near_all, owned * edge).astype(jnp.bfloat16), edge)
    state_grads = d_direct + returned

    bits, chunks, piece_arr = plan(batch, edge)
    devices = batch * edge
    pieces = grad_w2.reshape(PIECES, UNITS, H, H)
    small = jnp.concatenate([grad_wi, grad_wh, grad_b2.reshape(H, H)], axis=1).reshape(PIECES, UNITS, 7, H)
    small = small.transpose(0, 2, 1, 3).reshape(PIECES, 7 * UNITS, H)
    biases = jnp.concatenate([grad_bi, grad_bh]).reshape(6, H)
    biases = jnp.concatenate([biases, jnp.zeros((PIECES - 6, H), F32)], axis=0)[:, None]
    small = jnp.concatenate([small, biases, jnp.zeros((PIECES, EXTRA - 7 * UNITS - 1, H), F32)], axis=1)
    terms = []
    for chunk in chunks:
        block = pieces[:, :, chunk.first : chunk.first + chunk.rows].reshape(PIECES, -1, H)
        if chunk.extra:
            block = jnp.concatenate([block, small], axis=1)
        rel_of = sorted(range(PIECES // 2), key=chunk.place)
        order = jnp.array(rel_of + [PIECES // 2 + r for r in rel_of], jnp.int32)
        block = jnp.take(block, jnp.bitwise_xor(order, piece_arr[0]), axis=0).astype(BF16)
        shape = chunk.shape()
        kept, sent = block[: PIECES // 2].reshape(shape), block[PIECES // 2 :].reshape(shape)
        total = add([kept, swap(sent, bits[-1], devices)])
        for step in range(len(chunk.steps)):
            zero = (0,) * len(chunk.steps[step])
            total = add([total[zero]] + [swap(total[path], mask, devices) for path, mask in chunk.partners(step, bits)])
        terms.append(total)
    first = jnp.concatenate([grad_w1, grad_b1[None], jnp.zeros((15, H), F32)], axis=0)
    for n in range(devices.bit_length() - 1):
        mask = 1 << n
        if mask not in bits:
            terms = [rounded(w.astype(F32) + swap(w, mask, devices).astype(F32)) for w in terms]
        first = first + swap(first, mask, devices)
    for step in (3, 2, 1):
        terms = [gather_step(chunk, step, bits, devices, x) for x, chunk in zip(terms, chunks)]
    came = [swap(x, bits[chunk.order[0]], devices) for x, chunk in zip(terms, chunks)]
    early = early_half(chunks, bits, devices, piece_arr, terms)
    return new_states, state_grads, d_feats.T, first.astype(BF16), came, early


def per_device(batch, edge, *args):
    overflow, results = fast_path(batch, edge, args)
    results = lax.while_loop(
        lambda carry: carry[0], lambda carry: (jnp.bool_(False), slow_path(batch, edge, args)), (overflow, results)
    )[1]
    return finish(batch, edge, results)


def solution(mesh):
    batch, edge = mesh.shape["batch"], mesh.shape["edge"]
    nodes, edges, all_ = P("batch", "edge", None), P("batch", "edge"), P()
    return jax.shard_map(
        functools.partial(per_device, batch, edge),
        mesh=mesh,
        in_specs=(nodes, nodes, edges, edges, edges, edges) + (all_,) * 8 + (nodes,),
        out_specs=(nodes, nodes, nodes) + (all_,) * 8,
        check_vma=False,
    )
```

```python
import functools

import jax
import jax.numpy as jnp
from jax import lax
from jax.experimental import pallas as pl
from jax.experimental.pallas import tpu as pltpu
from jax.sharding import PartitionSpec as P

F32 = jnp.float32
BF16 = jnp.bfloat16
H = 128
CAP = 64
GROUP = 16
SUB = 8
SIDE = CAP // 2
PIECES = 32
UNITS = H // PIECES
EXTRA = 32
CHUNKS = (
    (0, 64, 0, ((3,), (2,), (1,), (0,))),
    (64, 64, EXTRA, ((2,), (3,), (1,), (0,))),
)
VMEM_LIMIT = 60 * 1024 * 1024
UNROLL = 4
BACK_UNROLL = 4
AGG = 64
TIED = (0, 1)
GIVE = 2
LAST_GIVE = 0
COST = 0.02
KSTEP = 64
MATRIX_FIRST = True


def nn(a, b):
    return lax.dot_general(a, b, (((1,), (0,)), ((), ())), preferred_element_type=F32)


def nt(a, b):
    return lax.dot_general(a, b, (((1,), (1,)), ((), ())), preferred_element_type=F32)


def eye(n):
    rows = lax.broadcasted_iota(jnp.int32, (n, n), 0)
    cols = lax.broadcasted_iota(jnp.int32, (n, n), 1)
    return jnp.where(rows == cols, 1.0, 0.0).astype(BF16)


def one_hot_rows(rel, count):
    rel = jnp.clip(rel, -1, count).astype(F32).astype(BF16)
    rows = lax.broadcasted_iota(jnp.int32, (count, rel.shape[1]), 0).astype(F32).astype(BF16)
    return jnp.where(rows == rel, jnp.ones((), BF16), jnp.zeros((), BF16))


def slot_hots(slot, count):
    return one_hot_rows(jnp.right_shift(slot, 7), count), one_hot_rows(jnp.bitwise_and(slot, H - 1), H)


def sort_kernel(shape, me_ref, target_ref, source_ref, mask_ref, label_ref, feats_ref, states_ref, out_ref, slot_ref, data_ref):
    holders, own, groups = shape
    blocks = groups // 2
    edges = target_ref.shape[1]
    target = target_ref[...]
    owner = jnp.right_shift(target, own.bit_length() - 1)
    local = jnp.bitwise_and(target, own - 1)
    bucket = owner * (2 * groups) + jnp.right_shift(local, 3)
    bucket = jnp.where(mask_ref[...] != 0, bucket, -1)
    buckets = holders * groups * 2
    turn = jnp.bitwise_and(me_ref[0], 3)

    block = 256
    rows = lax.broadcasted_iota(jnp.int32, (block, block), 0)
    cols = lax.broadcasted_iota(jnp.int32, (block, block), 1)
    upto = jnp.where(rows <= cols, 1.0, 0.0).astype(BF16)
    numbers = lax.broadcasted_iota(jnp.int32, (buckets, block), 0)
    hots = [numbers == bucket[:, b * block : (b + 1) * block] for b in range(edges // block)]
    counts = nn(jnp.concatenate([hot.astype(F32).astype(BF16) for hot in hots], axis=0), upto)
    carry = jnp.zeros((buckets, 1), F32)
    slots = []
    for b, hot in enumerate(hots):
        here = bucket[:, b * block : (b + 1) * block]
        within = counts[b * buckets : (b + 1) * buckets, :] + carry
        rank = jnp.sum(jnp.where(hot, within - 1.0, 0.0), axis=0, keepdims=True).astype(jnp.int32)
        carry = within[:, block - 1 : block]
        at = jnp.where(jnp.bitwise_and(here, 1) == 0, rank, CAP - 1 - rank)
        side = jnp.bitwise_and(jnp.bitwise_and(here, 2) + jnp.right_shift(at, 5) + turn, 3)
        place = jnp.right_shift(here, 2) * H + side * SIDE + jnp.bitwise_and(at, SIDE - 1)
        slots.append(jnp.where((here >= 0) & (rank < CAP), place, -1))
    both = carry + jnp.concatenate([carry[1:, :], carry[:1, :]], axis=0)
    first_of_two = jnp.bitwise_and(lax.broadcasted_iota(jnp.int32, (buckets, 1), 0), 1) == 0
    worst = jnp.max(jnp.where(first_of_two, both, 0.0), axis=0, keepdims=True)
    flag = jnp.where(worst > CAP, 1.0, 0.0)
    slot = jnp.concatenate(slots, axis=1)
    slot_ref[...] = slot

    data_ref[16:32, :] = jnp.zeros((16, edges), F32)
    data_ref[0:16, :] = feats_ref[...].astype(F32)
    source = source_ref[...]
    data_ref[16:17, :] = jnp.right_shift(source, 6).astype(F32)
    data_ref[17:18, :] = jnp.bitwise_and(source, 63).astype(F32)
    data_ref[18:19, :] = (local + 1).astype(F32)
    data = data_ref[...].astype(BF16)

    tags = []
    for t in range(own // H):
        label = label_ref[:, t * H : (t + 1) * H]
        tags += [jnp.right_shift(label, 6).astype(F32), jnp.bitwise_and(label, 63).astype(F32)]
    tags.append(jnp.broadcast_to(flag, (1, H)))
    tags.append(jnp.zeros((16 - 3 * blocks - len(tags), H), F32))
    high, low = slot_hots(slot, holders * blocks)
    together = min(4, holders)
    for s0 in range(0, holders, together):
        part = high[s0 * blocks : (s0 + together) * blocks, :]
        spread = (part[:, None, :] * data[None, :, :]).reshape(together * blocks * 32, edges)
        moved = nt(spread, low)
        for n in range(together):
            out = out_ref.at[s0 + n]
            out[0:own, :] = states_ref[...]
            ids = []
            for q in range(blocks):
                at = (n * blocks + q) * 32
                out[own + 16 * q : own + 16 * (q + 1), :] = moved[at : at + 16, :].astype(BF16)
                ids.append(moved[at + 16 : at + 19, :])
            out[own + 16 * blocks : own + 16 * blocks + 16, :] = jnp.concatenate(ids + tags, axis=0).astype(BF16)


def swap_rows(outer, inner, flip=None):
    n = outer * inner
    rows = lax.broadcasted_iota(jnp.int32, (n, n), 0)
    cols = lax.broadcasted_iota(jnp.int32, (n, n), 1)
    number = jnp.bitwise_and(rows, inner - 1)
    if flip is not None:
        number = jnp.bitwise_xor(number, flip)
    source = number * outer + jnp.right_shift(rows, inner.bit_length() - 1)
    return jnp.where(source == cols, 1.0, 0.0).astype(BF16)


def split_kernel(w_ref, out_ref, order_ref):
    @pl.when(pl.program_id(0) == 0)
    def _():
        order_ref[...] = swap_rows(16, 16)

    order = order_ref[...]
    for ib in range(0, H, 32):
        sides = []
        for half in range(2):
            rows = [w_ref[:, (ib + 16 * half + i) * H : (ib + 16 * half + i + 1) * H] for i in range(16)]
            sides.append(jnp.concatenate(rows, axis=0))
        moved = nn(order, jnp.concatenate(sides, axis=1)).astype(BF16)
        for half in range(2):
            at = ib + 16 * half
            out_ref[:, at : at + 16, :] = moved[:, half * H : (half + 1) * H].reshape(16, 16, H)


def front_kernel(shape, chunks, *refs):
    holders, own, groups = shape
    blocks = groups // 2
    refs = list(refs)
    take = lambda n: [refs.pop(0) for _ in range(n)]
    piece_ref, given, states_ref, own_label_ref, t_in, b2_ref, w1_ref, b1_ref, wi_ref, wh_ref, bi_ref, bh_ref, cot_ref = take(13)
    new_ref, direct_ref, d_ref, crossed_ref, lat_out, near_out, meta_out = take(7)
    outs = take(sum(len(chunk.heads) for chunk in chunks) + 1)
    table_ref, p_ref, sum_ref, small_ref, dt_ref, rows_ref, bias_ref, extra_ref, t_ref, lat_ref, near_ref, meta_ref = take(12)
    built = take(len(outs))
    (sems,) = refs
    waiting = []

    def copy(source, target):
        moving = pltpu.make_async_copy(source, target, sems.at[len(waiting)])
        moving.start()
        waiting.append(moving)
        return moving

    t_copy = copy(t_in, t_ref)

    nodes = holders * own
    lanes = holders * SIDE
    ident = eye(H)
    tags_at = own + 16 * blocks

    flag = jnp.zeros((1, 1), F32)
    for s in range(holders):
        tags = given[s, tags_at : tags_at + 16, :].astype(F32)
        flag = jnp.maximum(flag, tags[3 * blocks + 2 * (own // H) : 3 * blocks + 2 * (own // H) + 1, 0:1])
        for t in range(own // H):
            at = s * own + t * H
            table_ref[0:H, at : at + H] = nt(ident, given[s, t * H : (t + 1) * H, :]).astype(BF16)
            both = tags[3 * blocks + 2 * t : 3 * blocks + 2 * t + 2, :]
            table_ref[H : H + 16, at : at + H] = jnp.concatenate([both, jnp.zeros((14, H), F32)], axis=0).astype(BF16)
    for t in range(own // H):
        label = own_label_ref[:, t * H : (t + 1) * H]
        label = jnp.concatenate([jnp.right_shift(label, 6), jnp.bitwise_and(label, 63)], axis=0).astype(F32)
        cols = nt(ident, jnp.concatenate([label, jnp.zeros((14, H), F32)], axis=0).astype(BF16))
        small_ref[t * H : (t + 1) * H, 0:1] = cols[:, 0:1] * 64.0 + cols[:, 1:2]

    side = lax.broadcasted_iota(jnp.int32, (24, H), 1) // SIDE
    crossing = jnp.zeros((1, H), F32)
    for q in range(blocks):
        for s in range(0, holders, 4):
            parts = []
            for n in range(4):
                feats = given[s + n, own + 16 * q : own + 16 * (q + 1), :].astype(F32)
                ids = given[s + n, tags_at : tags_at + 16, :].astype(F32)[3 * q : 3 * q + 3, :]
                parts.append(jnp.concatenate([feats, ids, jnp.zeros((5, H), F32)], axis=0))
            at = slice(s // 4 * H, (s // 4 + 1) * H)
            for u in range(4):
                page = parts[(3 - u) % 4]
                for c in range(3):
                    page = jnp.where(side == c, parts[(c - u) % 4], page)
                meta_ref[4 * q + u, 0:24, at] = page
                low = float((4 * q + u) * SUB)
                node = page[18:19, :] - 1.0
                outside = (node >= 0.0) & ((node < low) | (node >= low + SUB))
                crossing = jnp.maximum(crossing, jnp.where(outside, 1.0, 0.0))
    crossed = jnp.max(crossing) > 0.0
    crossed_ref[0] = crossed.astype(jnp.int32)

    w1 = nt(ident, w1_ref[...]).astype(BF16)
    b1 = nt(ident, jnp.broadcast_to(b1_ref[...].astype(F32), (16, H)).astype(BF16))[:, 0:1]

    def both_pages(ref, g, rows):
        return jnp.concatenate([ref[2 * g + n, rows, :] for n in range(2)], axis=1)

    def group_step(usual, g, unused):
        data = both_pages(meta_ref, g, slice(0, 24))
        source = (data[16:17, :] * 64.0 + data[17:18, :]).astype(jnp.int32)
        picked = jnp.zeros((H + 16, 2 * lanes), F32)
        for c in range(0, nodes, 256):
            picked = picked + nn(table_ref[:, c : c + 256], one_hot_rows(source - c, 256))
        near = picked[0:H, :].astype(BF16)
        label = picked[H : H + 1, :] * 64.0 + picked[H + 1 : H + 2, :]
        inside = data[18:19, :] - 1.0 - (g * GROUP).astype(F32)
        numbers = lax.broadcasted_iota(jnp.int32, (GROUP, 2 * lanes), 0).astype(F32)
        own_label = small_ref[pl.ds(pl.multiple_of(g * GROUP, GROUP), GROUP), 0:1]
        member = jnp.where((numbers == inside) & (own_label == label), 1.0, 0.0)
        before = nn(w1, data[0:16, :].astype(BF16)) + b1
        latent = before / (1.0 + jnp.exp(-before))
        made = []
        for n in range(2):
            page = slice(n * lanes, (n + 1) * lanes)
            meta_ref[2 * g + n, 24:25, :] = source[:, page].astype(F32)
            meta_ref[2 * g + n, 32 : 32 + GROUP, :] = member[:, page]
            lat_ref[2 * g + n] = latent[:, page].astype(BF16)
            near_ref[2 * g + n] = near[:, page]
            mine = member[n * SUB : (n + 1) * SUB, :]
            if usual:
                units, states, mine = latent[:, page], near[:, page], mine[:, page]
            else:
                units, states = latent, near
            spread = (units[:, None, :] * mine[None, :, :]).reshape(H * SUB, -1).astype(BF16)
            made.append(nt(spread, states).reshape(H, SUB, H))
        at = pl.ds(pl.multiple_of(g * GROUP, GROUP), GROUP)
        p_ref[:, at, :] = jnp.concatenate(made, axis=1).astype(BF16)
        sum_ref[at, :] = nt(member.astype(BF16), near)
        return unused

    @pl.when(jnp.logical_not(crossed))
    def _():
        lax.fori_loop(0, groups, functools.partial(group_step, True), 0, unroll=UNROLL)

    @pl.when(crossed)
    def _():
        lax.fori_loop(0, groups, functools.partial(group_step, False), 0)

    copy(lat_ref, lat_out)
    copy(near_ref, near_out)
    copy(meta_ref, meta_out)

    def agg_step(n, total):
        left = jnp.concatenate([p_ref[n * AGG + m] for m in range(AGG)], axis=1)
        right = jnp.concatenate([t_ref[n * AGG + m] for m in range(AGG)], axis=1)
        return total + nt(left, right)

    total = nt(sum_ref[...].astype(BF16), b2_ref[...])
    t_copy.wait()
    total = lax.fori_loop(0, H // AGG, agg_step, total)

    mixed = total.astype(BF16)
    prior = states_ref[...]
    prior_f = prior.astype(F32)
    cot = cot_ref[...].astype(F32)
    wi, wh = wi_ref[...], wh_ref[...]
    gi = nn(mixed, wi) + bi_ref[...]
    gh = nn(prior, wh) + bh_ref[...]
    r = jax.nn.sigmoid(gi[:, 0:H] + gh[:, 0:H])
    u = jax.nn.sigmoid(gi[:, H : 2 * H] + gh[:, H : 2 * H])
    n = jnp.tanh(gi[:, 2 * H :] + r * gh[:, 2 * H :])
    new_ref[...] = ((1.0 - u) * n + u * prior_f).astype(BF16)
    d_pre = (1.0 - u) * cot * (1.0 - n * n)
    d_r = d_pre * gh[:, 2 * H :] * r * (1.0 - r)
    d_u = (prior_f - n) * cot * u * (1.0 - u)
    d_gi = jnp.concatenate([d_r, d_u, d_pre], axis=1)
    d_gh = jnp.concatenate([d_r, d_u, d_pre * r], axis=1)

    def halves(x):
        high = x.astype(BF16)
        return high, (x - high.astype(F32)).astype(BF16)

    def twice(x):
        return jnp.concatenate([x, x], axis=1)

    gi_high, gi_low = halves(d_gi)
    gh_high, gh_low = halves(d_gh)
    d_agg = nt(jnp.concatenate([gi_high, gi_low], axis=1), twice(wi)).astype(BF16)
    d_ref[...] = d_agg
    dt_ref[...] = nt(ident, d_agg).astype(BF16)
    direct_ref[...] = u * cot + nt(jnp.concatenate([gh_high, gh_low], axis=1), twice(wh))

    piece_me = piece_ref[0]
    joint = built[-1]

    def dest(c, rel):
        place = chunks[c].place(rel)
        if rel >= PIECES // 2:
            return joint, place, chunks[c].offset
        before = sum(len(chunk.heads) for chunk in chunks[:c])
        for n, head in enumerate(chunks[c].heads):
            count = PIECES // 2 >> len(head)
            if place < count:
                return built[before + n], place, 0
            place -= count

    mixed_t = nt(ident, mixed).astype(BF16)
    prior_t = nt(ident, prior).astype(BF16)
    from_input = nn(twice(mixed_t), jnp.concatenate([gi_high, gi_low], axis=0))
    from_state = nn(twice(prior_t), jnp.concatenate([gh_high, gh_low], axis=0))
    for t in range(3):
        rows_ref[t, 0:H, :] = from_input[:, t * H : (t + 1) * H]
        rows_ref[3 + t, 0:H, :] = from_state[:, t * H : (t + 1) * H]
    rows_ref[6, 0:H, :] = nn(dt_ref[...], sum_ref[...].astype(BF16))
    bias_ref[...] = jnp.zeros_like(bias_ref)
    for n, part in enumerate((d_gi, d_gh)):
        part = jnp.sum(part, axis=0, keepdims=True)
        for t in range(3):
            bias_ref[3 * n + t : 3 * n + t + 1, :] = part[:, t * H : (t + 1) * H]
    extra_ref[...] = jnp.zeros_like(extra_ref)
    extra_ref[29:30, :] = jnp.broadcast_to(flag, (1, H))
    last = chunks[-1]
    for rel in list(range(PIECES // 2, PIECES)) + list(range(PIECES // 2)):
        p = jnp.bitwise_xor(piece_me, rel)
        for t in range(7):
            extra_ref[UNITS * t : UNITS * (t + 1), :] = rows_ref[t, pl.ds(p * UNITS, UNITS), :]
        extra_ref[28:29, :] = bias_ref[pl.ds(p, 1), :]
        ref, place, offset = dest(len(chunks) - 1, rel)
        ref[place, offset + UNITS * last.rows : offset + last.height, :] = extra_ref[...].astype(BF16)

    for rel in list(range(PIECES // 2, PIECES)) + list(range(PIECES // 2)):
        k0 = jnp.bitwise_xor(piece_me, rel) * UNITS
        for m in range(0, UNITS, 2):
            out = nn(dt_ref[...], jnp.concatenate([p_ref[k0 + m], p_ref[k0 + m + 1]], axis=1)).astype(BF16)
            for c, chunk in enumerate(chunks):
                ref, place, offset = dest(c, rel)
                for h in range(2):
                    start = offset + (m + h) * chunk.rows
                    ref[place, start : start + chunk.rows, :] = out[
                        chunk.first : chunk.first + chunk.rows, h * H : (h + 1) * H
                    ]
        if rel == PIECES - 1:
            copy(joint, outs[-1])
    for n in range(len(built) - 1):
        copy(built[n], outs[n])
    for moving in waiting[1:]:
        moving.wait()


def spread_kernel(shape, d_ref, t_ref, b2_ref, wide_ref, bias_ref, dp_ref, order_ref):
    holders, own, groups = shape
    d = d_ref[...]

    @pl.when(pl.program_id(0) == 0)
    def _():
        bias_ref[...] = nn(d, b2_ref[...])
        order_ref[...] = swap_rows(16, 16)

    order = order_ref[...]
    for n in range(0, t_ref.shape[0], 2):
        out = nn(d, jnp.concatenate([t_ref[n], t_ref[n + 1]], axis=1)).astype(BF16)
        dp_ref[n] = out[:, :H]
        dp_ref[n + 1] = out[:, H:]
    for k in range(0, t_ref.shape[0], 16):
        for g in range(0, groups, 2):
            sides = [dp_ref[k : k + 16, (g + n) * GROUP : (g + n + 1) * GROUP, :].reshape(256, H) for n in range(2)]
            moved = nn(order, jnp.concatenate(sides, axis=1)).astype(BF16)
            for n in range(2):
                for v in range(GROUP):
                    wide_ref[g + n, k : k + 16, v * H : (v + 1) * H] = moved[v * 16 : (v + 1) * 16, n * H : (n + 1) * H]


def back_kernel(shape, masks, me_ref, *refs):
    holders, own, groups = shape
    blocks = groups // 2
    crossed_ref, wide_in, bias_ref, w1_ref, b1_ref, lat_in, near_in, meta_in = refs[:8]
    keep_d, keep_e, send_ref, first_ref = refs[8:12]
    part_ref, edge_ref, sum_ref, slab_ref, wide_ref, lat_ref, near_ref, meta_ref, sems = refs[12:]

    def coming(g):
        pages = pl.ds(2 * g, 2)
        return [
            pltpu.make_async_copy(wide_in.at[g], wide_ref.at[g], sems.at[0, g]),
            pltpu.make_async_copy(lat_in.at[pages], lat_ref.at[pages], sems.at[1, g]),
            pltpu.make_async_copy(near_in.at[pages], near_ref.at[pages], sems.at[2, g]),
            pltpu.make_async_copy(meta_in.at[pages], meta_ref.at[pages], sems.at[3, g]),
        ]

    for g in range(groups):
        for copy in coming(g):
            copy.start()
    nodes = holders * own
    lanes = holders * SIDE
    ident = eye(H)
    part_ref[...] = jnp.zeros_like(part_ref)
    w1n = w1_ref[...]
    w1 = nt(ident, w1n).astype(BF16)
    b1 = nt(ident, jnp.broadcast_to(b1_ref[...].astype(F32), (16, H)).astype(BF16))[:, 0:1]
    one_row = jnp.where(lax.broadcasted_iota(jnp.int32, (16, 2 * lanes), 0) == 0, 1.0, 0.0).astype(BF16)

    def both_pages(ref, g, rows):
        return jnp.concatenate([ref[2 * g + n, rows, :] for n in range(2)], axis=1)

    def group_step(usual, g, first_total):
        for copy in coming(g):
            copy.wait()
        wide = wide_ref[g]
        wide_t = jnp.concatenate([wide[:, v * H : (v + 1) * H].T for v in range(GROUP)], axis=1)
        bias_rows = bias_ref[pl.ds(pl.multiple_of(g * GROUP, GROUP), GROUP), :].astype(BF16)
        bias_t = nt(ident, bias_rows).astype(BF16)
        data = both_pages(meta_ref, g, slice(0, 16)).astype(BF16)
        source = both_pages(meta_ref, g, slice(24, 25)).astype(jnp.int32)
        member = both_pages(meta_ref, g, slice(32, 32 + GROUP)).astype(BF16)
        d_latent, d_near = [], []
        for n in range(2):
            low, number = (n * SUB, SUB) if usual else (0, GROUP)
            mine = meta_ref[2 * g + n, 32 + low : 32 + low + number, :].astype(BF16)
            part = slice(low * H, (low + number) * H)
            spread = (near_ref[2 * g + n][None, :, :] * mine[:, None, :]).reshape(number * H, lanes)
            d_latent.append(nn(wide[:, part], spread))
            spread = (lat_ref[2 * g + n][None, :, :] * mine[:, None, :]).reshape(number * H, lanes)
            d_near.append(nn(wide_t[:, part], spread))
        d_latent = jnp.concatenate(d_latent, axis=1)
        d_near = (jnp.concatenate(d_near, axis=1) + nn(bias_t, member)).astype(BF16)
        for c in range(0, nodes, 256):
            part_ref[c : c + 256, :] += nt(one_hot_rows(source - c, 256), d_near)
        before = nn(w1, data) + b1
        gate = 1.0 / (1.0 + jnp.exp(-before))
        d_before = (d_latent * gate * (1.0 + before * (1.0 - gate))).astype(BF16)
        edges = nn(w1n, d_before)
        for n in range(2):
            edge_ref[2 * g + n] = edges[:, n * lanes : (n + 1) * lanes]
        return first_total + nt(jnp.concatenate([data, one_row], axis=0), d_before)

    none = jnp.zeros((32, H), F32)

    @pl.when(crossed_ref[0] == 0)
    def _():
        sum_ref[...] = lax.fori_loop(0, groups, functools.partial(group_step, True), none, unroll=BACK_UNROLL)

    @pl.when(crossed_ref[0] != 0)
    def _():
        sum_ref[...] = lax.fori_loop(0, groups, functools.partial(group_step, False), none)

    first = sum_ref[...].astype(BF16)
    first_ref[...] = first
    half = holders // 2
    side = lax.broadcasted_iota(jnp.int32, (16, H), 1) // SIDE
    for q in range(blocks):
        for s in range(holders):
            at = slice(s // 4 * H, (s // 4 + 1) * H)
            parts = [edge_ref[4 * q + u, :, at] for u in range(4)]
            page = parts[(3 - s) % 4]
            for c in range(3):
                page = jnp.where(side == c, parts[(c - s) % 4], page)
            slab_ref[s, 16 * q : 16 * (q + 1), :] = page.astype(BF16)
    for n in range(holders):
        rel = sum(mask for i, mask in enumerate(reversed(masks)) if n >> i & 1)
        h = jnp.bitwise_xor(me_ref[0], rel)
        rows = part_ref[pl.ds(pl.multiple_of(h * own, own), own), :].astype(BF16)
        if n < half:
            keep_d[n] = rows
            keep_e[n] = slab_ref[h]
        else:
            send_ref[(n - half) * own : (n - half + 1) * own, :] = rows
            at = half * own + (n - half) * 16 * blocks
            send_ref[at : at + 16 * blocks, :] = slab_ref[h]


def gather_kernel(shape, sources, me_ref, slot_ref, direct_ref, part_ref, slabs_ref, state_ref, edge_ref, data_ref):
    holders, own, groups = shape
    blocks = groups // 2
    state_ref[...] = direct_ref[...] + part_ref[...].astype(F32)
    for n, rel in enumerate(sources):
        h = jnp.bitwise_xor(me_ref[0], rel)
        data_ref[pl.ds(pl.multiple_of(h * 16 * blocks, 16), 16 * blocks), :] = slabs_ref[n]
    edges = slot_ref.shape[1]
    data = data_ref[...]
    count = holders * blocks
    block = 512
    for b in range(edges // block):
        high, low = slot_hots(slot_ref[:, b * block : (b + 1) * block], count)
        high = high.astype(F32)
        found = nn(data, low)
        total = jnp.zeros((16, block), F32)
        for n in range(count):
            total = total + found[16 * n : 16 * (n + 1), :] * high[n : n + 1, :]
        edge_ref[:, b * block : (b + 1) * block] = total


class Chunk:
    def __init__(self, first, rows, extra, steps, offset):
        self.first, self.rows, self.extra, self.steps, self.offset = first, rows, extra, steps, offset
        self.height = UNITS * rows + extra
        self.order = sum(steps, ())
        ways = [(n,) for n in range(2)] if len(steps[0]) == 1 else [(n, m) for n in range(2) for m in range(2)]
        self.heads = [(0, 0), (0, 1), (1,)] if len(steps[0]) == 1 else ways

    def place(self, rel):
        at = 0
        for bit in self.order:
            at = at * 2 + (rel >> bit & 1)
        return at

    def shape(self):
        return (2,) * len(self.order) + (self.height, H)

    def partners(self, step, bits):
        group = self.steps[step]
        found = []
        for n in range(1, 2 ** len(group)):
            path = tuple(n >> (len(group) - 1 - i) & 1 for i in range(len(group)))
            found.append((path, sum(bits[bit] for bit, on in zip(group, path) if on)))
        return found


def plan(batch, edge):
    core, x = [edge], [edge << n for n in range(1, batch.bit_length() - 1)]
    z = [2 << n for n in reversed(range(3 - len(x)))]
    bits = z + [1] + x + core
    chunks, offset = [], 0
    for first, rows, extra, steps in CHUNKS:
        chunks.append(Chunk(first, rows, extra, steps, offset))
        offset += chunks[-1].height
    device = lax.axis_index(("batch", "edge")).astype(jnp.int32)
    piece = sum(jnp.where(device & mask != 0, 1 << n, 0) for n, mask in enumerate(bits))
    return bits, chunks, piece.astype(jnp.int32).reshape(1)


def swap(x, mask, devices):
    return lax.ppermute(x, ("batch", "edge"), [(i, i ^ mask) for i in range(devices)])


def add(terms):
    total = terms[0].astype(F32)
    for term in terms[1:]:
        total = total + term.astype(F32)
    return total.astype(BF16)


def rounded(x):
    return lax.reduce_precision(x.astype(F32), 8, 7).astype(BF16)


def jobs_of(chunks, arrived, cores):
    found = []
    for core in cores:
        for c, chunk in enumerate(chunks):
            last, beside = chunk.order[:2]
            for n in range(2):
                found.append((c, core, core * PIECES // 2 + (arrived << last) + (n << beside), 4 * n))
    return found


def unpack(chunks, jobs, me, order_ref, sources, block_refs, w_out, rows_ref, sems, beside=lambda: None):
    width = 4 * UNITS
    coming, leaving = [], []
    for n, (c, core, rel, place) in enumerate(jobs):
        coming.append(pltpu.make_async_copy(sources[n].at[pl.ds(place, 4)], block_refs[n], sems.at[n]))
        rows = pl.ds(pl.multiple_of(jnp.bitwise_xor(jnp.right_shift(me, 2), rel // 4) * width, width), width)
        lanes = pl.ds(chunks[c].first * H, chunks[c].rows * H)
        leaving.append(pltpu.make_async_copy(rows_ref.at[n % 3], w_out.at[rows, lanes], sems.at[len(jobs) + n]))
    for copy in coming:
        copy.start()
    order_ref[...] = swap_rows(32, 2 * UNITS, jnp.bitwise_and(me, 1) * UNITS)
    beside()
    for n, (c, core, rel, place) in enumerate(jobs):
        coming[n].wait()
        if n >= 3:
            leaving[n - 3].wait()
        rows = chunks[c].rows
        for pair in range(2):
            upper = jnp.bitwise_xor(jnp.bitwise_and(jnp.right_shift(me, 1), 1), pair)
            at_rows = pl.ds(pl.multiple_of(upper * 2 * UNITS, 2 * UNITS), 2 * UNITS)
            for ib in range(0, rows, 64):
                sides = []
                for at in (ib, ib + 32):
                    parts = [
                        block_refs[n][2 * pair + i, m * rows + at : m * rows + at + 32, :]
                        for i in range(2)
                        for m in range(UNITS)
                    ]
                    sides.append(jnp.concatenate(parts, axis=0))
                moved = nn(order_ref[...], jnp.concatenate(sides, axis=1))
                for side in range(2):
                    for i in range(32):
                        at = (ib + 32 * side + i) * H
                        rows_ref[n % 3, at_rows, at : at + H] = moved[8 * i : 8 * (i + 1), side * H : (side + 1) * H]
        leaving[n].start()

    def end():
        for copy in leaving[-3:]:
            copy.wait()

    return end


def small_piece(me, rel, extra, extra_ref, bias_ref):
    p = jnp.bitwise_xor(me, rel)
    extra = extra.astype(F32)
    for t in range(7):
        extra_ref[t, pl.ds(p * UNITS, UNITS), :] = extra[UNITS * t : UNITS * (t + 1), :]
    bias_ref[pl.ds(p, 1), :] = extra[28:29, :]


def small_pieces(chunks, jobs, me, block_refs, extra_ref, bias_ref):
    start = UNITS * chunks[-1].rows
    for n, (c, core, rel, place) in enumerate(jobs):
        if c == len(chunks) - 1:
            for i in range(4):
                small_piece(me, rel + i, block_refs[n][i, start : start + EXTRA, :], extra_ref, bias_ref)


def early_kernel(chunks, piece_ref, *refs):
    count = len(chunks)
    jobs = jobs_of(chunks, 0, (0, 1))
    sources = [refs[core * count + c] for c, core, rel, place in jobs]
    w_out, extra_ref, bias_ref = refs[2 * count : 2 * count + 3]
    block_refs, (rows_ref, order_ref, sems) = refs[2 * count + 3 : -3], refs[-3:]
    me = piece_ref[0]
    extra_ref[...] = jnp.zeros_like(extra_ref)
    bias_ref[...] = jnp.zeros_like(bias_ref)
    end = unpack(chunks, jobs, me, order_ref, sources, block_refs, w_out, rows_ref, sems)
    small_pieces(chunks, jobs, me, block_refs, extra_ref, bias_ref)
    end()


def late_kernel(chunks, piece_ref, *refs):
    count = len(chunks)
    jobs = jobs_of(chunks, 1, (0,))
    sources = [refs[c] for c, core, rel, place in jobs]
    w_in, w_out = refs[count : count + 2]
    block_refs, (rows_ref, order_ref, sems) = refs[count + 2 : -3], refs[-3:]
    unpack(chunks, jobs, piece_ref[0], order_ref, sources, block_refs, w_out, rows_ref, sems)()


def last_kernel(chunks, piece_ref, *refs):
    count = len(chunks)
    jobs = jobs_of(chunks, 1, (1,))
    sources = [refs[c] for c, core, rel, place in jobs]
    own_last, first_ref, extra_in, bias_in, w_in = refs[count : count + 5]
    w_out, w1_ref, b1_ref, wi_ref, wh_ref, b2_ref, bi_ref, bh_ref = refs[count + 5 : count + 13]
    block_refs, (rows_ref, order_ref, small_ref, extra_ref, bias_ref, sems) = refs[count + 13 : -6], refs[-6:]
    me = piece_ref[0]
    start = UNITS * chunks[-1].rows
    small = pltpu.make_async_copy(own_last.at[:, start : start + EXTRA, :], small_ref, sems.at[2 * len(jobs)])

    def beside():
        small.start()
        w1_ref[...] = first_ref[0:16, :].astype(F32)
        b1_ref[...] = first_ref[16:32, :].astype(F32)[0:1, :].reshape(H)
        extra_ref[...] = extra_in[...]
        bias_ref[...] = bias_in[...]

    end = unpack(chunks, jobs, me, order_ref, sources, block_refs, w_out, rows_ref, sems, beside)
    small_pieces(chunks, jobs, me, block_refs, extra_ref, bias_ref)
    small.wait()
    for c, core, rel, place in jobs_of(chunks, 1, (0,)):
        if c == count - 1:
            for i in range(4):
                small_piece(me, rel + i, small_ref[place + i], extra_ref, bias_ref)
    for t in range(3):
        wi_ref[:, t * H : (t + 1) * H] = extra_ref[t, 0:H, :]
        wh_ref[:, t * H : (t + 1) * H] = extra_ref[3 + t, 0:H, :]
        bi_ref[t * H : (t + 1) * H] = bias_ref[t : t + 1, :].reshape(H)
        bh_ref[t * H : (t + 1) * H] = bias_ref[3 + t : 4 + t, :].reshape(H)
    b2_ref[...] = extra_ref[6, 0:H, :]
    end()


def unpack_scratch(chunks, jobs, more=()):
    return (
        [pltpu.VMEM((4, chunks[c].height, H), BF16) for c, core, rel, place in jobs]
        + [pltpu.VMEM((3, 4 * UNITS, max(chunk.rows for chunk in chunks) * H), F32), pltpu.VMEM((256, 256), BF16)]
        + list(more)
        + [pltpu.SemaphoreType.DMA((2 * len(jobs) + 1,))]
    )


W_SHAPE = jax.ShapeDtypeStruct((H, H * H), F32)
SMALL = [jax.ShapeDtypeStruct((7, H + 8, H), F32), jax.ShapeDtypeStruct((PIECES + 8, H), F32)]


def early_half(chunks, bits, devices, piece_arr, parts):
    parts = [x.reshape(PIECES // 4, chunk.height, H) for x, chunk in zip(parts, chunks)]
    others = [swap(x, bits[-1], devices) for x in parts]
    return pl.pallas_call(
        functools.partial(early_kernel, chunks),
        name="assemble_early",
        in_specs=[smem()] + [anywhere()] * (2 * len(chunks)),
        out_specs=[anywhere(), vmem(), vmem()],
        scratch_shapes=unpack_scratch(chunks, jobs_of(chunks, 0, (0, 1))),
        out_shape=[W_SHAPE] + SMALL,
        compiler_params=params(),
        cost_estimate=cost(6),
    )(piece_arr, *parts, *others)


def vmem():
    return pl.BlockSpec(memory_space=pltpu.VMEM)


def anywhere():
    return pl.BlockSpec(memory_space=pl.ANY)


def smem():
    return pl.BlockSpec(memory_space=pltpu.SMEM)


def cost(us):
    return pl.CostEstimate(flops=int(us * COST * 1e9), bytes_accessed=int(us * COST * 3e6), transcendentals=0)


def params():
    return pltpu.CompilerParams(vmem_limit_bytes=VMEM_LIMIT)


def fast_path(batch, edge, args):
    (states, edge_feats, molecule, source, target, edge_mask, w_edge_in, b_edge_in, w_edge_out, b_edge_out,
     w_input, w_hidden, b_input, b_hidden, cotangent) = args
    devices = batch * edge
    states_here = states[0]
    own = states_here.shape[0]
    edges = source.shape[1]
    holders, groups = edge, own // GROUP
    shape = (holders, own, groups)
    blocks = groups // 2
    bits, chunks, piece_arr = plan(batch, edge)
    rest = [m for m in (1 << n for n in range(devices.bit_length() - 1)) if m not in bits]
    me_arr = lax.axis_index("edge").astype(jnp.int32).reshape(1)
    lanes = holders * SIDE
    pages = 2 * groups

    slots_out, slot = pl.pallas_call(
        functools.partial(sort_kernel, shape),
        name="edges_to_slots",
        out_shape=[
            jax.ShapeDtypeStruct((holders, own + 16 * blocks + 16, H), BF16),
            jax.ShapeDtypeStruct((1, edges), jnp.int32),
        ],
        in_specs=[smem()] + [vmem()] * 6,
        out_specs=[vmem()] * 2,
        scratch_shapes=[pltpu.VMEM((32, edges), F32)],
        compiler_params=params(),
    )(me_arr, target, source, edge_mask, molecule, jnp.swapaxes(edge_feats, 1, 2)[0], states_here)
    given = lax.all_to_all(slots_out, "edge", 0, 0)

    t_units = pl.pallas_call(
        split_kernel,
        name="split_weight",
        grid=(H // 16,),
        in_specs=[pl.BlockSpec((16, H * H), lambda i: (i, 0))],
        out_specs=pl.BlockSpec((16, H, H), lambda i: (i, 0, 0)),
        out_shape=jax.ShapeDtypeStruct((H, H, H), BF16),
        scratch_shapes=[pltpu.VMEM((256, 256), BF16)],
        compiler_params=params(),
        cost_estimate=cost(6),
    )(w_edge_out)
    b2 = b_edge_out.reshape(H, H)
    b1 = b_edge_in.reshape(1, H)
    built = [jax.ShapeDtypeStruct((PIECES // 2 >> len(h), c.height, H), BF16) for c in chunks for h in c.heads]
    built.append(jax.ShapeDtypeStruct((PIECES // 2, sum(c.height for c in chunks), H), BF16))
    front = pl.pallas_call(
        functools.partial(front_kernel, shape, chunks),
        name="messages_update_weight_gradient",
        out_shape=[
            jax.ShapeDtypeStruct((own, H), BF16),
            jax.ShapeDtypeStruct((own, H), F32),
            jax.ShapeDtypeStruct((own, H), BF16),
            jax.ShapeDtypeStruct((1,), jnp.int32),
            jax.ShapeDtypeStruct((pages, H, lanes), BF16),
            jax.ShapeDtypeStruct((pages, H, lanes), BF16),
            jax.ShapeDtypeStruct((pages, 32 + GROUP, lanes), F32),
        ]
        + built,
        in_specs=[smem()] + [vmem()] * 3 + [anywhere()] + [vmem()] * 8,
        out_specs=[vmem()] * 3 + [smem()] + [anywhere()] * (3 + len(built)),
        scratch_shapes=[
            pltpu.VMEM((H + 16, holders * own), BF16),
            pltpu.VMEM((H, own, H), BF16),
            pltpu.VMEM((own, H), F32),
            pltpu.VMEM((own, H), F32),
            pltpu.VMEM((H, own), BF16),
            pltpu.VMEM((7, H + 8, H), F32),
            pltpu.VMEM((PIECES + 8, H), F32),
            pltpu.VMEM((EXTRA, H), F32),
            pltpu.VMEM((H, H, H), BF16),
            pltpu.VMEM((pages, H, lanes), BF16),
            pltpu.VMEM((pages, H, lanes), BF16),
            pltpu.VMEM((pages, 32 + GROUP, lanes), F32),
        ]
        + [pltpu.VMEM(h.shape, BF16) for h in built]
        + [pltpu.SemaphoreType.DMA((4 + len(built),))],
        compiler_params=params(),
    )(
        piece_arr, given, states_here, molecule, t_units, b2, w_edge_in, b1, w_input, w_hidden,
        b_input.astype(F32).reshape(1, -1), b_hidden.astype(F32).reshape(1, -1), cotangent[0],
    )
    new_states, direct, d_agg, crossed, latent, near, meta = front[:7]
    built = front[7:]

    matrix_gradients = pl.pallas_call(
        functools.partial(spread_kernel, shape),
        name="matrix_gradients",
        out_shape=[jax.ShapeDtypeStruct((groups, H, GROUP * H), BF16), jax.ShapeDtypeStruct((own, H), F32)],
        grid=(H // KSTEP,),
        in_specs=[
            pl.BlockSpec((own, H), lambda i: (0, 0)),
            pl.BlockSpec((KSTEP, H, H), lambda i: (i, 0, 0)),
            pl.BlockSpec((H, H), lambda i: (0, 0)),
        ],
        out_specs=[
            pl.BlockSpec((groups, KSTEP, GROUP * H), lambda i: (0, i, 0)),
            pl.BlockSpec((own, H), lambda i: (0, 0)),
        ],
        scratch_shapes=[pltpu.VMEM((KSTEP, own, H), BF16), pltpu.VMEM((256, 256), BF16)],
        compiler_params=params(),
        cost_estimate=cost(6),
    )

    back_masks = [1 << n for n in range(edge.bit_length() - 1)]

    def edge_work(wide, bias):
        return pl.pallas_call(
            functools.partial(back_kernel, shape, back_masks),
            name="edge_gradients",
            out_shape=[
                jax.ShapeDtypeStruct((holders // 2, own, H), BF16),
                jax.ShapeDtypeStruct((holders // 2, 16 * blocks, H), BF16),
                jax.ShapeDtypeStruct((holders // 2 * (own + 16 * blocks), H), BF16),
                jax.ShapeDtypeStruct((32, H), BF16),
            ],
            in_specs=[smem()] * 2 + [anywhere()] + [vmem()] * 3 + [anywhere()] * 3,
            out_specs=[vmem()] * 4,
            scratch_shapes=[
                pltpu.VMEM((holders * own, H), F32),
                pltpu.VMEM((pages, 16, lanes), F32),
                pltpu.VMEM((32, H), F32),
                pltpu.VMEM((holders, 16 * blocks, H), BF16),
                pltpu.VMEM((groups, H, GROUP * H), BF16),
                pltpu.VMEM((pages, H, lanes), BF16),
                pltpu.VMEM((pages, H, lanes), BF16),
                pltpu.VMEM((pages, 32 + GROUP, lanes), F32),
                pltpu.SemaphoreType.DMA((4, groups)),
            ],
            compiler_params=params(),
            cost_estimate=cost(14),
        )(me_arr, crossed, wide, bias, w_edge_in, b1, latent, near, meta)

    if MATRIX_FIRST:
        sent, d_agg = lax.optimization_barrier((built[-1], d_agg))
        other = swap(sent, bits[-1], devices)
        other, (wide, bias) = lax.optimization_barrier((other, matrix_gradients(d_agg, t_units, b2)))
    else:
        other = swap(built[-1], bits[-1], devices)
        wide, bias = matrix_gradients(d_agg, t_units, b2)
    other = other.reshape((2,) * 4 + (-1, H))
    arrays = iter(built)
    kept = [{head: next(arrays) for head in chunk.heads} for chunk in chunks]
    got = [[] for _ in chunks]

    def mine(c, path):
        for head, x in kept[c].items():
            if path[: len(head)] == head:
                return x.reshape((2,) * (4 - len(head)) + x.shape[1:])[path[len(head) :]]

    def partial_sum(c, path):
        rows = slice(chunks[c].offset, chunks[c].offset + chunks[c].height)
        parts = [mine(c, path), other[path][..., rows, :]]
        for n, arrays in enumerate(got[c]):
            done = sum(len(group) for group in chunks[c].steps[: n + 1])
            parts += [x[path[done:]] for x in arrays]
        return add(parts)

    def scatter_step(step, work=None, given=()):
        begun = []
        for c, chunk in enumerate(chunks):
            done = (0,) * sum(len(group) for group in chunk.steps[:step])
            if step < len(chunk.steps):
                begun.append([partial_sum(c, done + path) for path, mask in chunk.partners(step, bits)])
            else:
                begun.append([])
        if work is not None:
            begun, given = lax.optimization_barrier((begun, given))
        new = [
            [swap(x, mask, devices) for x, (path, mask) in zip(begun[c], chunk.partners(step, bits))] if begun[c] else []
            for c, chunk in enumerate(chunks)
        ]
        result = None
        if work is not None:
            result = work(*given)
            for c in TIED:
                new[c], result = lax.optimization_barrier((new[c], result))
        for c in range(len(chunks)):
            if new[c]:
                got[c].append(new[c])
        return result

    keep_d, keep_e, send, first = scatter_step(0, edge_work, (wide, bias))
    for n in range(edge.bit_length() - 1, devices.bit_length() - 1):
        first = rounded(first.astype(F32) + swap(first, 1 << n, devices).astype(F32))
    scatter_step(1)
    slabs, sources = keep_e[:, None], [0]

    def give_back(mask, after):
        nonlocal keep_d, slabs, sources, send, first
        if after is not None:
            send, after = lax.optimization_barrier((send, after))
        n = keep_d.shape[0]
        cut = n * own
        arrived = swap(jnp.concatenate([send, first], axis=0), mask, devices)
        keep_d = add([keep_d, arrived[:cut].reshape(n, own, H)])
        slabs = jnp.concatenate([slabs, arrived[cut:-32].reshape(n, -1, 16 * blocks, H)], axis=1)
        first = rounded(first.astype(F32) + arrived[-32:].astype(F32))
        sources = sources + [s ^ mask for s in sources]
        if n > 1:
            send = jnp.concatenate([keep_d[n // 2 :].reshape(-1, H), slabs[n // 2 :].reshape(-1, H)], axis=0)
            keep_d, slabs = keep_d[: n // 2], slabs[: n // 2]

    give_back(1, got[1][1])
    scatter_step(2)
    scatter_step(3)
    parts = [partial_sum(c, (0,) * 4) for c in range(len(chunks))]
    for mask in rest:
        parts = [rounded(x.astype(F32) + swap(x, mask, devices).astype(F32)) for x in parts]
    overflow = parts[-1][UNITS * chunks[-1].rows + 29, 0] > 0.0
    for step in (3, 2, 1):
        if step == 2:
            parts[1], overflow = lax.optimization_barrier((parts[1], overflow))
        if step == GIVE:
            for mask in back_masks[1:-1]:
                give_back(mask, parts[0] if mask == 2 else None)
        for c, chunk in enumerate(chunks):
            parts[c] = gather_step(chunk, step, bits, devices, parts[c])
    give_back(back_masks[-1], parts[LAST_GIVE])
    came = [swap(x, bits[chunk.order[0]], devices) for x, chunk in zip(parts, chunks)]
    early = early_half(chunks, bits, devices, piece_arr, parts)
    state_grads, edge_grads = pl.pallas_call(
        functools.partial(gather_kernel, shape, sources),
        name="slots_to_edges",
        out_shape=[
            jax.ShapeDtypeStruct((own, H), F32),
            jax.ShapeDtypeStruct((edge_feats.shape[2], edges), F32),
        ],
        in_specs=[smem()] + [vmem()] * 4,
        out_specs=[vmem()] * 2,
        scratch_shapes=[pltpu.VMEM((holders * 16 * blocks, H), BF16)],
        compiler_params=params(),
        cost_estimate=cost(3),
    )(me_arr, slot, direct, keep_d[0], slabs[0])
    return overflow, (new_states, state_grads, edge_grads, first, came, early)


def gather_step(chunk, step, bits, devices, x):
    partners = chunk.partners(step, bits)
    all_ = jnp.stack([x] + [swap(x, mask, devices) for path, mask in partners], axis=0)
    return all_.reshape((2,) * len(chunk.steps[step]) + x.shape)


def finish(batch, edge, results):
    new_states, state_grads, edge_grads, first, came, early = results
    bits, chunks, piece_arr = plan(batch, edge)
    devices = batch * edge
    came = [x.reshape(PIECES // 4, chunk.height, H) for x, chunk in zip(came, chunks)]
    others = [swap(x, bits[-1], devices) for x in came]
    grad_w2, extras, biases = early
    grad_w2 = pl.pallas_call(
        functools.partial(late_kernel, chunks),
        name="assemble_late",
        in_specs=[smem()] + [anywhere()] * (len(chunks) + 1),
        out_specs=anywhere(),
        scratch_shapes=unpack_scratch(chunks, jobs_of(chunks, 1, (0,))),
        out_shape=W_SHAPE,
        input_output_aliases={len(chunks) + 1: 0},
        compiler_params=params(),
        cost_estimate=cost(4),
    )(piece_arr, *came, grad_w2)
    more = [pltpu.VMEM((PIECES // 4, EXTRA, H), BF16)] + [pltpu.VMEM(x.shape, F32) for x in SMALL]
    grad_w2, grad_w1, grad_b1, grad_wi, grad_wh, grad_b2, grad_bi, grad_bh = pl.pallas_call(
        functools.partial(last_kernel, chunks),
        name="assemble_last",
        in_specs=[smem()] + [anywhere()] * (len(chunks) + 1) + [vmem()] * 3 + [anywhere()],
        out_specs=[anywhere()] + [vmem()] * 7,
        scratch_shapes=unpack_scratch(chunks, jobs_of(chunks, 1, (1,)), more),
        out_shape=[W_SHAPE, jax.ShapeDtypeStruct((16, H), F32), jax.ShapeDtypeStruct((H,), F32)]
        + [jax.ShapeDtypeStruct((H, 3 * H), F32)] * 2
        + [jax.ShapeDtypeStruct((H, H), F32)]
        + [jax.ShapeDtypeStruct((3 * H,), F32)] * 2,
        input_output_aliases={len(chunks) + 5: 0},
        compiler_params=params(),
    )(piece_arr, *others, came[-1], first, extras, biases, grad_w2)
    return (
        new_states[None],
        state_grads[None],
        jnp.swapaxes(edge_grads[None], 1, 2),
        grad_w1,
        grad_b1,
        grad_w2,
        grad_b2.reshape(-1),
        grad_wi,
        grad_wh,
        grad_bi,
        grad_bh,
    )


HIGH = lax.Precision.HIGHEST


def gated_update(mixed, prior, w_input, w_hidden, b_input, b_hidden):
    width = prior.shape[1]
    from_input = jnp.dot(mixed, w_input, precision=HIGH) + b_input
    from_state = jnp.dot(prior, w_hidden, precision=HIGH) + b_hidden
    reset = jax.nn.sigmoid(from_input[:, :width] + from_state[:, :width])
    update = jax.nn.sigmoid(from_input[:, width : 2 * width] + from_state[:, width : 2 * width])
    candidate = jnp.tanh(from_input[:, 2 * width :] + reset * from_state[:, 2 * width :])
    return (1.0 - update) * candidate + update * prior


def edge_hidden(feats, w_edge_in, b_edge_in):
    return jax.nn.silu(jnp.dot(feats, w_edge_in, precision=HIGH) + b_edge_in)


def pick_by(index_rows, piece):
    columns = lax.broadcasted_iota(jnp.int32, (1, piece.shape[0]), 1)
    onehot = (index_rows[:, None] == columns).astype(jnp.bfloat16)
    return jnp.dot(onehot, piece, preferred_element_type=jnp.float32)


def spread_by(index_rows, values, count):
    rows = lax.broadcasted_iota(jnp.int32, (count, 1), 0)
    onehot = (rows == index_rows[None, :]).astype(jnp.bfloat16)
    return jnp.dot(onehot, values, preferred_element_type=jnp.float32)


def from_all(x, edge):
    got = lax.all_to_all(jnp.broadcast_to(x[None], (edge,) + x.shape), "edge", 0, 0)
    return got.reshape((-1,) + x.shape[1:])


def to_owners(x, edge):
    got = lax.all_to_all(x.reshape((edge, -1) + x.shape[1:]), "edge", 0, 0)
    return jnp.sum(got.astype(F32), axis=0)


def slow_path(batch, edge, args):
    (states, edge_feats, molecule, source, target, edge_mask, w_edge_in, b_edge_in, w_edge_out, b_edge_out,
     w_input, w_hidden, b_input, b_hidden, cotangent) = args
    states_here = states[0]
    feats = edge_feats[0]
    source_ids = source[0]
    target_ids = target[0]
    width = states_here.shape[1]
    owned = states_here.shape[0]
    edges = source_ids.shape[0]
    block = min(512, edges)
    count = edges // block
    labels = from_all(molecule[0], edge)
    same = (jnp.take(labels, source_ids) == jnp.take(labels, target_ids)).astype(jnp.float32)
    valid = edge_mask[0].astype(jnp.float32) * same
    near = pick_by(source_ids, from_all(states_here, edge)).astype(
        jnp.bfloat16
    )
    hidden, edge_pull = jax.vjp(
        edge_hidden,
        feats.astype(jnp.float32),
        w_edge_in.astype(jnp.float32),
        b_edge_in.astype(jnp.float32),
    )
    latent_blocks = hidden.astype(jnp.bfloat16).reshape(count, block, -1)
    near_blocks = near.reshape(count, block, width)
    bias_out = b_edge_out.astype(jnp.float32)

    def expand(latent):
        flat = jnp.dot(latent, w_edge_out, preferred_element_type=jnp.float32) + bias_out
        return flat.astype(jnp.bfloat16).reshape(latent.shape[0], width, width)

    def apply(mats, vectors):
        return jnp.einsum("bij,bj->bi", mats, vectors, preferred_element_type=jnp.float32)

    outgoing = lax.map(lambda item: apply(expand(item[0]), item[1]), (latent_blocks, near_blocks))
    messages = (outgoing.reshape(edges, width) * valid[:, None]).astype(jnp.bfloat16)
    summed = to_owners(spread_by(target_ids, messages, edge * owned), edge)
    mixed = summed.astype(jnp.bfloat16).astype(jnp.float32)
    updated, update_pull = jax.vjp(
        gated_update,
        mixed,
        states_here.astype(jnp.float32),
        w_input.astype(jnp.float32),
        w_hidden.astype(jnp.float32),
        b_input.astype(jnp.float32),
        b_hidden.astype(jnp.float32),
    )
    new_states = updated.astype(jnp.bfloat16)
    d_mixed, d_direct, grad_wi, grad_wh, grad_bi, grad_bh = update_pull(
        cotangent[0].astype(jnp.float32)
    )
    pulled = pick_by(
        target_ids, from_all(d_mixed.astype(jnp.bfloat16), edge)
    )
    d_message = (pulled * valid[:, None]).astype(jnp.bfloat16)
    d_message_blocks = d_message.reshape(count, block, width)

    def backward_core(carry, mats, latent, vectors, d_out):
        grad_weight, grad_bias = carry
        outer = (
            d_out.astype(jnp.float32)[:, :, None] * vectors.astype(jnp.float32)[:, None, :]
        ).astype(jnp.bfloat16)
        flat = outer.reshape(latent.shape[0], width * width)
        d_latent = lax.dot_general(
            flat, w_edge_out, (((1,), (1,)), ((), ())), preferred_element_type=jnp.float32
        )
        grad_weight = grad_weight + lax.dot_general(
            latent, flat, (((0,), (0,)), ((), ())), preferred_element_type=jnp.float32
        )
        grad_bias = grad_bias + jnp.sum(flat.astype(jnp.float32), axis=0)
        d_vectors = jnp.einsum(
            "bij,bi->bj", mats, d_out, preferred_element_type=jnp.float32
        ).astype(jnp.bfloat16)
        return ((grad_weight, grad_bias), (d_latent, d_vectors))

    start_carry = (
        jnp.zeros((w_edge_out.shape[0], width * width), jnp.float32),
        jnp.zeros((width * width,), jnp.float32),
    )

    def backward_block(carry, item):
        return backward_core(carry, expand(item[0]), item[0], item[1], item[2])

    sums_out, per_edge = lax.scan(
        backward_block, start_carry, (latent_blocks, near_blocks, d_message_blocks)
    )
    grad_w2, grad_b2 = sums_out
    d_latent_all = per_edge[0].reshape(edges, -1)
    d_near_all = per_edge[1].reshape(edges, width)
    d_feats, grad_w1, grad_b1 = edge_pull(d_latent_all)
    returned = to_owners(spread_by(source_ids, d_near_all, owned * edge).astype(jnp.bfloat16), edge)
    state_grads = d_direct + returned

    bits, chunks, piece_arr = plan(batch, edge)
    devices = batch * edge
    pieces = grad_w2.reshape(PIECES, UNITS, H, H)
    small = jnp.concatenate([grad_wi, grad_wh, grad_b2.reshape(H, H)], axis=1).reshape(PIECES, UNITS, 7, H)
    small = small.transpose(0, 2, 1, 3).reshape(PIECES, 7 * UNITS, H)
    biases = jnp.concatenate([grad_bi, grad_bh]).reshape(6, H)
    biases = jnp.concatenate([biases, jnp.zeros((PIECES - 6, H), F32)], axis=0)[:, None]
    small = jnp.concatenate([small, biases, jnp.zeros((PIECES, EXTRA - 7 * UNITS - 1, H), F32)], axis=1)
    terms = []
    for chunk in chunks:
        block = pieces[:, :, chunk.first : chunk.first + chunk.rows].reshape(PIECES, -1, H)
        if chunk.extra:
            block = jnp.concatenate([block, small], axis=1)
        rel_of = sorted(range(PIECES // 2), key=chunk.place)
        order = jnp.array(rel_of + [PIECES // 2 + r for r in rel_of], jnp.int32)
        block = jnp.take(block, jnp.bitwise_xor(order, piece_arr[0]), axis=0).astype(BF16)
        shape = chunk.shape()
        kept, sent = block[: PIECES // 2].reshape(shape), block[PIECES // 2 :].reshape(shape)
        total = add([kept, swap(sent, bits[-1], devices)])
        for step in range(len(chunk.steps)):
            zero = (0,) * len(chunk.steps[step])
            total = add([total[zero]] + [swap(total[path], mask, devices) for path, mask in chunk.partners(step, bits)])
        terms.append(total)
    first = jnp.concatenate([grad_w1, grad_b1[None], jnp.zeros((15, H), F32)], axis=0)
    for n in range(devices.bit_length() - 1):
        mask = 1 << n
        if mask not in bits:
            terms = [rounded(w.astype(F32) + swap(w, mask, devices).astype(F32)) for w in terms]
        first = first + swap(first, mask, devices)
    for step in (3, 2, 1):
        terms = [gather_step(chunk, step, bits, devices, x) for x, chunk in zip(terms, chunks)]
    came = [swap(x, bits[chunk.order[0]], devices) for x, chunk in zip(terms, chunks)]
    early = early_half(chunks, bits, devices, piece_arr, terms)
    return new_states, state_grads, d_feats.T, first.astype(BF16), came, early


def per_device(batch, edge, *args):
    overflow, results = fast_path(batch, edge, args)
    results = lax.while_loop(
        lambda carry: carry[0], lambda carry: (jnp.bool_(False), slow_path(batch, edge, args)), (overflow, results)
    )[1]
    return finish(batch, edge, results)


def solution(mesh):
    batch, edge = mesh.shape["batch"], mesh.shape["edge"]
    nodes, edges, all_ = P("batch", "edge", None), P("batch", "edge"), P()
    return jax.shard_map(
        functools.partial(per_device, batch, edge),
        mesh=mesh,
        in_specs=(nodes, nodes, edges, edges, edges, edges) + (all_,) * 8 + (nodes,),
        out_specs=(nodes, nodes, nodes) + (all_,) * 8,
        check_vma=False,
    )
```
